256 devices in a mesh: section: 4 (over y), dp: 64 (over x, z, core).
Axes of the slice: x: 4, y: 4, z: 8, core: 2. Of those that a mesh axis runs over, the one named last changes fastest.
Arguments:
- prompt_states: bfloat16 [4, 4096, 5120], P('section', 'dp'), may hold values from -6 to 6
- answer_states: bfloat16 [4, 16384, 5120], P('section', 'dp'), may hold values from -6 to 6
- prompt_cotangent: bfloat16 [4, 4096, 512], P('section', 'dp'), may hold values from -3 to 3
- answer_cotangent: bfloat16 [4, 16384, 512], P('section', 'dp'), may hold values from -3 to 3
- norm_gain: bfloat16 [4, 5120], P('section'), may hold values from 0.5 to 1.5
- weights: bfloat16 [4, 5120, 768], P('section', 'dp'), may hold values from -3 to 3
- answer_length: int32 [4, 256], P('section', 'dp'), may hold values from 1 to 64, as said below
- answer_owner: int32 [4, 256], P('section', 'dp'), may hold values from 0 to 15, as said below
Outputs:
- prompt_grads_back: bfloat16 [4, 4096, 5120], P('section', 'dp')
- answer_grads_back: bfloat16 [4, 16384, 5120], P('section', 'dp')
- weight_grads: float32 [4, 5120, 768], P('section', 'dp')
- gain_grads: float32 [4, 5120], P('section', 'dp')
The draws below stay inside these ranges and needn't reach their ends.
Inputs may be any that keep to these rules, and one draw needn't show every extreme that they name: `answer_length`: in each layer some answer has length 64. `answer_owner`: in each layer every prompt is named by exactly 16 answer slots.
All inputs are finite; a program needn't handle non-finite values.
Results may differ from the reference program's by a relative error of at most 0.014.
Values may be sent and summed in bfloat16 or wider, within the bound.
No kernel may reach another device: no remote copies, remote signals or barrier semaphores. Data moves between devices by JAX's collectives and lax.ppermute only.
A program may use at most 128 MiB of HBM per device.

```python
import jax
import jax.numpy as jnp
from jax import lax

D = 5120
HD = 128
HEADS = 4
GROUP = 16
PL_DEV = 64
RMAX = 64
LAYERS = 4
PLEN = 256
RT = 256
N_PROMPTS = 16
N_RESP = 256
N_DP = 64


def draw_weights(key, part):
    key = jax.random.fold_in(key, 11)
    noise_key = jax.random.fold_in(key, 0)
    base_noise = jnp.clip(jax.random.normal(noise_key, (LAYERS, D, (HEADS + 2) * HD), jnp.float32), -6.0, 6.0)
    drawn_rows = base_noise * D ** (-0.5)
    return jnp.clip(drawn_rows, -3.0, 3.0).astype(jnp.bfloat16)


def draw_answer_length(key, part):
    key = jax.random.fold_in(key, 12)
    pick_key, length_key = jax.random.split(key)
    drawn_lengths = jax.random.randint(length_key, (LAYERS, N_RESP), 1, RMAX + 1)
    chosen = jax.random.randint(pick_key, (LAYERS, 1), 0, N_RESP)
    slot_index = jnp.arange(N_RESP)[None, :]
    return jnp.where(slot_index == chosen, RMAX, drawn_lengths).astype(jnp.int32)


def permute_slots(sub_key):
    return jax.random.permutation(sub_key, N_RESP)


def draw_answer_owner(key, part):
    key = jax.random.fold_in(key, 13)
    layer_keys = jax.random.split(key, LAYERS)
    shuffled = jax.vmap(permute_slots)(layer_keys)
    return (shuffled // GROUP).astype(jnp.int32)


def steps_of(own_key, dims, cuts, smallest, top_value):
    def one(axis_at, shards_of):
        draws = jax.random.uniform(jax.random.fold_in(jax.random.fold_in(own_key, 6), axis_at), (shards_of,), jnp.float32, smallest / len(cuts), top_value / len(cuts))
        return jnp.repeat(jnp.exp(draws), dims[axis_at] // shards_of).reshape((-1,) + (1,) * (len(dims) - axis_at - 1))

    factor_of = one(*cuts[0])
    for cut in cuts[1:]:
        factor_of = factor_of * one(*cut)
    return factor_of


def normal_values(rng, shape, spread, limit, shards=(), kind=jnp.bfloat16):
    drawn = jax.random.normal(rng, shape, jnp.float32) * spread
    if len(shards) > 0:
        drawn = steps_of(rng, shape, shards, -0.22, 0.18) * drawn
    return jnp.clip(drawn, min=-limit, max=limit).astype(kind)


def setup_inputs(seed: int = 0) -> dict:
    arg_keys = jax.random.split(jax.random.key(seed), 9)
    return {
        "prompt_states": normal_values(arg_keys[0], (LAYERS, N_DP * PL_DEV, D), 1.0, 6.0, ((0, 4), (1, 64))),
        "answer_states": normal_values(arg_keys[1], (LAYERS, N_DP * RT, D), 1.0, 6.0, ((0, 4), (1, 64))),
        "prompt_cotangent": normal_values(arg_keys[2], (LAYERS, N_DP * PL_DEV, HEADS * HD), 0.5, 3.0, ((0, 4), (1, 64))),
        "answer_cotangent": normal_values(arg_keys[3], (LAYERS, N_DP * RT, HEADS * HD), 0.5, 3.0, ((0, 4), (1, 64))),
        "norm_gain": jnp.clip(1.0 + 0.1 * jax.random.normal(arg_keys[4], (LAYERS, D), jnp.float32), 0.5, 1.5).astype(jnp.bfloat16),
        "weights": draw_weights(jax.random.fold_in(arg_keys[8], 71), 0),
        "answer_length": draw_answer_length(jax.random.fold_in(arg_keys[8], 71), 0),
        "answer_owner": draw_answer_owner(jax.random.fold_in(arg_keys[8], 71), 0),
    }


EPSILON = 1e-06
HIGHEST_PRECISION = lax.Precision.HIGHEST

def norm_rows(inputs, norm_gain):
    wide = inputs.astype(jnp.float32)
    inverse = lax.rsqrt(lax.optimization_barrier(jnp.mean(wide * wide, axis=-1, keepdims=True)) + EPSILON)
    scaled = (wide * inverse * norm_gain.astype(jnp.float32)).astype(jnp.bfloat16)
    return (wide, inverse, scaled)

def batched(einsum_form, left_side, right_side):
    left_side = lax.optimization_barrier(left_side)
    right_side = lax.optimization_barrier(right_side)
    return jnp.einsum(einsum_form, left_side.astype(jnp.float32), right_side.astype(jnp.float32))

def soft_rows(queries, key_rows, allowed):
    score_scale = queries.shape[-1] ** (-0.5)
    scores = score_scale * batched('bnqh,bmh->bqnm', queries, key_rows)
    scores = jnp.where(allowed[:, None, :, :], scores, -jnp.inf)
    row_max = lax.optimization_barrier(jnp.max(scores, axis=-1, keepdims=True))
    raised = jnp.exp(scores - row_max)
    return raised / lax.optimization_barrier(jnp.sum(raised, axis=-1, keepdims=True))

def attention_grads(queries, key_rows, value_rows, soft_probs, head_live):
    score_scale = queries.shape[-1] ** (-0.5)
    probs_low = soft_probs.astype(jnp.bfloat16)
    grad_probs = batched('bnqh,bmh->bqnm', head_live, value_rows)
    row_delta = lax.optimization_barrier(jnp.sum(soft_probs * grad_probs, axis=-1, keepdims=True))
    dscore = (soft_probs * (grad_probs - row_delta)).astype(jnp.bfloat16)
    grad_queries = score_scale * batched('bqnm,bmh->bnqh', dscore, key_rows)
    grad_keys = score_scale * batched('bqnm,bnqh->bmh', dscore, queries)
    grad_values = batched('bqnm,bnqh->bmh', probs_low, head_live)
    return (grad_queries, grad_keys, grad_values)

def section_grads(prompt_states, answer_states, prompt_cotangent, answer_cotangent, norm_gain, weights, answer_length, answer_owner):
    prompt_rows = prompt_states.shape[0]
    query_cols = HEADS * HD
    inputs = jnp.concatenate([prompt_states, answer_states], axis=0)
    upstream = jnp.concatenate([prompt_cotangent, answer_cotangent], axis=0)
    wide, inverse, scaled = norm_rows(inputs, norm_gain)
    triple = jnp.dot(scaled, weights, preferred_element_type=jnp.float32).astype(jnp.bfloat16)
    queries = triple[:, :query_cols]
    key_rows = triple[:, query_cols:query_cols + HD]
    value_rows = triple[:, query_cols + HD:]
    prompt_queries = queries[:prompt_rows].reshape(N_PROMPTS, PLEN, HEADS, HD)
    prompt_keys = key_rows[:prompt_rows].reshape(N_PROMPTS, PLEN, HD)
    prompt_values = value_rows[:prompt_rows].reshape(N_PROMPTS, PLEN, HD)
    positions = jnp.arange(PLEN)
    causal = jnp.broadcast_to(positions[:, None] >= positions[None, :], (N_PROMPTS, PLEN, PLEN))
    probs_prompt = soft_rows(prompt_queries, prompt_keys, causal)
    prompt_head = upstream[:prompt_rows].reshape(N_PROMPTS, PLEN, HEADS, HD)
    grad_q_prompt, grad_k_prompt, grad_v_prompt = attention_grads(prompt_queries, prompt_keys, prompt_values, probs_prompt, prompt_head)
    answer_queries = queries[prompt_rows:].reshape(N_RESP, RMAX, HEADS, HD)
    answer_keys = key_rows[prompt_rows:].reshape(N_RESP, RMAX, HD)
    answer_values = value_rows[prompt_rows:].reshape(N_RESP, RMAX, HD)
    owned_keys = jnp.concatenate([prompt_keys[answer_owner], answer_keys], axis=1)
    owned_values = jnp.concatenate([prompt_values[answer_owner], answer_values], axis=1)
    steps_along = jnp.arange(RMAX)
    living = steps_along[None, :] < answer_length[:, None]
    earlier = (steps_along[:, None] >= steps_along[None, :])[None, :, :] & living[:, None, :]
    visible = jnp.concatenate([jnp.ones((N_RESP, RMAX, PLEN), dtype=jnp.bool_), earlier], axis=2)
    probs_answer = soft_rows(answer_queries, owned_keys, visible)
    live_scale = living.astype(jnp.float32)[:, :, None, None]
    answer_head = (upstream[prompt_rows:].reshape(N_RESP, RMAX, HEADS, HD).astype(jnp.float32) * live_scale).astype(jnp.bfloat16)
    grad_q_answer, grad_k_answer, grad_v_answer = attention_grads(answer_queries, owned_keys, owned_values, probs_answer, answer_head)
    owner_marks = (answer_owner[:, None] == jnp.arange(N_PROMPTS)[None, :]).astype(jnp.float32)
    key_total = grad_k_prompt + jnp.einsum('rp,rmh->pmh', owner_marks, grad_k_answer[:, :PLEN], precision=HIGHEST_PRECISION)
    value_total = grad_v_prompt + jnp.einsum('rp,rmh->pmh', owner_marks, grad_v_answer[:, :PLEN], precision=HIGHEST_PRECISION)
    grad_queries = jnp.concatenate([grad_q_prompt.reshape(-1, query_cols), grad_q_answer.reshape(-1, query_cols)], axis=0)
    grad_keys = jnp.concatenate([key_total.reshape(-1, HD), grad_k_answer[:, PLEN:].reshape(-1, HD)], axis=0)
    grad_values = jnp.concatenate([value_total.reshape(-1, HD), grad_v_answer[:, PLEN:].reshape(-1, HD)], axis=0)
    grad_triple = jnp.concatenate([grad_queries, grad_keys, grad_values], axis=1).astype(jnp.bfloat16)
    grad_hidden = jnp.dot(grad_triple, weights.T, preferred_element_type=jnp.float32)
    weight_grads = jnp.dot(scaled.T, grad_triple, preferred_element_type=jnp.float32)
    gain_grads = lax.optimization_barrier(jnp.sum(grad_hidden * wide * inverse, axis=0))
    mixed = grad_hidden * norm_gain.astype(jnp.float32)
    moved = inverse * mixed - wide * inverse ** 3 * lax.optimization_barrier(jnp.mean(wide * mixed, axis=-1, keepdims=True))
    grads_in = moved.astype(jnp.bfloat16)
    return (grads_in[:prompt_rows], grads_in[prompt_rows:], weight_grads, gain_grads)

def reference(prompt_states, answer_states, prompt_cotangent, answer_cotangent, norm_gain, weights, answer_length, answer_owner):
    collected = [section_grads(prompt_states[layer_index], answer_states[layer_index], prompt_cotangent[layer_index], answer_cotangent[layer_index], norm_gain[layer_index], weights[layer_index], answer_length[layer_index], answer_owner[layer_index]) for layer_index in range(LAYERS)]
    prompt_back = jnp.stack([result_set[0] for result_set in collected])
    answer_back = jnp.stack([result_set[1] for result_set in collected])
    weight_stack = jnp.stack([result_set[2] for result_set in collected])
    gain_stack = jnp.stack([result_set[3] for result_set in collected])
    return (jnp.roll(prompt_back, -1, axis=0), jnp.roll(answer_back, -1, axis=0), weight_stack, gain_stack)
```

```python
import functools

import jax
import jax.numpy as jnp
from jax import lax
from jax.experimental import pallas as pl
from jax.experimental.pallas import tpu as pltpu
from jax.sharding import Mesh, PartitionSpec as P

HD = 128
HEADS = 4
QC = HEADS * HD
D = 5120
PR = 64
AR = 256
SLOTS = 4
SR = 64
NX, NZ, NC = 4, 8, 2
WR = 80
BLK = D // NX
PROMPTS = 16
PLEN = 256
EPSILON = 1e-06
SCALE = HD**-0.5
BF = jnp.bfloat16
F32 = jnp.float32
VMEM_BYTES = 56 * 1024 * 1024


def shift(value, axis, steps):
    count = lax.axis_size(axis)
    if steps % count == 0:
        return value
    return lax.ppermute(value, axis, [(s, (s + steps) % count) for s in range(count)])


def params():
    return pltpu.CompilerParams(vmem_limit_bytes=VMEM_BYTES)


def nt(a, b):
    return lax.dot_general(a, b, (((1,), (1,)), ((), ())), preferred_element_type=F32)


def tn(a, b):
    return lax.dot_general(a, b, (((0,), (0,)), ((), ())), preferred_element_type=F32)


def nn(a, b):
    return jnp.dot(a, b, preferred_element_type=F32)


def ring(value, axis):
    count = lax.axis_size(axis)
    half = count // 2
    pieces = {0: value}
    up = down = value
    for j in range(1, half):
        up = shift(up, axis, 1)
        down = shift(down, axis, -1)
        pieces[j] = up
        pieces[count - j] = down
    cut = value.shape[0] // 2
    pieces[half] = jnp.concatenate([shift(up[:cut], axis, 1), shift(down[cut:], axis, -1)], axis=0)
    return jnp.stack([pieces[j] for j in range(count)])


def direct(value, axis):
    return jnp.stack([shift(value, axis, k) for k in range(lax.axis_size(axis))])


def gather_xz(value):
    return ring(direct(value, "x"), "z")


def gather_zx(value):
    return ring(direct(value, "z"), "x")


def project_kernel(ids, a_ref, *refs, orders):
    count = len(orders)
    pieces = refs[: 2 * count]
    out_ref = refs[2 * count]
    w_refs = refs[2 * count + 1 : 3 * count + 1]
    sem = refs[-1]
    x, z, c = ids[0], ids[1], ids[2]
    copies = []
    for s, order in enumerate(orders):
        for rel in range(2):
            piece = pieces[2 * s + rel]
            for j in range(NZ):
                src = piece.at[j] if order == "zx" else piece.at[:, j]
                dst = w_refs[s].at[:, lax.rem(z - j + NZ, NZ), lax.rem(c + rel, 2)]
                copy = pltpu.make_async_copy(src, dst, sem.at[s, rel, j])
                copy.start()
                copies.append(copy)
    for copy in copies:
        copy.wait()
    for s in range(count):
        width = w_refs[s].shape[-1]
        total = jnp.zeros((a_ref.shape[0], width), F32)
        for k in range(NX):
            at = pl.multiple_of(lax.rem(x - k + NX, NX) * BLK, BLK)
            total += nn(a_ref[:, pl.ds(at, BLK)], w_refs[s][k].reshape(BLK, width))
        out_ref[:, s * width : (s + 1) * width] = total.astype(BF)


def project(ids, scaled, streams, orders):
    width = streams[0][0].shape[-1]
    rows = scaled.shape[0]
    count = len(streams)
    any_spec = pl.BlockSpec(memory_space=pl.ANY)
    vm = pl.BlockSpec(memory_space=pltpu.VMEM)
    return pl.pallas_call(
        functools.partial(project_kernel, orders=orders),
        out_shape=[jax.ShapeDtypeStruct((rows, width * count), BF)]
        + [jax.ShapeDtypeStruct((NX, NZ, NC, WR, width), BF)] * count,
        in_specs=[pl.BlockSpec(memory_space=pltpu.SMEM), vm] + [any_spec] * (2 * count),
        out_specs=[vm] * (1 + count),
        scratch_shapes=[pltpu.SemaphoreType.DMA((count, 2, NZ))],
        compiler_params=params(),
        cost_estimate=pl.CostEstimate(
            flops=2 * rows * D * width * count, bytes_accessed=2 * D * width * count * 2, transcendentals=0
        ),
        name="project",
    )(ids, scaled, *[p for pair in streams for p in pair])


def stacked(value):
    return jnp.concatenate([value[:, h * HD : (h + 1) * HD] for h in range(HEADS)], axis=0)


def attention_kernel(
    ids, owners, lengths, q_ref, kv_ref, gp_ref, ga_ref, ks_ref, kt_ref, vs_ref, vt_ref,
    gq_ref, gkv_ref, own_ref, sib_ref, kbuf, vbuf, dense, sem,
):
    x, z, c = ids[0], ids[1], ids[2]
    own_prompt = x * 4 + z // 2
    prompts = [owners[s] for s in range(SLOTS)] + [own_prompt]
    copies = []
    for b, p in enumerate(prompts):
        k = lax.rem(x - p // 4 + NX, NX)
        for half in range(2):
            j = lax.rem(z - (lax.rem(p, 4) * 2 + half) + NZ, NZ)
            for rel in range(2):
                at = pl.multiple_of((half * 2 + lax.rem(c + rel, 2)) * PR, PR)
                kr = (ks_ref, kt_ref)[rel]
                vr = (vs_ref, vt_ref)[rel]
                copies.append(pltpu.make_async_copy(kr.at[j, k], kbuf.at[b, pl.ds(at, PR)], sem.at[0, b, half, rel]))
                copies.append(pltpu.make_async_copy(vr.at[k, j], vbuf.at[b, pl.ds(at, PR)], sem.at[1, b, half, rel]))
                copies[-2].start()
                copies[-1].start()
    dense[...] = jnp.zeros_like(dense)
    row_step = lax.rem(lax.broadcasted_iota(jnp.int32, (HEADS * SR, SR), 0), SR)
    col_step = lax.broadcasted_iota(jnp.int32, (HEADS * SR, SR), 1)
    live_step = lax.broadcasted_iota(jnp.int32, (SR, QC), 0)
    per_block = 8
    for b in range(SLOTS + 1):
        for copy in copies[b * per_block : (b + 1) * per_block]:
            copy.wait()
        keys, values = kbuf[b], vbuf[b]
        if b < SLOTS:
            lo = PR + b * SR
            length = lengths[b]
            upstream = ga_ref[b * SR : (b + 1) * SR, :]
            upstream = jnp.where(live_step < length, upstream.astype(F32), 0.0).astype(BF)
        else:
            lo = 0
            upstream = gp_ref[...]
        q4 = stacked(q_ref[lo : lo + SR, :])
        g4 = stacked(upstream)
        s1 = SCALE * nt(q4, keys)
        gp1 = nt(g4, values)
        if b < SLOTS:
            k_own = kv_ref[lo : lo + SR, :HD]
            v_own = kv_ref[lo : lo + SR, HD:]
            s2 = SCALE * nt(q4, k_own)
            gp2 = nt(g4, v_own)
            seen = (row_step >= col_step) & (col_step < length)
            s2 = jnp.where(seen, s2, -jnp.inf)
            top = jnp.maximum(jnp.max(s1, axis=1, keepdims=True), jnp.max(s2, axis=1, keepdims=True))
            e1 = jnp.exp(s1 - top)
            e2 = jnp.exp(s2 - top)
            norm = 1.0 / (jnp.sum(e1, axis=1, keepdims=True) + jnp.sum(e2, axis=1, keepdims=True))
            p1 = e1 * norm
            p2 = e2 * norm
            delta = jnp.sum(p1 * gp1, axis=1, keepdims=True) + jnp.sum(p2 * gp2, axis=1, keepdims=True)
            d2 = (p2 * (gp2 - delta)).astype(BF)
        else:
            offset = (lax.rem(z, 2) * 2 + c) * PR
            rows = lax.rem(lax.broadcasted_iota(jnp.int32, (HEADS * SR, PLEN), 0), SR) + offset
            cols = lax.broadcasted_iota(jnp.int32, (HEADS * SR, PLEN), 1)
            s1 = jnp.where(rows >= cols, s1, -jnp.inf)
            top = jnp.max(s1, axis=1, keepdims=True)
            e1 = jnp.exp(s1 - top)
            p1 = e1 * (1.0 / jnp.sum(e1, axis=1, keepdims=True))
            delta = jnp.sum(p1 * gp1, axis=1, keepdims=True)
        d1 = (p1 * (gp1 - delta)).astype(BF)
        gq = nn(d1, keys)
        if b < SLOTS:
            gq += nn(d2, k_own)
            gkv_ref[b * SR : (b + 1) * SR, :HD] = (SCALE * tn(d2, q4)).astype(BF)
            gkv_ref[b * SR : (b + 1) * SR, HD:] = tn(p2.astype(BF), g4).astype(BF)
        gq = (SCALE * gq).astype(BF)
        for h in range(HEADS):
            gq_ref[lo : lo + SR, h * HD : (h + 1) * HD] = gq[h * SR : (h + 1) * SR, :]
        p = prompts[b]
        dense[p, :, :, :HD] += (SCALE * tn(d1, q4)).reshape(4, PR, HD)
        dense[p, :, :, HD:] += tn(p1.astype(BF), g4).reshape(4, PR, HD)
    for half in range(2):
        own_ref[:, half] = dense[:, half * 2 + c].astype(BF)
        sib_ref[:, half] = dense[:, half * 2 + 1 - c].astype(BF)


def attention(ids, owners, lengths, q, kv, gp, ga, ks, kt, vs, vt):
    smem = pl.BlockSpec(memory_space=pltpu.SMEM)
    vm = pl.BlockSpec(memory_space=pltpu.VMEM)
    any_spec = pl.BlockSpec(memory_space=pl.ANY)
    return pl.pallas_call(
        attention_kernel,
        out_shape=[
            jax.ShapeDtypeStruct((PR + AR, QC), BF),
            jax.ShapeDtypeStruct((AR, 2 * HD), BF),
            jax.ShapeDtypeStruct((PROMPTS, 2, PR, 2 * HD), BF),
            jax.ShapeDtypeStruct((PROMPTS, 2, PR, 2 * HD), BF),
        ],
        in_specs=[smem] * 3 + [vm] * 4 + [any_spec] * 4,
        out_specs=[vm] * 4,
        scratch_shapes=[
            pltpu.VMEM((SLOTS + 1, PLEN, HD), BF),
            pltpu.VMEM((SLOTS + 1, PLEN, HD), BF),
            pltpu.VMEM((PROMPTS, 4, PR, 2 * HD), F32),
            pltpu.SemaphoreType.DMA((2, SLOTS + 1, 2, 2)),
        ],
        compiler_params=params(),
        cost_estimate=pl.CostEstimate(flops=2 * 10**9, bytes_accessed=8 * 10**6, transcendentals=400000),
        name="attention",
    )(ids, owners, lengths, q, kv, gp, ga, ks, kt, vs, vt)


def input_grads_kernel(ids, gq_ref, gkv_ref, q_ref, kv_ref, inv_ref, x_ref, gain_ref, w1, w2, w3, out_ref):
    del ids
    gq, gkv = gq_ref[...], gkv_ref[...]
    inv = inv_ref[...]
    row_dot = jnp.sum(gq.astype(F32) * q_ref[...].astype(F32), axis=1, keepdims=True)
    row_dot += jnp.sum(gkv.astype(F32) * kv_ref[...].astype(F32), axis=1, keepdims=True)
    coefficient = inv * inv * row_dot * (1.0 / D)
    hidden = nt(gq[:, : 2 * HD], w1[0].reshape(BLK, 2 * HD))
    hidden += nt(gq[:, 2 * HD :], w2[0].reshape(BLK, 2 * HD))
    hidden += nt(gkv, w3[0].reshape(BLK, 2 * HD))
    moved = inv * gain_ref[...].astype(F32) * hidden - x_ref[...].astype(F32) * coefficient
    out_ref[...] = moved.astype(BF)


def input_grads(ids, gq, gkv, q, kv, inv, states, gain, w1, w2, w3):
    rows = states.shape[0]

    def whole(k, ids):
        return (0, 0)

    def column(k, ids):
        return (0, lax.rem(ids[0] - k + NX, NX))

    def block(k, ids):
        return (k, 0, 0, 0, 0)

    w_spec = pl.BlockSpec((1, NZ, NC, WR, 2 * HD), block)
    return pl.pallas_call(
        input_grads_kernel,
        out_shape=jax.ShapeDtypeStruct((rows, D), BF),
        grid_spec=pltpu.PrefetchScalarGridSpec(
            num_scalar_prefetch=1,
            grid=(NX,),
            in_specs=[
                pl.BlockSpec((rows, QC), whole),
                pl.BlockSpec((rows, 2 * HD), whole),
                pl.BlockSpec((rows, QC), whole),
                pl.BlockSpec((rows, 2 * HD), whole),
                pl.BlockSpec((rows, 1), whole),
                pl.BlockSpec((rows, BLK), column),
                pl.BlockSpec((1, BLK), column),
                w_spec,
                w_spec,
                w_spec,
            ],
            out_specs=pl.BlockSpec((rows, BLK), column),
        ),
        compiler_params=params(),
        cost_estimate=pl.CostEstimate(
            flops=2 * rows * D * 768, bytes_accessed=2 * D * 768 + 4 * rows * D, transcendentals=0
        ),
        name="input_grads",
    )(ids, gq, gkv, q, kv, inv, states, gain, w1, w2, w3)


def weight_grads_kernel(ids, st_ref, g_ref, own_ref, sib_ref):
    width = g_ref.shape[1]
    total = nn(st_ref[...], g_ref[...]).astype(BF).reshape(NZ, NC, WR, width)

    @pl.when(ids[2] == 0)
    def _():
        own_ref[0] = total[:, 0]
        sib_ref[0] = total[:, 1]

    @pl.when(ids[2] == 1)
    def _():
        own_ref[0] = total[:, 1]
        sib_ref[0] = total[:, 0]


def weight_grads(ids, scaled_t, grads):
    rows, width = grads.shape
    spec = pl.BlockSpec((1, NZ, WR, width), lambda k, ids: (k, 0, 0, 0))
    return pl.pallas_call(
        weight_grads_kernel,
        out_shape=[jax.ShapeDtypeStruct((NX, NZ, WR, width), BF)] * 2,
        grid_spec=pltpu.PrefetchScalarGridSpec(
            num_scalar_prefetch=1,
            grid=(NX,),
            in_specs=[
                pl.BlockSpec((BLK, rows), lambda k, ids: (k, 0)),
                pl.BlockSpec((rows, width), lambda k, ids: (0, 0)),
            ],
            out_specs=[spec, spec],
        ),
        compiler_params=params(),
        cost_estimate=pl.CostEstimate(
            flops=2 * rows * D * width, bytes_accessed=2 * D * (rows + width), transcendentals=0
        ),
        name="weight_grads",
    )(ids, scaled_t, grads)


def exchange(value, axis):
    return lax.all_to_all(value, axis, 0, 0, tiled=True)


def add_up(value):
    return jnp.sum(value.astype(F32), axis=0)


def reduce_weights(own, sib):
    both = (own.astype(F32) + shift(sib, "c", 1).astype(F32)).astype(BF)
    part = add_up(exchange(both, "x")).astype(BF)
    return add_up(exchange(part, "z"))


def per_device(
    prompt_states,
    answer_states,
    prompt_cotangent,
    answer_cotangent,
    norm_gain,
    weights,
    answer_length,
    answer_owner,
):
    x, z, c = lax.axis_index("x"), lax.axis_index("z"), lax.axis_index("c")
    ids = jnp.stack([x, z, c]).astype(jnp.int32)
    lengths, owners = answer_length[0], answer_owner[0]
    shard = weights[0]
    gain = norm_gain[0].astype(F32)

    kv_piece = gather_zx(shard[:, QC:])
    q1_piece = gather_xz(shard[:, : 2 * HD])
    q2_piece = gather_zx(shard[:, 2 * HD : QC])
    kv_sib = shift(kv_piece, "c", 1)
    q1_sib = shift(q1_piece, "c", 1)
    q2_sib = shift(q2_piece, "c", 1)

    inputs = jnp.concatenate([prompt_states[0], answer_states[0]], axis=0)
    wide = inputs.astype(F32)
    inverse = lax.rsqrt(jnp.mean(wide * wide, axis=-1, keepdims=True) + EPSILON)
    scaled = (wide * inverse * gain).astype(BF)
    scaled_t = scaled.T

    kv, w3 = project(ids, scaled, [(kv_piece, kv_sib)], ["xz"])
    keys, values = kv[:PR, :HD], kv[:PR, HD:]
    ks = direct(direct(keys, "x"), "z")
    vs = direct(direct(values, "z"), "x")
    kt = shift(ks, "c", 1)
    vt = shift(vs, "c", 1)
    q, w1, w2 = project(ids, scaled, [(q1_piece, q1_sib), (q2_piece, q2_sib)], ["zx", "xz"])

    gq, gkv_answer, own, sib = attention(
        ids, owners, lengths, q, kv, prompt_cotangent[0], answer_cotangent[0], ks, kt, vs, vt
    )

    terms = (own.astype(F32) + shift(sib, "c", 1).astype(F32)).astype(BF).reshape(NX * NZ, PR, 2 * HD)
    gkv_prompt = add_up(exchange(terms, ("x", "z"))).astype(BF)

    answer_back = input_grads(
        ids, gq[PR:], gkv_answer, q[PR:], kv[PR:], inverse[PR:], answer_states[0], norm_gain, w1, w2, w3
    )
    answer_out = shift(answer_back, "section", -1)

    query_total = reduce_weights(*weight_grads(ids, scaled_t, gq))

    gkv = jnp.concatenate([gkv_prompt, gkv_answer], axis=0)
    prompt_back = input_grads(
        ids, gq[:PR], gkv_prompt, q[:PR], kv[:PR], inverse[:PR], prompt_states[0], norm_gain, w1, w2, w3
    )
    prompt_out = shift(prompt_back, "section", -1)
    pair_total = reduce_weights(*weight_grads(ids, scaled_t, gkv))

    weight_total = jnp.concatenate([query_total, pair_total], axis=1)
    own_gain = lax.dynamic_slice(gain, (((x * NZ + z) * NC + c) * WR,), (WR,))
    gain_total = jnp.sum(weight_total * shard.astype(F32), axis=1) / own_gain
    return (prompt_out[None], answer_out[None], weight_total[None], gain_total[None])


def solution(mesh):
    fine = Mesh(mesh.devices.reshape(mesh.devices.shape[0], NX, NZ, NC), ("section", "x", "z", "c"))
    dp = ("x", "z", "c")
    placed = (
        P("section", dp, None),
        P("section", dp, None),
        P("section", dp, None),
        P("section", dp, None),
        P("section", None),
        P("section", dp, None),
        P("section", dp),
        P("section", dp),
    )
    return jax.shard_map(
        per_device,
        mesh=fine,
        in_specs=placed,
        out_specs=(
            P("section", dp, None),
            P("section", dp, None),
            P("section", dp, None),
            P("section", dp),
        ),
        check_vma=False,
    )
```

```python
import functools

import jax
import jax.numpy as jnp
from jax import lax
from jax.experimental import pallas as pl
from jax.experimental.pallas import tpu as pltpu
from jax.sharding import Mesh, PartitionSpec as P

HD = 128
HEADS = 4
QC = HEADS * HD
D = 5120
PR = 64
AR = 256
SLOTS = 4
SR = 64
NX, NZ, NC = 4, 8, 2
WR = 80
BLK = D // NX
PROMPTS = 16
PLEN = 256
EPSILON = 1e-06
SCALE = HD**-0.5
BF = jnp.bfloat16
F32 = jnp.float32
VMEM_BYTES = 56 * 1024 * 1024


def shift(value, axis, steps):
    count = lax.axis_size(axis)
    if steps % count == 0:
        return value
    return lax.ppermute(value, axis, [(s, (s + steps) % count) for s in range(count)])


def params():
    return pltpu.CompilerParams(vmem_limit_bytes=VMEM_BYTES)


def nt(a, b):
    return lax.dot_general(a, b, (((1,), (1,)), ((), ())), preferred_element_type=F32)


def tn(a, b):
    return lax.dot_general(a, b, (((0,), (0,)), ((), ())), preferred_element_type=F32)


def nn(a, b):
    return jnp.dot(a, b, preferred_element_type=F32)


def exchange(value, axis):
    return lax.all_to_all(value, axis, 0, 0, tiled=True)


def spread(value, axis):
    count = lax.axis_size(axis)
    return exchange(jnp.broadcast_to(value[None], (count, *value.shape)), axis)


def project_kernel(ids, a_ref, *refs, orders):
    count = len(orders)
    pieces = refs[: 2 * count]
    out_ref = refs[2 * count]
    w_refs = refs[2 * count + 1 : 3 * count + 1]
    sem = refs[-1]
    c = ids[2]
    copies = []
    for s, order in enumerate(orders):
        for rel in range(2):
            piece, core = pieces[2 * s + rel], lax.rem(c + rel, 2)
            for i in range(NX):
                src = piece.at[i] if order == "xz" else piece.at[:, i]
                copy = pltpu.make_async_copy(src, w_refs[s].at[i, :, core], sem.at[s, rel, i])
                copy.start()
                copies.append(copy)
    for copy in copies:
        copy.wait()
    at = 0
    for s in range(count):
        width = w_refs[s].shape[-1]
        out_ref[:, at : at + width] = nn(a_ref[...], w_refs[s][...].reshape(D, width)).astype(BF)
        at += width


def project(ids, scaled, streams, orders):
    widths = [pair[0].shape[-1] for pair in streams]
    rows = scaled.shape[0]
    count = len(streams)
    any_spec = pl.BlockSpec(memory_space=pl.ANY)
    vm = pl.BlockSpec(memory_space=pltpu.VMEM)
    return pl.pallas_call(
        functools.partial(project_kernel, orders=orders),
        out_shape=[jax.ShapeDtypeStruct((rows, sum(widths)), BF)]
        + [jax.ShapeDtypeStruct((NX, NZ, NC, WR, width), BF) for width in widths],
        in_specs=[pl.BlockSpec(memory_space=pltpu.SMEM), vm] + [any_spec] * (2 * count),
        out_specs=[vm] * (1 + count),
        scratch_shapes=[pltpu.SemaphoreType.DMA((count, 2, NX))],
        compiler_params=params(),
        cost_estimate=pl.CostEstimate(
            flops=2 * rows * D * sum(widths), bytes_accessed=2 * D * sum(widths) * 2, transcendentals=0
        ),
        name="project",
    )(ids, scaled, *[p for pair in streams for p in pair])


def stacked(value):
    return jnp.concatenate([value[:, h * HD : (h + 1) * HD] for h in range(HEADS)], axis=0)


def attention_kernel(
    ids, owners, lengths, q_ref, kv_ref, gp_ref, ga_ref, s_ref, t_ref,
    gq_ref, gkv_ref, own_ref, sib_ref, pairs, dense, sem,
):
    x, z, c = ids[0], ids[1], ids[2]
    own_prompt = x * 4 + z // 2
    prompts = [owners[s] for s in range(SLOTS)] + [own_prompt]
    copies = []
    for b, p in enumerate(prompts):
        for half in range(2):
            chip = p * 2 + half
            for rel in range(2):
                at = pl.multiple_of((half * 2 + lax.rem(c + rel, 2)) * PR, PR)
                src = (s_ref, t_ref)[rel].at[chip]
                copies.append(pltpu.make_async_copy(src, pairs.at[b, pl.ds(at, PR)], sem.at[b, half, rel]))
                copies[-1].start()
    dense[...] = jnp.zeros_like(dense)
    row_step = lax.rem(lax.broadcasted_iota(jnp.int32, (HEADS * SR, SR), 0), SR)
    col_step = lax.broadcasted_iota(jnp.int32, (HEADS * SR, SR), 1)
    live_step = lax.broadcasted_iota(jnp.int32, (SR, QC), 0)
    per_block = 4
    for b in range(SLOTS + 1):
        for copy in copies[b * per_block : (b + 1) * per_block]:
            copy.wait()
        keys, values = pairs[b, :, :HD], pairs[b, :, HD:]
        if b < SLOTS:
            lo = PR + b * SR
            length = lengths[b]
            upstream = ga_ref[b * SR : (b + 1) * SR, :]
            upstream = jnp.where(live_step < length, upstream.astype(F32), 0.0).astype(BF)
        else:
            lo = 0
            upstream = gp_ref[...]
        q4 = stacked(q_ref[lo : lo + SR, :])
        g4 = stacked(upstream)
        s1 = SCALE * nt(q4, keys)
        gp1 = nt(g4, values)
        if b < SLOTS:
            k_own = kv_ref[lo : lo + SR, :HD]
            v_own = kv_ref[lo : lo + SR, HD:]
            s2 = SCALE * nt(q4, k_own)
            gp2 = nt(g4, v_own)
            seen = (row_step >= col_step) & (col_step < length)
            s2 = jnp.where(seen, s2, -jnp.inf)
            top = jnp.maximum(jnp.max(s1, axis=1, keepdims=True), jnp.max(s2, axis=1, keepdims=True))
            e1 = jnp.exp(s1 - top)
            e2 = jnp.exp(s2 - top)
            norm = 1.0 / (jnp.sum(e1, axis=1, keepdims=True) + jnp.sum(e2, axis=1, keepdims=True))
            p1 = e1 * norm
            p2 = e2 * norm
            delta = jnp.sum(p1 * gp1, axis=1, keepdims=True) + jnp.sum(p2 * gp2, axis=1, keepdims=True)
            d2 = (p2 * (gp2 - delta)).astype(BF)
        else:
            offset = (lax.rem(z, 2) * 2 + c) * PR
            rows = lax.rem(lax.broadcasted_iota(jnp.int32, (HEADS * SR, PLEN), 0), SR) + offset
            cols = lax.broadcasted_iota(jnp.int32, (HEADS * SR, PLEN), 1)
            s1 = jnp.where(rows >= cols, s1, -jnp.inf)
            top = jnp.max(s1, axis=1, keepdims=True)
            e1 = jnp.exp(s1 - top)
            p1 = e1 * (1.0 / jnp.sum(e1, axis=1, keepdims=True))
            delta = jnp.sum(p1 * gp1, axis=1, keepdims=True)
        d1 = (p1 * (gp1 - delta)).astype(BF)
        gq = nn(d1, keys)
        if b < SLOTS:
            gq += nn(d2, k_own)
            gkv_ref[b * SR : (b + 1) * SR, :HD] = (SCALE * tn(d2, q4)).astype(BF)
            gkv_ref[b * SR : (b + 1) * SR, HD:] = tn(p2.astype(BF), g4).astype(BF)
        gq = (SCALE * gq).astype(BF)
        for h in range(HEADS):
            gq_ref[lo : lo + SR, h * HD : (h + 1) * HD] = gq[h * SR : (h + 1) * SR, :]
        p = prompts[b]
        dense[p, :, :, :HD] += (SCALE * tn(d1, q4)).reshape(4, PR, HD)
        dense[p, :, :, HD:] += tn(p1.astype(BF), g4).reshape(4, PR, HD)
    for half in range(2):
        own_ref[:, half] = dense[:, half * 2 + c].astype(BF)
        sib_ref[:, half] = dense[:, half * 2 + 1 - c].astype(BF)


def attention(ids, owners, lengths, q, kv, gp, ga, pairs, pairs_sib):
    smem = pl.BlockSpec(memory_space=pltpu.SMEM)
    vm = pl.BlockSpec(memory_space=pltpu.VMEM)
    any_spec = pl.BlockSpec(memory_space=pl.ANY)
    return pl.pallas_call(
        attention_kernel,
        out_shape=[
            jax.ShapeDtypeStruct((PR + AR, QC), BF),
            jax.ShapeDtypeStruct((AR, 2 * HD), BF),
            jax.ShapeDtypeStruct((PROMPTS, 2, PR, 2 * HD), BF),
            jax.ShapeDtypeStruct((PROMPTS, 2, PR, 2 * HD), BF),
        ],
        in_specs=[smem] * 3 + [vm] * 4 + [any_spec] * 2,
        out_specs=[vm] * 4,
        scratch_shapes=[
            pltpu.VMEM((SLOTS + 1, PLEN, 2 * HD), BF),
            pltpu.VMEM((PROMPTS, 4, PR, 2 * HD), F32),
            pltpu.SemaphoreType.DMA((SLOTS + 1, 2, 2)),
        ],
        compiler_params=params(),
        cost_estimate=pl.CostEstimate(flops=2 * 10**9, bytes_accessed=8 * 10**6, transcendentals=400000),
        name="attention",
    )(ids, owners, lengths, q, kv, gp, ga, pairs, pairs_sib)


def input_grads_kernel(gq_ref, gkv_ref, q_ref, kv_ref, inv_ref, x_ref, gain_ref, wq_ref, wkv_ref, out_ref):
    gq, gkv = gq_ref[...], gkv_ref[...]
    inv = inv_ref[...]
    row_dot = jnp.sum(gq.astype(F32) * q_ref[...].astype(F32), axis=1, keepdims=True)
    row_dot += jnp.sum(gkv.astype(F32) * kv_ref[...].astype(F32), axis=1, keepdims=True)
    coefficient = inv * inv * row_dot * (1.0 / D)
    hidden = nn(gq, wq_ref[...]) + nn(gkv, wkv_ref[...])
    moved = inv * gain_ref[...].astype(F32) * hidden - x_ref[...].astype(F32) * coefficient
    out_ref[...] = moved.astype(BF)


def input_grads(gq, gkv, q, kv, inv, states, gain, wq, wkv):
    rows = states.shape[0]

    def whole(k):
        return (0, 0)

    def column(k):
        return (0, k)

    return pl.pallas_call(
        input_grads_kernel,
        out_shape=jax.ShapeDtypeStruct((rows, D), BF),
        grid=(NX,),
        in_specs=[
            pl.BlockSpec((rows, QC), whole),
            pl.BlockSpec((rows, 2 * HD), whole),
            pl.BlockSpec((rows, QC), whole),
            pl.BlockSpec((rows, 2 * HD), whole),
            pl.BlockSpec((rows, 1), whole),
            pl.BlockSpec((rows, BLK), column),
            pl.BlockSpec((1, BLK), column),
            pl.BlockSpec((QC, BLK), column),
            pl.BlockSpec((2 * HD, BLK), column),
        ],
        out_specs=pl.BlockSpec((rows, BLK), column),
        compiler_params=params(),
        cost_estimate=pl.CostEstimate(
            flops=2 * rows * D * 768, bytes_accessed=2 * D * 768 + 4 * rows * D, transcendentals=0
        ),
        name="input_grads",
    )(gq, gkv, q, kv, inv, states, gain, wq, wkv)


def weight_grads_kernel(ids, st_ref, g_ref, after_ref, own_ref, sib_ref):
    del after_ref
    width = g_ref.shape[1]
    total = nn(st_ref[...], g_ref[...]).astype(BF).reshape(NZ, NC, WR, width)

    @pl.when(ids[2] == 0)
    def _():
        own_ref[0] = total[:, 0]
        sib_ref[0] = total[:, 1]

    @pl.when(ids[2] == 1)
    def _():
        own_ref[0] = total[:, 1]
        sib_ref[0] = total[:, 0]


def weight_grads(ids, scaled_t, grads, after):
    rows, width = grads.shape
    spec = pl.BlockSpec((1, NZ, WR, width), lambda k, ids: (k, 0, 0, 0))
    return pl.pallas_call(
        weight_grads_kernel,
        out_shape=[jax.ShapeDtypeStruct((NX, NZ, WR, width), BF)] * 2,
        grid_spec=pltpu.PrefetchScalarGridSpec(
            num_scalar_prefetch=1,
            grid=(NX,),
            in_specs=[
                pl.BlockSpec((BLK, rows), lambda k, ids: (k, 0)),
                pl.BlockSpec((rows, width), lambda k, ids: (0, 0)),
                pl.BlockSpec(memory_space=pl.ANY),
            ],
            out_specs=[spec, spec],
        ),
        compiler_params=params(),
        cost_estimate=pl.CostEstimate(
            flops=2 * rows * D * width, bytes_accessed=2 * D * (rows + width), transcendentals=0
        ),
        name="weight_grads",
    )(ids, scaled_t, grads, after)


def add_up(value):
    return jnp.sum(value.astype(F32), axis=0)


def reduce_weights(own, sib):
    both = (own.astype(F32) + shift(sib, "c", 1).astype(F32)).astype(BF)
    part = add_up(exchange(both, "x")).astype(BF)
    return add_up(exchange(part, "z"))


def per_device(
    prompt_states,
    answer_states,
    prompt_cotangent,
    answer_cotangent,
    norm_gain,
    weights,
    answer_length,
    answer_owner,
):
    x, z, c = lax.axis_index("x"), lax.axis_index("z"), lax.axis_index("c")
    ids = jnp.stack([x, z, c]).astype(jnp.int32)
    lengths, owners = answer_length[0], answer_owner[0]
    shard = weights[0]
    gain = norm_gain[0].astype(F32)

    kv_piece = spread(spread(shard[:, QC:], "z"), "x")
    q1_piece = spread(spread(shard[:, :HD], "x"), "z")
    q2_piece = spread(spread(shard[:, HD:QC], "z"), "x")
    kv_sib = shift(kv_piece, "c", 1)
    q1_sib = shift(q1_piece, "c", 1)
    q2_sib = shift(q2_piece, "c", 1)

    inputs = jnp.concatenate([prompt_states[0], answer_states[0]], axis=0)
    wide = inputs.astype(F32)
    inverse = lax.rsqrt(jnp.mean(wide * wide, axis=-1, keepdims=True) + EPSILON)
    scaled = (wide * inverse * gain).astype(BF)
    scaled_t = scaled.T

    kv, w_kv = project(ids, scaled, [(kv_piece, kv_sib)], ["xz"])
    pairs = spread(kv[:PR], ("x", "z"))
    pairs_sib = shift(pairs, "c", 1)
    q, w_q1, w_q2 = project(ids, scaled, [(q1_piece, q1_sib), (q2_piece, q2_sib)], ["zx", "xz"])
    wt_kv = w_kv.reshape(D, 2 * HD).T
    wt_q = jnp.concatenate([w_q1.reshape(D, HD).T, w_q2.reshape(D, QC - HD).T], axis=0)

    gq, gkv_answer, own, sib = attention(
        ids, owners, lengths, q, kv, prompt_cotangent[0], answer_cotangent[0], pairs, pairs_sib
    )

    answer_back = input_grads(
        gq[PR:], gkv_answer, q[PR:], kv[PR:], inverse[PR:], answer_states[0], norm_gain, wt_q, wt_kv
    )
    answer_out = shift(answer_back, "section", -1)

    terms = (own.astype(F32) + shift(sib, "c", 1).astype(F32)).astype(BF).reshape(NX * NZ, PR, 2 * HD)
    gkv_prompt = add_up(exchange(terms, ("x", "z"))).astype(BF)

    query_total = reduce_weights(*weight_grads(ids, scaled_t, gq, answer_back))

    gkv = jnp.concatenate([gkv_prompt, gkv_answer], axis=0)
    pair_own, pair_sib = weight_grads(ids, scaled_t, gkv, gkv)
    prompt_back = input_grads(
        gq[:PR], gkv_prompt, q[:PR], kv[:PR], inverse[:PR], prompt_states[0], norm_gain, wt_q, wt_kv
    )
    prompt_out = shift(prompt_back, "section", -1)
    pair_total = reduce_weights(pair_own, pair_sib)

    weight_total = jnp.concatenate([query_total, pair_total], axis=1)
    own_gain = lax.dynamic_slice(gain, (((x * NZ + z) * NC + c) * WR,), (WR,))
    gain_total = jnp.sum(weight_total * shard.astype(F32), axis=1) / own_gain
    return (prompt_out[None], answer_out[None], weight_total[None], gain_total[None])


def solution(mesh):
    fine = Mesh(mesh.devices.reshape(mesh.devices.shape[0], NX, NZ, NC), ("section", "x", "z", "c"))
    dp = ("x", "z", "c")
    placed = (
        P("section", dp, None),
        P("section", dp, None),
        P("section", dp, None),
        P("section", dp, None),
        P("section", None),
        P("section", dp, None),
        P("section", dp),
        P("section", dp),
    )
    return jax.shard_map(
        per_device,
        mesh=fine,
        in_specs=placed,
        out_specs=(
            P("section", dp, None),
            P("section", dp, None),
            P("section", dp, None),
            P("section", dp),
        ),
        check_vma=False,
    )
```

```python
import functools

import jax
import jax.numpy as jnp
from jax import lax
from jax.experimental import pallas as pl
from jax.experimental.pallas import tpu as pltpu
from jax.sharding import Mesh, PartitionSpec as P

HD = 128
HEADS = 4
QC = HEADS * HD
D = 5120
PR = 64
AR = 256
SLOTS = 4
SR = 64
NX, NZ, NC = 4, 8, 2
WR = 80
BLK = D // NX
PROMPTS = 16
PLEN = 256
EPSILON = 1e-06
SCALE = HD**-0.5
BF = jnp.bfloat16
F32 = jnp.float32
MIB = 1024 * 1024


def shift(value, axis, steps):
    count = lax.axis_size(axis)
    if steps % count == 0:
        return value
    return lax.ppermute(value, axis, [(s, (s + steps) % count) for s in range(count)])


def params(mib):
    return pltpu.CompilerParams(vmem_limit_bytes=mib * MIB)


def cheap():
    return pl.CostEstimate(flops=10**6, bytes_accessed=10**5, transcendentals=0)


ANY = pl.BlockSpec(memory_space=pl.ANY)
VM = pl.BlockSpec(memory_space=pltpu.VMEM)
SM = pl.BlockSpec(memory_space=pltpu.SMEM)


def nt(a, b):
    return lax.dot_general(a, b, (((1,), (1,)), ((), ())), preferred_element_type=F32)


def tn(a, b):
    return lax.dot_general(a, b, (((0,), (0,)), ((), ())), preferred_element_type=F32)


def nn(a, b):
    return jnp.dot(a, b, preferred_element_type=F32)


def exchange(value, axis):
    return lax.all_to_all(value, axis, 0, 0, tiled=True)


def spread(value, axis):
    count = lax.axis_size(axis)
    return exchange(jnp.broadcast_to(value[None], (count, *value.shape)), axis)


def placed_copies(value, lo, rows, count, after):
    def kernel(value_ref, *refs):
        out_ref = refs[-1]
        for i in range(count):
            out_ref[i] = value_ref[lo : lo + rows]

    return pl.pallas_call(
        kernel,
        out_shape=jax.ShapeDtypeStruct((count, rows, *value.shape[1:]), value.dtype),
        in_specs=[VM] + [ANY] * len(after),
        out_specs=VM,
        compiler_params=params(16),
        cost_estimate=cheap(),
        name="copies",
    )(value, *after)


def stack_after(pieces, after):
    def kernel(*refs):
        out_ref = refs[-1]
        for i in range(len(pieces)):
            out_ref[i] = refs[i][...]

    return pl.pallas_call(
        kernel,
        out_shape=jax.ShapeDtypeStruct((len(pieces), *pieces[0].shape), pieces[0].dtype),
        in_specs=[VM] * len(pieces) + [ANY],
        out_specs=VM,
        compiler_params=params(16),
        cost_estimate=cheap(),
        name="stack",
    )(*pieces, after)


def ring_x(value, after=None):
    rows = value.shape[0]
    cut = rows // 2
    up, down = shift(value, "x", 1), shift(value, "x", -1)
    if after is None:
        up_half, down_half = up[:cut], down[cut:]
    else:
        up_half = placed_copies(up, 0, cut, 1, after)[0]
        down_half = placed_copies(down, cut, cut, 1, after)[0]
    far = jnp.concatenate([shift(up_half, "x", 1), shift(down_half, "x", -1)], axis=0)
    return jnp.stack([value, up, far, down])


def norm_kernel(p_ref, a_ref, gain_ref, scaled_ref, inv_ref):
    gain = gain_ref[...].astype(F32)
    for ref, lo, rows in ((p_ref, 0, PR), (a_ref, PR, AR)):
        for r in range(0, rows, 32):
            wide = ref[r : r + 32, :].astype(F32)
            inv = lax.rsqrt(jnp.mean(wide * wide, axis=-1, keepdims=True) + EPSILON)
            scaled_ref[lo + r : lo + r + 32, :] = (wide * inv * gain).astype(BF)
            inv_ref[lo + r : lo + r + 32, :] = inv


def norm(prompt, answer, gain):
    rows = PR + AR
    return pl.pallas_call(
        norm_kernel,
        out_shape=[jax.ShapeDtypeStruct((rows, D), BF), jax.ShapeDtypeStruct((rows, 1), F32)],
        in_specs=[VM] * 3,
        out_specs=[VM] * 2,
        compiler_params=params(24),
        cost_estimate=cheap(),
        name="norm",
    )(prompt, answer, gain)


def place(ids, s_ref, t_ref, w_ref, sem):
    copies = []
    for k in range(NX):
        for rel in range(2):
            dst = w_ref.at[k, :, lax.rem(ids[2] + rel, 2)]
            copies.append(pltpu.make_async_copy((s_ref, t_ref)[rel].at[k], dst, sem.at[k, rel]))
            copies[-1].start()
    return copies


def block_columns(ids, k):
    return pl.ds(pl.multiple_of(lax.rem(ids[0] - k + NX, NX) * BLK, BLK), BLK)


def project_kernel(ids, a_ref, s_ref, t_ref, out_ref, w_ref, sem):
    width = w_ref.shape[-1]
    copies = place(ids, s_ref, t_ref, w_ref, sem)
    total = jnp.zeros((PR + AR, width), F32)
    for k in range(NX):
        copies[2 * k].wait()
        copies[2 * k + 1].wait()
        total += nn(a_ref[:, block_columns(ids, k)], w_ref[k].reshape(BLK, width))
    out_ref[...] = total.astype(BF)


def project(ids, scaled, pieces, pieces_sib):
    width = pieces.shape[-1]
    rows = scaled.shape[0]
    return pl.pallas_call(
        project_kernel,
        out_shape=jax.ShapeDtypeStruct((rows, width), BF),
        in_specs=[SM, VM, ANY, ANY],
        out_specs=VM,
        scratch_shapes=[pltpu.VMEM((NX, NZ, NC, WR, width), BF), pltpu.SemaphoreType.DMA((NX, 2))],
        compiler_params=params(16),
        cost_estimate=cheap(),
        name="project",
    )(ids, scaled, pieces, pieces_sib)


def stacked(value):
    return jnp.concatenate([value[:, h * HD : (h + 1) * HD] for h in range(HEADS)], axis=0)


def attention_kernel(
    ids, owners, lengths, q_ref, kv_ref, gp_ref, ga_ref, s_ref, t_ref, after_ref,
    gq_ref, gkv_ref, own_ref, sib_ref, pairs, dense, sem,
):
    del after_ref
    x, z, c = ids[0], ids[1], ids[2]
    own_prompt = x * 4 + z // 2
    prompts = [owners[s] for s in range(SLOTS)] + [own_prompt]
    copies = []
    for b, p in enumerate(prompts):
        k = lax.rem(x - p // 4 + NX, NX)
        for half in range(2):
            for rel in range(2):
                at = pl.multiple_of((half * 2 + lax.rem(c + rel, 2)) * PR, PR)
                src = (s_ref, t_ref)[rel].at[k, lax.rem(p, 4) * 2 + half]
                copies.append(pltpu.make_async_copy(src, pairs.at[b, pl.ds(at, PR)], sem.at[b, half, rel]))
                copies[-1].start()
    dense[...] = jnp.zeros_like(dense)
    row_step = lax.rem(lax.broadcasted_iota(jnp.int32, (HEADS * SR, SR), 0), SR)
    col_step = lax.broadcasted_iota(jnp.int32, (HEADS * SR, SR), 1)
    live_step = lax.broadcasted_iota(jnp.int32, (SR, QC), 0)
    per_block = 4
    for b in range(SLOTS + 1):
        for copy in copies[b * per_block : (b + 1) * per_block]:
            copy.wait()
        keys, values = pairs[b, :, :HD], pairs[b, :, HD:]
        if b < SLOTS:
            lo = PR + b * SR
            length = lengths[b]
            upstream = ga_ref[b * SR : (b + 1) * SR, :]
            upstream = jnp.where(live_step < length, upstream.astype(F32), 0.0).astype(BF)
        else:
            lo = 0
            upstream = gp_ref[...]
        q4 = stacked(q_ref[lo : lo + SR, :])
        g4 = stacked(upstream)
        s1 = SCALE * nt(q4, keys)
        gp1 = nt(g4, values)
        if b < SLOTS:
            k_own = kv_ref[lo : lo + SR, :HD]
            v_own = kv_ref[lo : lo + SR, HD:]
            s2 = SCALE * nt(q4, k_own)
            gp2 = nt(g4, v_own)
            seen = (row_step >= col_step) & (col_step < length)
            s2 = jnp.where(seen, s2, -jnp.inf)
            top = jnp.maximum(jnp.max(s1, axis=1, keepdims=True), jnp.max(s2, axis=1, keepdims=True))
            e1 = jnp.exp(s1 - top)
            e2 = jnp.exp(s2 - top)
            norm = 1.0 / (jnp.sum(e1, axis=1, keepdims=True) + jnp.sum(e2, axis=1, keepdims=True))
            p1 = e1 * norm
            p2 = e2 * norm
            delta = jnp.sum(p1 * gp1, axis=1, keepdims=True) + jnp.sum(p2 * gp2, axis=1, keepdims=True)
            d2 = (p2 * (gp2 - delta)).astype(BF)
        else:
            offset = (lax.rem(z, 2) * 2 + c) * PR
            rows = lax.rem(lax.broadcasted_iota(jnp.int32, (HEADS * SR, PLEN), 0), SR) + offset
            cols = lax.broadcasted_iota(jnp.int32, (HEADS * SR, PLEN), 1)
            s1 = jnp.where(rows >= cols, s1, -jnp.inf)
            top = jnp.max(s1, axis=1, keepdims=True)
            e1 = jnp.exp(s1 - top)
            p1 = e1 * (1.0 / jnp.sum(e1, axis=1, keepdims=True))
            delta = jnp.sum(p1 * gp1, axis=1, keepdims=True)
        d1 = (p1 * (gp1 - delta)).astype(BF)
        gq = nn(d1, keys)
        if b < SLOTS:
            gq += nn(d2, k_own)
            gkv_ref[b * SR : (b + 1) * SR, :HD] = (SCALE * tn(d2, q4)).astype(BF)
            gkv_ref[b * SR : (b + 1) * SR, HD:] = tn(p2.astype(BF), g4).astype(BF)
        gq = (SCALE * gq).astype(BF)
        for h in range(HEADS):
            gq_ref[lo : lo + SR, h * HD : (h + 1) * HD] = gq[h * SR : (h + 1) * SR, :]
        p = prompts[b]
        dense[p, :, :, :HD] += (SCALE * tn(d1, q4)).reshape(4, PR, HD)
        dense[p, :, :, HD:] += tn(p1.astype(BF), g4).reshape(4, PR, HD)
    for half in range(2):
        own_ref[:, half] = dense[:, half * 2 + c].astype(BF)
        sib_ref[:, half] = dense[:, half * 2 + 1 - c].astype(BF)


def attention(ids, owners, lengths, q, kv, gp, ga, pairs, pairs_sib, after):
    return pl.pallas_call(
        attention_kernel,
        out_shape=[
            jax.ShapeDtypeStruct((PR + AR, QC), BF),
            jax.ShapeDtypeStruct((AR, 2 * HD), BF),
            jax.ShapeDtypeStruct((PROMPTS, 2, PR, 2 * HD), BF),
            jax.ShapeDtypeStruct((PROMPTS, 2, PR, 2 * HD), BF),
        ],
        in_specs=[SM] * 3 + [VM] * 4 + [ANY] * 3,
        out_specs=[VM] * 4,
        scratch_shapes=[
            pltpu.VMEM((SLOTS + 1, PLEN, 2 * HD), BF),
            pltpu.VMEM((PROMPTS, 4, PR, 2 * HD), F32),
            pltpu.SemaphoreType.DMA((SLOTS + 1, 2, 2)),
        ],
        compiler_params=params(24),
        cost_estimate=cheap(),
        name="attention",
    )(ids, owners, lengths, q, kv, gp, ga, pairs, pairs_sib, after)


def input_grads_kernel(
    ids, gq_ref, gkv_ref, q_ref, kv_ref, inv_ref, gain_ref, x_ref, qs_ref, qt_ref, ks_ref, kt_ref,
    out_ref, wq, wkv, states, result, sem_q, sem_kv, sem_x, sem_out,
):
    q_copies = place(ids, qs_ref, qt_ref, wq, sem_q)
    kv_copies = place(ids, ks_ref, kt_ref, wkv, sem_kv)
    x_copy = pltpu.make_async_copy(x_ref, states, sem_x)
    x_copy.start()
    gq, gkv = gq_ref[...], gkv_ref[...]
    inv = inv_ref[...]
    row_dot = jnp.sum(gq.astype(F32) * q_ref[...].astype(F32), axis=1, keepdims=True)
    row_dot += jnp.sum(gkv.astype(F32) * kv_ref[...].astype(F32), axis=1, keepdims=True)
    coefficient = inv * inv * row_dot * (1.0 / D)
    out_copies = []
    for k in range(NX):
        for copy in q_copies[2 * k : 2 * k + 2] + kv_copies[2 * k : 2 * k + 2]:
            copy.wait()
        cols = block_columns(ids, k)
        hidden = nt(gq, wq[k].reshape(BLK, QC)) + nt(gkv, wkv[k].reshape(BLK, 2 * HD))
        if k == 0:
            x_copy.wait()
        moved = inv * gain_ref[:, cols].astype(F32) * hidden - states[:, cols].astype(F32) * coefficient
        result[k] = moved.astype(BF)
        out_copies.append(pltpu.make_async_copy(result.at[k], out_ref.at[:, cols], sem_out.at[k]))
        out_copies[-1].start()
    for copy in out_copies:
        copy.wait()


def input_grads(ids, gq, gkv, q, kv, inv, gain, states, q_pieces, q_sib, kv_pieces, kv_sib):
    rows = states.shape[0]
    return pl.pallas_call(
        input_grads_kernel,
        out_shape=jax.ShapeDtypeStruct((rows, D), BF),
        in_specs=[SM] + [VM] * 6 + [ANY] * 5,
        out_specs=ANY,
        scratch_shapes=[
            pltpu.VMEM((NX, NZ, NC, WR, QC), BF),
            pltpu.VMEM((NX, NZ, NC, WR, 2 * HD), BF),
            pltpu.VMEM((rows, D), BF),
            pltpu.VMEM((NX, rows, BLK), BF),
            pltpu.SemaphoreType.DMA((NX, 2)),
            pltpu.SemaphoreType.DMA((NX, 2)),
            pltpu.SemaphoreType.DMA,
            pltpu.SemaphoreType.DMA((NX,)),
        ],
        compiler_params=params(28),
        cost_estimate=cheap(),
        name="input_grads",
    )(ids, gq, gkv, q, kv, inv, gain, states, q_pieces, q_sib, kv_pieces, kv_sib)


def weight_grads_kernel(ids, own_ref, sib_ref, g_ref, gs_ref, after_ref, plus_ref, minus_ref, u_ref, l_ref, mine_ref):
    del after_ref
    x = ids[0]
    width = g_ref.shape[1]
    g, gs = g_ref[...], gs_ref[...]

    def product(k, lo, count):
        at = pl.ds(lax.rem(x + k, NX) * NZ + lo, count)
        rows = count * WR
        total = nn(own_ref[at].reshape(rows, PR + AR), g) + nn(sib_ref[at].reshape(rows, PR + AR), gs)
        return total.astype(BF).reshape(count, WR, width)

    half = NZ // 2
    plus_ref[0] = product(2, 0, half)
    minus_ref[0] = product(2, half, half)
    plus_ref[1] = product(1, half, half)
    minus_ref[1] = product(3, 0, half)
    u_ref[...] = product(1, 0, half)
    l_ref[...] = product(3, half, half)
    mine_ref[...] = product(0, 0, NZ)


def weight_grads(ids, own, sib, grads, grads_sib, after):
    width = grads.shape[1]
    half = NZ // 2

    def shape(*dims):
        return jax.ShapeDtypeStruct((*dims, WR, width), BF)

    return pl.pallas_call(
        weight_grads_kernel,
        out_shape=[shape(2, half), shape(2, half), shape(half), shape(half), shape(NZ)],
        in_specs=[SM] + [VM] * 4 + [ANY],
        out_specs=[VM] * 5,
        compiler_params=params(24),
        cost_estimate=cheap(),
        name="weight_grads",
    )(ids, own, sib, grads, grads_sib, after)


def add_up(value):
    return jnp.sum(value.astype(F32), axis=0)


def wide_sum(*values):
    total = values[0].astype(F32)
    for value in values[1:]:
        total += value.astype(F32)
    return total


def reduce_weights(plus, minus, upper, lower, mine):
    half = NZ // 2
    plus, minus = shift(plus, "x", 1), shift(minus, "x", -1)
    upper = shift(wide_sum(upper, plus[0]).astype(BF), "x", 1)
    lower = shift(wide_sum(lower, minus[0]).astype(BF), "x", -1)
    part = jnp.concatenate(
        [wide_sum(mine[:half], minus[1], upper), wide_sum(mine[half:], plus[1], lower)], axis=0
    ).astype(BF)
    return add_up(exchange(part, "z"))


def per_device(
    prompt_states,
    answer_states,
    prompt_cotangent,
    answer_cotangent,
    norm_gain,
    weights,
    answer_length,
    answer_owner,
):
    x, z, c = lax.axis_index("x"), lax.axis_index("z"), lax.axis_index("c")
    ids = jnp.stack([x, z, c]).astype(jnp.int32)
    lengths, owners = answer_length[0], answer_owner[0]
    shard = weights[0]
    gain = norm_gain[0].astype(F32)

    kv_line = spread(shard[:, QC:], "z")
    scaled, inverse = norm(prompt_states[0], answer_states[0], norm_gain)
    q_line = exchange(placed_copies(shard[:, :QC], 0, WR, NZ, (kv_line,)), "z")
    scaled_t = scaled.T.reshape(NX * NZ, NC, WR, PR + AR)
    own_t = lax.dynamic_index_in_dim(scaled_t, c, 1, keepdims=False)
    other_t = lax.dynamic_index_in_dim(scaled_t, 1 - c, 1, keepdims=False)
    sib_t = shift(other_t, "c", 1)
    kv_pieces = ring_x(placed_copies(kv_line, 0, NZ, 1, (inverse,))[0])
    kv_sib = shift(kv_pieces, "c", 1)
    kv = project(ids, scaled, kv_pieces, kv_sib)
    pair_line = spread(kv[:PR], "z")
    q_pieces = ring_x(placed_copies(q_line, 0, NZ, 1, (kv_pieces,))[0], (own_t, other_t, pair_line))
    q_sib = shift(q_pieces, "c", 1)
    q = project(ids, scaled, q_pieces, q_sib)
    pairs = stack_after([shift(pair_line, "x", k) for k in range(NX)], q)
    pairs_sib = shift(pairs, "c", 1)

    gq, gkv_answer, own, sib = attention(
        ids, owners, lengths, q, kv, prompt_cotangent[0], answer_cotangent[0], pairs, pairs_sib, sib_t
    )
    gq_sib = shift(gq, "c", 1)
    weight_pieces = (q_pieces, q_sib, kv_pieces, kv_sib)

    answer_back = input_grads(
        ids, gq[PR:], gkv_answer, q[PR:], kv[PR:], inverse[PR:], norm_gain, answer_states[0], *weight_pieces
    )
    answer_out = shift(answer_back, "section", -1)

    terms = (own.astype(F32) + shift(sib, "c", 1).astype(F32)).astype(BF).reshape(NX * NZ, PR, 2 * HD)
    gkv_prompt = add_up(exchange(terms, ("x", "z"))).astype(BF)

    query_total = reduce_weights(*weight_grads(ids, own_t, sib_t, gq, gq_sib, answer_back))

    gkv = jnp.concatenate([gkv_prompt, gkv_answer], axis=0)
    gkv_sib = shift(gkv, "c", 1)
    pair_parts = weight_grads(ids, own_t, sib_t, gkv, gkv_sib, gkv)
    prompt_back = input_grads(
        ids, gq[:PR], gkv_prompt, q[:PR], kv[:PR], inverse[:PR], norm_gain, prompt_states[0], *weight_pieces
    )
    prompt_out = shift(prompt_back, "section", -1)
    pair_total = reduce_weights(*pair_parts)

    weight_total = jnp.concatenate([query_total, pair_total], axis=1)
    own_gain = lax.dynamic_slice(gain, (((x * NZ + z) * NC + c) * WR,), (WR,))
    gain_total = jnp.sum(weight_total * shard.astype(F32), axis=1) / own_gain
    return (prompt_out[None], answer_out[None], weight_total[None], gain_total[None])


def solution(mesh):
    fine = Mesh(mesh.devices.reshape(mesh.devices.shape[0], NX, NZ, NC), ("section", "x", "z", "c"))
    dp = ("x", "z", "c")
    placed = (
        P("section", dp, None),
        P("section", dp, None),
        P("section", dp, None),
        P("section", dp, None),
        P("section", None),
        P("section", dp, None),
        P("section", dp),
        P("section", dp),
    )
    return jax.shard_map(
        per_device,
        mesh=fine,
        in_specs=placed,
        out_specs=(
            P("section", dp, None),
            P("section", dp, None),
            P("section", dp, None),
            P("section", dp),
        ),
        check_vma=False,
    )
```

```python
import functools

import jax
import jax.numpy as jnp
from jax import lax
from jax.experimental import pallas as pl
from jax.experimental.pallas import tpu as pltpu
from jax.sharding import Mesh, PartitionSpec as P

HD = 128
HEADS = 4
QC = HEADS * HD
D = 5120
PR = 64
AR = 256
SLOTS = 4
SR = 64
NX, NZ, NC = 4, 8, 2
WR = 80
BLK = D // NX
PROMPTS = 16
PLEN = 256
EPSILON = 1e-06
SCALE = HD**-0.5
BF = jnp.bfloat16
F32 = jnp.float32
MIB = 1024 * 1024


def shift(value, axis, steps):
    count = lax.axis_size(axis)
    if steps % count == 0:
        return value
    return lax.ppermute(value, axis, [(s, (s + steps) % count) for s in range(count)])


def params(mib):
    return pltpu.CompilerParams(vmem_limit_bytes=mib * MIB)


def cheap():
    return pl.CostEstimate(flops=10**6, bytes_accessed=10**5, transcendentals=0)


ANY = pl.BlockSpec(memory_space=pl.ANY)
HBM = pl.BlockSpec(memory_space=pltpu.HBM)
VM = pl.BlockSpec(memory_space=pltpu.VMEM)
SM = pl.BlockSpec(memory_space=pltpu.SMEM)


def nt(a, b):
    return lax.dot_general(a, b, (((1,), (1,)), ((), ())), preferred_element_type=F32)


def tn(a, b):
    return lax.dot_general(a, b, (((0,), (0,)), ((), ())), preferred_element_type=F32)


def nn(a, b):
    return jnp.dot(a, b, preferred_element_type=F32)


def exchange(value, axis):
    return lax.all_to_all(value, axis, 0, 0, tiled=True)


def spread(value, axis):
    count = lax.axis_size(axis)
    return exchange(jnp.broadcast_to(value[None], (count, *value.shape)), axis)


def placed_copies(value, rows, columns, count, after):
    row_part, column_part = slice(*rows), slice(*columns)

    def kernel(value_ref, *refs):
        out_ref = refs[-1]
        for i in range(count):
            out_ref[i] = value_ref[row_part, ..., column_part]

    middle = value.shape[1:-1]
    shape = (count, rows[1] - rows[0], *middle, columns[1] - columns[0])
    return pl.pallas_call(
        kernel,
        out_shape=jax.ShapeDtypeStruct(shape, value.dtype),
        in_specs=[VM] + [ANY] * len(after),
        out_specs=VM,
        compiler_params=params(4),
        cost_estimate=cheap(),
        name="copies",
    )(value, *after)


def add_after(left, right, after):
    def kernel(left_ref, right_ref, *refs):
        out_ref = refs[-1]
        out_ref[...] = (left_ref[...].astype(F32) + right_ref[0].astype(F32)).astype(BF)

    return pl.pallas_call(
        kernel,
        out_shape=jax.ShapeDtypeStruct(left.shape, BF),
        in_specs=[VM, VM] + [ANY] * len(after),
        out_specs=VM,
        compiler_params=params(6),
        cost_estimate=cheap(),
        name="add",
    )(left, right, *after)


def forward(value):
    def kernel(value_ref, out_ref, sem):
        copy = pltpu.make_async_copy(value_ref, out_ref, sem)
        copy.start()
        copy.wait()

    return pl.pallas_call(
        kernel,
        out_shape=jax.ShapeDtypeStruct(value.shape, value.dtype),
        in_specs=[ANY],
        out_specs=HBM,
        scratch_shapes=[pltpu.SemaphoreType.DMA],
        compiler_params=params(4),
        cost_estimate=cheap(),
        name="forward",
    )(value)


def stack_after(pieces, after):
    def kernel(*refs):
        out_ref = refs[-1]
        for i in range(len(pieces)):
            out_ref[i] = refs[i][...]

    return pl.pallas_call(
        kernel,
        out_shape=jax.ShapeDtypeStruct((len(pieces), *pieces[0].shape), pieces[0].dtype),
        in_specs=[VM] * len(pieces) + [ANY],
        out_specs=VM,
        compiler_params=params(4),
        cost_estimate=cheap(),
        name="stack",
    )(*pieces, after)


def ring_x(value, after=()):
    rows, width = value.shape[0], value.shape[-1]
    cut = rows // 2
    up, down = shift(value, "x", 1), shift(value, "x", -1)
    up_half = placed_copies(up, (0, cut), (0, width), 1, after)[0]
    down_half = placed_copies(down, (cut, rows), (0, width), 1, after)[0]
    far = jnp.concatenate([shift(up_half, "x", 1), shift(down_half, "x", -1)], axis=0)
    return jnp.stack([value, up, far, down]), up, far


def norm_kernel(p_ref, a_ref, gain_ref, scaled_ref, inv_ref):
    gain = gain_ref[...].astype(F32)
    for ref, lo, rows in ((p_ref, 0, PR), (a_ref, PR, AR)):
        for r in range(0, rows, 32):
            wide = ref[r : r + 32, :].astype(F32)
            inv = lax.rsqrt(jnp.mean(wide * wide, axis=-1, keepdims=True) + EPSILON)
            scaled_ref[lo + r : lo + r + 32, :] = (wide * inv * gain).astype(BF)
            inv_ref[lo + r : lo + r + 32, :] = inv


def norm(prompt, answer, gain):
    rows = PR + AR
    return pl.pallas_call(
        norm_kernel,
        out_shape=[jax.ShapeDtypeStruct((rows, D), BF), jax.ShapeDtypeStruct((rows, 1), F32)],
        in_specs=[VM] * 3,
        out_specs=[VM] * 2,
        compiler_params=params(16),
        cost_estimate=cheap(),
        name="norm",
    )(prompt, answer, gain)


def place(ids, s_ref, t_ref, w_ref, sem):
    copies = []
    for k in range(NX):
        for rel in range(2):
            dst = w_ref.at[k, :, lax.rem(ids[2] + rel, 2)]
            copies.append(pltpu.make_async_copy((s_ref, t_ref)[rel].at[k], dst, sem.at[k, rel]))
            copies[-1].start()
    return copies


def block_columns(ids, k):
    return pl.ds(pl.multiple_of(lax.rem(ids[0] - k + NX, NX) * BLK, BLK), BLK)


def project_kernel(ids, a_ref, s_ref, t_ref, out_ref, w_ref, sem):
    width = w_ref.shape[-1]
    copies = place(ids, s_ref, t_ref, w_ref, sem)
    total = jnp.zeros((PR + AR, width), F32)
    for k in range(NX):
        copies[2 * k].wait()
        copies[2 * k + 1].wait()
        total += nn(a_ref[:, block_columns(ids, k)], w_ref[k].reshape(BLK, width))
    out_ref[...] = total.astype(BF)


def project(ids, scaled, pieces, pieces_sib):
    width = pieces.shape[-1]
    rows = scaled.shape[0]
    return pl.pallas_call(
        project_kernel,
        out_shape=jax.ShapeDtypeStruct((rows, width), BF),
        in_specs=[SM, VM, HBM, HBM],
        out_specs=VM,
        scratch_shapes=[pltpu.VMEM((NX, NZ, NC, WR, width), BF), pltpu.SemaphoreType.DMA((NX, 2))],
        compiler_params=params(16),
        cost_estimate=cheap(),
        name="project",
    )(ids, scaled, pieces, pieces_sib)


def stacked(value):
    return jnp.concatenate([value[:, h * HD : (h + 1) * HD] for h in range(HEADS)], axis=0)


def attention_kernel(
    ids, owners, lengths, q_ref, kv_ref, gp_ref, ga_ref, s_ref, t_ref, after_ref,
    gq_ref, gkv_ref, own_ref, sib_ref, pairs, dense, sem,
):
    del after_ref
    x, z, c = ids[0], ids[1], ids[2]
    own_prompt = x * 4 + z // 2
    prompts = [owners[s] for s in range(SLOTS)] + [own_prompt]
    copies = []
    for b, p in enumerate(prompts):
        k = lax.rem(x - p // 4 + NX, NX)
        for half in range(2):
            for rel in range(2):
                at = pl.multiple_of((half * 2 + lax.rem(c + rel, 2)) * PR, PR)
                src = (s_ref, t_ref)[rel].at[k, lax.rem(p, 4) * 2 + half]
                copies.append(pltpu.make_async_copy(src, pairs.at[b, pl.ds(at, PR)], sem.at[b, half, rel]))
                copies[-1].start()
    dense[...] = jnp.zeros_like(dense)
    row_step = lax.rem(lax.broadcasted_iota(jnp.int32, (HEADS * SR, SR), 0), SR)
    col_step = lax.broadcasted_iota(jnp.int32, (HEADS * SR, SR), 1)
    live_step = lax.broadcasted_iota(jnp.int32, (SR, QC), 0)
    per_block = 4
    for b in range(SLOTS + 1):
        for copy in copies[b * per_block : (b + 1) * per_block]:
            copy.wait()
        keys, values = pairs[b, :, :HD], pairs[b, :, HD:]
        if b < SLOTS:
            lo = PR + b * SR
            length = lengths[b]
            upstream = ga_ref[b * SR : (b + 1) * SR, :]
            upstream = jnp.where(live_step < length, upstream.astype(F32), 0.0).astype(BF)
        else:
            lo = 0
            upstream = gp_ref[...]
        q4 = stacked(q_ref[lo : lo + SR, :])
        g4 = stacked(upstream)
        s1 = SCALE * nt(q4, keys)
        gp1 = nt(g4, values)
        if b < SLOTS:
            k_own = kv_ref[lo : lo + SR, :HD]
            v_own = kv_ref[lo : lo + SR, HD:]
            s2 = SCALE * nt(q4, k_own)
            gp2 = nt(g4, v_own)
            seen = (row_step >= col_step) & (col_step < length)
            s2 = jnp.where(seen, s2, -jnp.inf)
            top = jnp.maximum(jnp.max(s1, axis=1, keepdims=True), jnp.max(s2, axis=1, keepdims=True))
            e1 = jnp.exp(s1 - top)
            e2 = jnp.exp(s2 - top)
            norm = 1.0 / (jnp.sum(e1, axis=1, keepdims=True) + jnp.sum(e2, axis=1, keepdims=True))
            p1 = e1 * norm
            p2 = e2 * norm
            delta = jnp.sum(p1 * gp1, axis=1, keepdims=True) + jnp.sum(p2 * gp2, axis=1, keepdims=True)
            d2 = (p2 * (gp2 - delta)).astype(BF)
        else:
            offset = (lax.rem(z, 2) * 2 + c) * PR
            rows = lax.rem(lax.broadcasted_iota(jnp.int32, (HEADS * SR, PLEN), 0), SR) + offset
            cols = lax.broadcasted_iota(jnp.int32, (HEADS * SR, PLEN), 1)
            s1 = jnp.where(rows >= cols, s1, -jnp.inf)
            top = jnp.max(s1, axis=1, keepdims=True)
            e1 = jnp.exp(s1 - top)
            p1 = e1 * (1.0 / jnp.sum(e1, axis=1, keepdims=True))
            delta = jnp.sum(p1 * gp1, axis=1, keepdims=True)
        d1 = (p1 * (gp1 - delta)).astype(BF)
        gq = nn(d1, keys)
        if b < SLOTS:
            gq += nn(d2, k_own)
            gkv_ref[b * SR : (b + 1) * SR, :HD] = (SCALE * tn(d2, q4)).astype(BF)
            gkv_ref[b * SR : (b + 1) * SR, HD:] = tn(p2.astype(BF), g4).astype(BF)
        gq = (SCALE * gq).astype(BF)
        for h in range(HEADS):
            gq_ref[lo : lo + SR, h * HD : (h + 1) * HD] = gq[h * SR : (h + 1) * SR, :]
        p = prompts[b]
        dense[p, :, :, :HD] += (SCALE * tn(d1, q4)).reshape(4, PR, HD)
        dense[p, :, :, HD:] += tn(p1.astype(BF), g4).reshape(4, PR, HD)
    for half in range(2):
        own_ref[:, half] = dense[:, half * 2 + c].astype(BF)
        sib_ref[:, half] = dense[:, half * 2 + 1 - c].astype(BF)


def attention(ids, owners, lengths, q, kv, gp, ga, pairs, pairs_sib, after):
    return pl.pallas_call(
        attention_kernel,
        out_shape=[
            jax.ShapeDtypeStruct((PR + AR, QC), BF),
            jax.ShapeDtypeStruct((AR, 2 * HD), BF),
            jax.ShapeDtypeStruct((PROMPTS, 2, PR, 2 * HD), BF),
            jax.ShapeDtypeStruct((PROMPTS, 2, PR, 2 * HD), BF),
        ],
        in_specs=[SM] * 3 + [VM] * 4 + [ANY] * 3,
        out_specs=[VM] * 4,
        scratch_shapes=[
            pltpu.VMEM((SLOTS + 1, PLEN, 2 * HD), BF),
            pltpu.VMEM((PROMPTS, 4, PR, 2 * HD), F32),
            pltpu.SemaphoreType.DMA((SLOTS + 1, 2, 2)),
        ],
        compiler_params=params(16),
        cost_estimate=cheap(),
        name="attention",
    )(ids, owners, lengths, q, kv, gp, ga, pairs, pairs_sib, after)


def row_coefficient(gq, gkv, q, kv, inv):
    row_dot = jnp.sum(gq.astype(F32) * q.astype(F32), axis=1, keepdims=True)
    row_dot += jnp.sum(gkv.astype(F32) * kv.astype(F32), axis=1, keepdims=True)
    return inv * inv * row_dot * (1.0 / D)


def answer_grads_kernel(
    ids, gq_ref, gkv_ref, q_ref, kv_ref, inv_ref, gain_ref, x_ref, qs_ref, qt_ref, ks_ref, kt_ref,
    out_ref, share_ref, wq, wkv, states, result, sem_q, sem_kv, sem_x, sem_out,
):
    q_copies = place(ids, qs_ref, qt_ref, wq, sem_q)
    kv_copies = place(ids, ks_ref, kt_ref, wkv, sem_kv)
    x_copy = pltpu.make_async_copy(x_ref, states, sem_x)
    x_copy.start()
    gq, gkv = gq_ref[...], gkv_ref[...]
    inv = inv_ref[PR:, :]
    coefficient = row_coefficient(gq_ref[PR:, :], gkv, q_ref[PR:, :], kv_ref[PR:, :], inv)
    out_copies = []
    for k in range(NX):
        for copy in q_copies[2 * k : 2 * k + 2] + kv_copies[2 * k : 2 * k + 2]:
            copy.wait()
        cols = block_columns(ids, k)
        by_query = nt(gq, wq[k].reshape(BLK, QC))
        share_ref[:, cols] = by_query[:PR]
        hidden = by_query[PR:] + nt(gkv, wkv[k].reshape(BLK, 2 * HD))
        if k == 0:
            x_copy.wait()
        moved = inv * gain_ref[:, cols].astype(F32) * hidden - states[:, cols].astype(F32) * coefficient
        result[k] = moved.astype(BF)
        out_copies.append(pltpu.make_async_copy(result.at[k], out_ref.at[:, cols], sem_out.at[k]))
        out_copies[-1].start()
    for copy in out_copies:
        copy.wait()


def answer_grads(ids, gq, gkv, q, kv, inv, gain, states, pieces):
    return pl.pallas_call(
        answer_grads_kernel,
        out_shape=[jax.ShapeDtypeStruct((AR, D), BF), jax.ShapeDtypeStruct((PR, D), F32)],
        in_specs=[SM] + [VM] * 6 + [HBM] * 5,
        out_specs=[HBM, VM],
        scratch_shapes=[
            pltpu.VMEM((NX, NZ, NC, WR, QC), BF),
            pltpu.VMEM((NX, NZ, NC, WR, 2 * HD), BF),
            pltpu.VMEM((AR, D), BF),
            pltpu.VMEM((NX, AR, BLK), BF),
            pltpu.SemaphoreType.DMA((NX, 2)),
            pltpu.SemaphoreType.DMA((NX, 2)),
            pltpu.SemaphoreType.DMA,
            pltpu.SemaphoreType.DMA((NX,)),
        ],
        compiler_params=params(24),
        cost_estimate=cheap(),
        name="answer_grads",
    )(ids, gq, gkv, q, kv, inv, gain, states, *pieces)


def prompt_grads_kernel(
    ids, gq_ref, gkv_ref, q_ref, kv_ref, inv_ref, gain_ref, x_ref, share_ref, ks_ref, kt_ref, out_ref, wkv, sem
):
    copies = place(ids, ks_ref, kt_ref, wkv, sem)
    gkv = gkv_ref[...]
    inv = inv_ref[:PR, :]
    coefficient = row_coefficient(gq_ref[:PR, :], gkv, q_ref[:PR, :], kv_ref[:PR, :], inv)
    for k in range(NX):
        copies[2 * k].wait()
        copies[2 * k + 1].wait()
        cols = block_columns(ids, k)
        hidden = share_ref[:, cols] + nt(gkv, wkv[k].reshape(BLK, 2 * HD))
        moved = inv * gain_ref[:, cols].astype(F32) * hidden - x_ref[:, cols].astype(F32) * coefficient
        out_ref[:, cols] = moved.astype(BF)


def prompt_grads(ids, gq, gkv, q, kv, inv, gain, states, share, pieces):
    return pl.pallas_call(
        prompt_grads_kernel,
        out_shape=jax.ShapeDtypeStruct((PR, D), BF),
        in_specs=[SM] + [VM] * 8 + [HBM] * 2,
        out_specs=VM,
        scratch_shapes=[pltpu.VMEM((NX, NZ, NC, WR, 2 * HD), BF), pltpu.SemaphoreType.DMA((NX, 2))],
        compiler_params=params(12),
        cost_estimate=cheap(),
        name="prompt_grads",
    )(ids, gq, gkv, q, kv, inv, gain, states, share, *pieces)


def weight_grads_kernel(ids, own_ref, sib_ref, g_ref, gs_ref, *refs):
    plus_ref, minus_ref, u_ref, l_ref, mine_ref = refs[-5:]
    x = ids[0]
    width = g_ref.shape[1]
    g, gs = g_ref[...], gs_ref[...]

    def product(k, lo, count):
        at = pl.ds(lax.rem(x + k, NX) * NZ + lo, count)
        rows = count * WR
        total = nn(own_ref[at].reshape(rows, PR + AR), g) + nn(sib_ref[at].reshape(rows, PR + AR), gs)
        return total.astype(BF).reshape(count, WR, width)

    half = NZ // 2
    plus_ref[0] = product(2, 0, half)
    minus_ref[0] = product(2, half, half)
    plus_ref[1] = product(1, half, half)
    minus_ref[1] = product(3, 0, half)
    u_ref[...] = product(1, 0, half)
    l_ref[...] = product(3, half, half)
    mine_ref[...] = product(0, 0, NZ)


def weight_grads(ids, own, sib, grads, grads_sib, after):
    width = grads.shape[1]
    half = NZ // 2

    def shape(*dims):
        return jax.ShapeDtypeStruct((*dims, WR, width), BF)

    return pl.pallas_call(
        weight_grads_kernel,
        out_shape=[shape(2, half), shape(2, half), shape(half), shape(half), shape(NZ)],
        in_specs=[SM] + [VM] * 4 + [ANY] * len(after),
        out_specs=[VM] * 5,
        compiler_params=params(16),
        cost_estimate=cheap(),
        name="weight_grads",
    )(ids, own, sib, grads, grads_sib, *after)


def add_up(value):
    return jnp.sum(value.astype(F32), axis=0)


def join(upper, lower, plus, minus, mine, after):
    half = NZ // 2

    def kernel(upper_ref, lower_ref, plus_ref, minus_ref, mine_ref, *refs):
        out_ref = refs[-1]
        first = mine_ref[:half].astype(F32) + minus_ref[1].astype(F32) + upper_ref[...].astype(F32)
        second = mine_ref[half:].astype(F32) + plus_ref[1].astype(F32) + lower_ref[...].astype(F32)
        out_ref[:half] = first.astype(BF)
        out_ref[half:] = second.astype(BF)

    return pl.pallas_call(
        kernel,
        out_shape=jax.ShapeDtypeStruct(mine.shape, BF),
        in_specs=[VM] * 5 + [ANY] * len(after),
        out_specs=VM,
        compiler_params=params(10),
        cost_estimate=cheap(),
        name="join",
    )(upper, lower, plus, minus, mine, *after)


def first_hop(plus, minus):
    return shift(plus, "x", 1), shift(minus, "x", -1)


def second_hop(plus, minus, upper, lower, after):
    return shift(add_after(upper, plus, after), "x", 1), shift(add_after(lower, minus, after), "x", -1)


def per_device(
    prompt_states,
    answer_states,
    prompt_cotangent,
    answer_cotangent,
    norm_gain,
    weights,
    answer_length,
    answer_owner,
):
    x, z, c = lax.axis_index("x"), lax.axis_index("z"), lax.axis_index("c")
    ids = jnp.stack([x, z, c]).astype(jnp.int32)
    lengths, owners = answer_length[0], answer_owner[0]
    shard = weights[0]
    gain = norm_gain[0].astype(F32)

    line = spread(shard, "z")
    scaled, inverse = norm(prompt_states[0], answer_states[0], norm_gain)
    scaled_t = scaled.T.reshape(NX * NZ, NC, WR, PR + AR)
    own_t = lax.dynamic_index_in_dim(scaled_t, c, 1, keepdims=False)
    other_t = lax.dynamic_index_in_dim(scaled_t, 1 - c, 1, keepdims=False)
    sib_t = shift(other_t, "c", 1)
    kv_line = placed_copies(line, (0, NZ), (QC, QC + 2 * HD), 1, (inverse,))[0]
    kv_pieces, kv_up, kv_far = ring_x(kv_line)
    kv_sib = shift(kv_pieces, "c", 1)
    kv = project(ids, scaled, kv_pieces, kv_sib)
    pair_line = spread(kv[:PR], "z")
    q_line = placed_copies(line, (0, NZ), (0, QC), 1, (kv_up,))[0]
    q_pieces, _, _ = ring_x(q_line, (own_t, other_t, pair_line))
    q_sib = shift(q_pieces, "c", 1)
    q = project(ids, scaled, q_pieces, q_sib)
    pairs = stack_after([shift(pair_line, "x", k) for k in range(NX)], q)
    pairs_sib = shift(pairs, "c", 1)

    gq, gkv_answer, own, sib = attention(
        ids, owners, lengths, q, kv, prompt_cotangent[0], answer_cotangent[0], pairs, pairs_sib, sib_t
    )
    gq_sib = shift(gq, "c", 1)
    answer_back, share = answer_grads(
        ids, gq, gkv_answer, q, kv, inverse, norm_gain, answer_states[0], (q_pieces, q_sib, kv_pieces, kv_sib)
    )
    answer_out = shift(answer_back, "section", -1)
    query_parts = weight_grads(ids, own_t, sib_t, gq, gq_sib, (answer_back,))
    query_hop = first_hop(*query_parts[:2])

    terms = (own.astype(F32) + shift(sib, "c", 1).astype(F32)).astype(BF).reshape(NX * NZ, PR, 2 * HD)
    gkv_prompt = add_up(exchange(terms, ("x", "z"))).astype(BF)
    gkv = jnp.concatenate([gkv_prompt, gkv_answer], axis=0)
    gkv_sib = shift(gkv, "c", 1)
    pair_parts = weight_grads(ids, own_t, sib_t, gkv, gkv_sib, query_hop)
    pair_hop = first_hop(*pair_parts[:2])
    query_second = second_hop(*query_hop, *query_parts[2:4], (pair_parts[0],))
    prompt_back = prompt_grads(
        ids, gq, gkv_prompt, q, kv, inverse, norm_gain, prompt_states[0], share, (kv_pieces, kv_sib)
    )
    prompt_out = forward(shift(prompt_back, "section", -1))
    pair_second = second_hop(*pair_hop, *pair_parts[2:4], (prompt_back,))
    query_last = exchange(join(*query_second, *query_hop, query_parts[4], pair_hop), "z")
    pair_last = exchange(join(*pair_second, *pair_hop, pair_parts[4], (answer_out, query_last)), "z")
    query_total, pair_total = add_up(query_last), add_up(pair_last)

    weight_total = jnp.concatenate([query_total, pair_total], axis=1)
    own_gain = lax.dynamic_slice(gain, (((x * NZ + z) * NC + c) * WR,), (WR,))
    gain_total = jnp.sum(weight_total * shard.astype(F32), axis=1) / own_gain
    return (prompt_out[None], forward(answer_out)[None], weight_total[None], gain_total[None])


def solution(mesh):
    fine = Mesh(mesh.devices.reshape(mesh.devices.shape[0], NX, NZ, NC), ("section", "x", "z", "c"))
    dp = ("x", "z", "c")
    placed = (
        P("section", dp, None),
        P("section", dp, None),
        P("section", dp, None),
        P("section", dp, None),
        P("section", None),
        P("section", dp, None),
        P("section", dp),
        P("section", dp),
    )
    return jax.shard_map(
        per_device,
        mesh=fine,
        in_specs=placed,
        out_specs=(
            P("section", dp, None),
            P("section", dp, None),
            P("section", dp, None),
            P("section", dp),
        ),
        check_vma=False,
    )
```

```python
import functools

import jax
import jax.numpy as jnp
from jax import lax
from jax.experimental import pallas as pl
from jax.experimental.pallas import tpu as pltpu
from jax.sharding import Mesh, PartitionSpec as P

HD = 128
HEADS = 4
QC = HEADS * HD
D = 5120
PR = 64
AR = 256
SLOTS = 4
SR = 64
NX, NZ, NC = 4, 8, 2
WR = 80
BLK = D // NX
PROMPTS = 16
PLEN = 256
EPSILON = 1e-06
SCALE = HD**-0.5
BF = jnp.bfloat16
F32 = jnp.float32
MIB = 1024 * 1024


def shift(value, axis, steps):
    count = lax.axis_size(axis)
    if steps % count == 0:
        return value
    return lax.ppermute(value, axis, [(s, (s + steps) % count) for s in range(count)])


def params(mib):
    return pltpu.CompilerParams(vmem_limit_bytes=mib * MIB)


def cheap():
    return pl.CostEstimate(flops=10**6, bytes_accessed=10**5, transcendentals=0)


ANY = pl.BlockSpec(memory_space=pl.ANY)
HBM = pl.BlockSpec(memory_space=pltpu.HBM)
VM = pl.BlockSpec(memory_space=pltpu.VMEM)
SM = pl.BlockSpec(memory_space=pltpu.SMEM)


def nt(a, b):
    return lax.dot_general(a, b, (((1,), (1,)), ((), ())), preferred_element_type=F32)


def tn(a, b):
    return lax.dot_general(a, b, (((0,), (0,)), ((), ())), preferred_element_type=F32)


def nn(a, b):
    return jnp.dot(a, b, preferred_element_type=F32)


def exchange(value, axis):
    return lax.all_to_all(value, axis, 0, 0, tiled=True)


def spread(value, axis):
    count = lax.axis_size(axis)
    return exchange(jnp.broadcast_to(value[None], (count, *value.shape)), axis)


def placed_copies(value, rows, columns, count, after):
    row_part, column_part = slice(*rows), slice(*columns)

    def kernel(value_ref, *refs):
        out_ref = refs[-1]
        for i in range(count):
            out_ref[i] = value_ref[row_part, ..., column_part]

    middle = value.shape[1:-1]
    shape = (count, rows[1] - rows[0], *middle, columns[1] - columns[0])
    return pl.pallas_call(
        kernel,
        out_shape=jax.ShapeDtypeStruct(shape, value.dtype),
        in_specs=[VM] + [ANY] * len(after),
        out_specs=VM,
        compiler_params=params(4),
        cost_estimate=cheap(),
        name="copies",
    )(value, *after)


def add_after(left, right, after):
    def kernel(left_ref, right_ref, *refs):
        out_ref = refs[-1]
        out_ref[...] = (left_ref[...].astype(F32) + right_ref[0].astype(F32)).astype(BF)

    return pl.pallas_call(
        kernel,
        out_shape=jax.ShapeDtypeStruct(left.shape, BF),
        in_specs=[VM, VM] + [ANY] * len(after),
        out_specs=VM,
        compiler_params=params(6),
        cost_estimate=cheap(),
        name="add",
    )(left, right, *after)


def forward(value):
    rows, width = value.shape
    spec = pl.BlockSpec((32, width), lambda i: (i, 0))

    def kernel(value_ref, out_ref):
        out_ref[...] = value_ref[...]

    return pl.pallas_call(
        kernel,
        out_shape=jax.ShapeDtypeStruct(value.shape, value.dtype),
        grid=(rows // 32,),
        in_specs=[spec],
        out_specs=spec,
        compiler_params=params(4),
        cost_estimate=cheap(),
        name="forward",
    )(value)


def stack_after(pieces, after):
    def kernel(*refs):
        out_ref = refs[-1]
        for i in range(len(pieces)):
            out_ref[i] = refs[i][...]

    return pl.pallas_call(
        kernel,
        out_shape=jax.ShapeDtypeStruct((len(pieces), *pieces[0].shape), pieces[0].dtype),
        in_specs=[VM] * len(pieces) + [ANY],
        out_specs=VM,
        compiler_params=params(4),
        cost_estimate=cheap(),
        name="stack",
    )(*pieces, after)


def held(value, after):
    return placed_copies(value, (0, value.shape[0]), (0, value.shape[-1]), 1, after)[0]


def ring_x(value):
    cut = value.shape[0] // 2
    up, down = shift(value, "x", 1), shift(value, "x", -1)
    far = jnp.concatenate([shift(up[:cut], "x", 1), shift(down[cut:], "x", -1)], axis=0)
    return jnp.stack([value, up, far, down]), (up, down)


def direct_x(value):
    return jnp.stack([shift(value, "x", k) for k in range(NX)])


def ring_z(value, gates):
    half = NZ // 2
    value = held(value, gates[0])
    pieces = {0: value}
    up = down = value
    for j in range(1, half):
        if j > 1:
            up, down = held(up, gates[j - 1]), held(down, gates[j - 1])
        up, down = shift(up, "z", 1), shift(down, "z", -1)
        pieces[j], pieces[NZ - j] = up, down
    rows, width = value.shape[0], value.shape[-1]
    cut = rows // 2
    up_half = placed_copies(up, (0, cut), (0, width), 1, gates[3])[0]
    down_half = placed_copies(down, (cut, rows), (0, width), 1, gates[3])[0]
    pieces[half] = jnp.concatenate([shift(up_half, "z", 1), shift(down_half, "z", -1)], axis=0)
    return jnp.stack([pieces[j] for j in range(NZ)])


def norm_kernel(p_ref, a_ref, gain_ref, scaled_ref, inv_ref):
    gain = gain_ref[...].astype(F32)
    for ref, lo, rows in ((p_ref, 0, PR), (a_ref, PR, AR)):
        for r in range(0, rows, 32):
            wide = ref[r : r + 32, :].astype(F32)
            inv = lax.rsqrt(jnp.mean(wide * wide, axis=-1, keepdims=True) + EPSILON)
            scaled_ref[lo + r : lo + r + 32, :] = (wide * inv * gain).astype(BF)
            inv_ref[lo + r : lo + r + 32, :] = inv


def norm(prompt, answer, gain):
    rows = PR + AR
    return pl.pallas_call(
        norm_kernel,
        out_shape=[jax.ShapeDtypeStruct((rows, D), BF), jax.ShapeDtypeStruct((rows, 1), F32)],
        in_specs=[VM] * 3,
        out_specs=[VM] * 2,
        compiler_params=params(16),
        cost_estimate=cheap(),
        name="norm",
    )(prompt, answer, gain)


def place(ids, s_ref, t_ref, w_ref, sem):
    if s_ref.shape[0] == NX:
        copies = []
        for k in range(NX):
            for rel in range(2):
                dst = w_ref.at[k, :, lax.rem(ids[2] + rel, 2)]
                copies.append(pltpu.make_async_copy((s_ref, t_ref)[rel].at[k], dst, sem.at[k, rel]))
                copies[-1].start()
        return [copies[2 * k : 2 * k + 2] for k in range(NX)]
    copies = []
    for j in range(NZ):
        for rel in range(2):
            dst = w_ref.at[:, lax.rem(ids[1] - j + NZ, NZ), lax.rem(ids[2] + rel, 2)]
            copies.append(pltpu.make_async_copy((s_ref, t_ref)[rel].at[j], dst, sem.at[j, rel]))
            copies[-1].start()
    return [copies, [], [], []]


def block_columns(ids, k):
    return pl.ds(pl.multiple_of(lax.rem(ids[0] - k + NX, NX) * BLK, BLK), BLK)


def project_kernel(ids, a_ref, s_ref, t_ref, out_ref, w_ref, sem):
    width = w_ref.shape[-1]
    copies = place(ids, s_ref, t_ref, w_ref, sem)
    total = jnp.zeros((PR + AR, width), F32)
    for k in range(NX):
        for copy in copies[k]:
            copy.wait()
        total += nn(a_ref[:, block_columns(ids, k)], w_ref[k].reshape(BLK, width))
    out_ref[...] = total.astype(BF)


def project(ids, scaled, pieces, pieces_sib):
    width = pieces.shape[-1]
    rows = scaled.shape[0]
    return pl.pallas_call(
        project_kernel,
        out_shape=jax.ShapeDtypeStruct((rows, width), BF),
        in_specs=[SM, VM, HBM, HBM],
        out_specs=VM,
        scratch_shapes=[pltpu.VMEM((NX, NZ, NC, WR, width), BF), pltpu.SemaphoreType.DMA((NZ, 2))],
        compiler_params=params(16),
        cost_estimate=cheap(),
        name="project",
    )(ids, scaled, pieces, pieces_sib)


def stacked(value):
    return jnp.concatenate([value[:, h * HD : (h + 1) * HD] for h in range(HEADS)], axis=0)


def attention_kernel(
    ids, owners, lengths, q_ref, kv_ref, gp_ref, ga_ref, s_ref, t_ref, after_ref,
    gq_ref, gkv_ref, own_ref, sib_ref, pairs, dense, sem,
):
    del after_ref
    x, z, c = ids[0], ids[1], ids[2]
    own_prompt = x * 4 + z // 2
    prompts = [owners[s] for s in range(SLOTS)] + [own_prompt]
    copies = []
    for b, p in enumerate(prompts):
        k = lax.rem(x - p // 4 + NX, NX)
        for half in range(2):
            for rel in range(2):
                at = pl.multiple_of((half * 2 + lax.rem(c + rel, 2)) * PR, PR)
                src = (s_ref, t_ref)[rel].at[k, lax.rem(p, 4) * 2 + half]
                copies.append(pltpu.make_async_copy(src, pairs.at[b, pl.ds(at, PR)], sem.at[b, half, rel]))
                copies[-1].start()
    dense[...] = jnp.zeros_like(dense)
    row_step = lax.rem(lax.broadcasted_iota(jnp.int32, (HEADS * SR, SR), 0), SR)
    col_step = lax.broadcasted_iota(jnp.int32, (HEADS * SR, SR), 1)
    live_step = lax.broadcasted_iota(jnp.int32, (SR, QC), 0)
    per_block = 4
    for b in range(SLOTS + 1):
        for copy in copies[b * per_block : (b + 1) * per_block]:
            copy.wait()
        keys, values = pairs[b, :, :HD], pairs[b, :, HD:]
        if b < SLOTS:
            lo = PR + b * SR
            length = lengths[b]
            upstream = ga_ref[b * SR : (b + 1) * SR, :]
            upstream = jnp.where(live_step < length, upstream.astype(F32), 0.0).astype(BF)
        else:
            lo = 0
            upstream = gp_ref[...]
        q4 = stacked(q_ref[lo : lo + SR, :])
        g4 = stacked(upstream)
        s1 = SCALE * nt(q4, keys)
        gp1 = nt(g4, values)
        if b < SLOTS:
            k_own = kv_ref[lo : lo + SR, :HD]
            v_own = kv_ref[lo : lo + SR, HD:]
            s2 = SCALE * nt(q4, k_own)
            gp2 = nt(g4, v_own)
            seen = (row_step >= col_step) & (col_step < length)
            s2 = jnp.where(seen, s2, -jnp.inf)
            top = jnp.maximum(jnp.max(s1, axis=1, keepdims=True), jnp.max(s2, axis=1, keepdims=True))
            e1 = jnp.exp(s1 - top)
            e2 = jnp.exp(s2 - top)
            norm = 1.0 / (jnp.sum(e1, axis=1, keepdims=True) + jnp.sum(e2, axis=1, keepdims=True))
            p1 = e1 * norm
            p2 = e2 * norm
            delta = jnp.sum(p1 * gp1, axis=1, keepdims=True) + jnp.sum(p2 * gp2, axis=1, keepdims=True)
            d2 = (p2 * (gp2 - delta)).astype(BF)
        else:
            offset = (lax.rem(z, 2) * 2 + c) * PR
            rows = lax.rem(lax.broadcasted_iota(jnp.int32, (HEADS * SR, PLEN), 0), SR) + offset
            cols = lax.broadcasted_iota(jnp.int32, (HEADS * SR, PLEN), 1)
            s1 = jnp.where(rows >= cols, s1, -jnp.inf)
            top = jnp.max(s1, axis=1, keepdims=True)
            e1 = jnp.exp(s1 - top)
            p1 = e1 * (1.0 / jnp.sum(e1, axis=1, keepdims=True))
            delta = jnp.sum(p1 * gp1, axis=1, keepdims=True)
        d1 = (p1 * (gp1 - delta)).astype(BF)
        gq = nn(d1, keys)
        if b < SLOTS:
            gq += nn(d2, k_own)
            gkv_ref[b * SR : (b + 1) * SR, :HD] = (SCALE * tn(d2, q4)).astype(BF)
            gkv_ref[b * SR : (b + 1) * SR, HD:] = tn(p2.astype(BF), g4).astype(BF)
        gq = (SCALE * gq).astype(BF)
        for h in range(HEADS):
            gq_ref[lo : lo + SR, h * HD : (h + 1) * HD] = gq[h * SR : (h + 1) * SR, :]
        p = prompts[b]
        dense[p, :, :, :HD] += (SCALE * tn(d1, q4)).reshape(4, PR, HD)
        dense[p, :, :, HD:] += tn(p1.astype(BF), g4).reshape(4, PR, HD)
    for half in range(2):
        own_ref[:, half] = dense[:, half * 2 + c].astype(BF)
        sib_ref[:, half] = dense[:, half * 2 + 1 - c].astype(BF)


def attention(ids, owners, lengths, q, kv, gp, ga, pairs, pairs_sib, after):
    return pl.pallas_call(
        attention_kernel,
        out_shape=[
            jax.ShapeDtypeStruct((PR + AR, QC), BF),
            jax.ShapeDtypeStruct((AR, 2 * HD), BF),
            jax.ShapeDtypeStruct((PROMPTS, 2, PR, 2 * HD), BF),
            jax.ShapeDtypeStruct((PROMPTS, 2, PR, 2 * HD), BF),
        ],
        in_specs=[SM] * 3 + [VM] * 4 + [ANY] * 3,
        out_specs=[VM] * 4,
        scratch_shapes=[
            pltpu.VMEM((SLOTS + 1, PLEN, 2 * HD), BF),
            pltpu.VMEM((PROMPTS, 4, PR, 2 * HD), F32),
            pltpu.SemaphoreType.DMA((SLOTS + 1, 2, 2)),
        ],
        compiler_params=params(16),
        cost_estimate=cheap(),
        name="attention",
    )(ids, owners, lengths, q, kv, gp, ga, pairs, pairs_sib, after)


def row_coefficient(gq, gkv, q, kv, inv):
    row_dot = jnp.sum(gq.astype(F32) * q.astype(F32), axis=1, keepdims=True)
    row_dot += jnp.sum(gkv.astype(F32) * kv.astype(F32), axis=1, keepdims=True)
    return inv * inv * row_dot * (1.0 / D)


def answer_grads_kernel(
    ids, gq_ref, gkv_ref, q_ref, kv_ref, inv_ref, gain_ref, x_ref, qs_ref, qt_ref, ks_ref, kt_ref,
    out_ref, share_ref, wq, wkv, states, result, sem_q, sem_kv, sem_x, sem_out,
):
    q_copies = place(ids, qs_ref, qt_ref, wq, sem_q)
    kv_copies = place(ids, ks_ref, kt_ref, wkv, sem_kv)
    x_copy = pltpu.make_async_copy(x_ref, states, sem_x)
    x_copy.start()
    gq, gkv = gq_ref[...], gkv_ref[...]
    inv = inv_ref[PR:, :]
    coefficient = row_coefficient(gq_ref[PR:, :], gkv, q_ref[PR:, :], kv_ref[PR:, :], inv)
    out_copies = []
    for k in range(NX):
        for copy in q_copies[k] + kv_copies[k]:
            copy.wait()
        cols = block_columns(ids, k)
        by_query = nt(gq, wq[k].reshape(BLK, QC))
        share_ref[:, cols] = by_query[:PR]
        hidden = by_query[PR:] + nt(gkv, wkv[k].reshape(BLK, 2 * HD))
        if k == 0:
            x_copy.wait()
        moved = inv * gain_ref[:, cols].astype(F32) * hidden - states[:, cols].astype(F32) * coefficient
        result[k] = moved.astype(BF)
        out_copies.append(pltpu.make_async_copy(result.at[k], out_ref.at[:, cols], sem_out.at[k]))
        out_copies[-1].start()
    for copy in out_copies:
        copy.wait()


def answer_grads(ids, gq, gkv, q, kv, inv, gain, states, pieces):
    return pl.pallas_call(
        answer_grads_kernel,
        out_shape=[jax.ShapeDtypeStruct((AR, D), BF), jax.ShapeDtypeStruct((PR, D), F32)],
        in_specs=[SM] + [VM] * 6 + [HBM] * 5,
        out_specs=[HBM, VM],
        scratch_shapes=[
            pltpu.VMEM((NX, NZ, NC, WR, QC), BF),
            pltpu.VMEM((NX, NZ, NC, WR, 2 * HD), BF),
            pltpu.VMEM((AR, D), BF),
            pltpu.VMEM((NX, AR, BLK), BF),
            pltpu.SemaphoreType.DMA((NZ, 2)),
            pltpu.SemaphoreType.DMA((NZ, 2)),
            pltpu.SemaphoreType.DMA,
            pltpu.SemaphoreType.DMA((NX,)),
        ],
        compiler_params=params(24),
        cost_estimate=cheap(),
        name="answer_grads",
    )(ids, gq, gkv, q, kv, inv, gain, states, *pieces)


def prompt_grads_kernel(
    ids, gq_ref, gkv_ref, q_ref, kv_ref, inv_ref, gain_ref, x_ref, share_ref, ks_ref, kt_ref, out_ref, wkv, sem
):
    copies = place(ids, ks_ref, kt_ref, wkv, sem)
    gkv = gkv_ref[...]
    inv = inv_ref[:PR, :]
    coefficient = row_coefficient(gq_ref[:PR, :], gkv, q_ref[:PR, :], kv_ref[:PR, :], inv)
    for k in range(NX):
        for copy in copies[k]:
            copy.wait()
        cols = block_columns(ids, k)
        hidden = share_ref[:, cols] + nt(gkv, wkv[k].reshape(BLK, 2 * HD))
        moved = inv * gain_ref[:, cols].astype(F32) * hidden - x_ref[:, cols].astype(F32) * coefficient
        out_ref[:, cols] = moved.astype(BF)


def prompt_grads(ids, gq, gkv, q, kv, inv, gain, states, share, pieces):
    return pl.pallas_call(
        prompt_grads_kernel,
        out_shape=jax.ShapeDtypeStruct((PR, D), BF),
        in_specs=[SM] + [VM] * 8 + [HBM] * 2,
        out_specs=VM,
        scratch_shapes=[pltpu.VMEM((NX, NZ, NC, WR, 2 * HD), BF), pltpu.SemaphoreType.DMA((NZ, 2))],
        compiler_params=params(12),
        cost_estimate=cheap(),
        name="prompt_grads",
    )(ids, gq, gkv, q, kv, inv, gain, states, share, *pieces)


def weight_grads_kernel(ids, own_ref, sib_ref, g_ref, gs_ref, *refs):
    plus_ref, minus_ref, u_ref, l_ref, mine_ref = refs[-5:]
    x = ids[0]
    width = g_ref.shape[1]
    g, gs = g_ref[...], gs_ref[...]

    def product(k, lo, count):
        at = pl.ds(lax.rem(x + k, NX) * NZ + lo, count)
        rows = count * WR
        total = nn(own_ref[at].reshape(rows, PR + AR), g) + nn(sib_ref[at].reshape(rows, PR + AR), gs)
        return total.astype(BF).reshape(count, WR, width)

    half = NZ // 2
    plus_ref[0] = product(2, 0, half)
    minus_ref[0] = product(2, half, half)
    plus_ref[1] = product(1, half, half)
    minus_ref[1] = product(3, 0, half)
    u_ref[...] = product(1, 0, half)
    l_ref[...] = product(3, half, half)
    mine_ref[...] = product(0, 0, NZ)


def weight_grads(ids, own, sib, grads, grads_sib, after):
    width = grads.shape[1]
    half = NZ // 2

    def shape(*dims):
        return jax.ShapeDtypeStruct((*dims, WR, width), BF)

    return pl.pallas_call(
        weight_grads_kernel,
        out_shape=[shape(2, half), shape(2, half), shape(half), shape(half), shape(NZ)],
        in_specs=[SM] + [VM] * 4 + [ANY] * len(after),
        out_specs=[VM] * 5,
        compiler_params=params(16),
        cost_estimate=cheap(),
        name="weight_grads",
    )(ids, own, sib, grads, grads_sib, *after)


def add_up(value):
    return jnp.sum(value.astype(F32), axis=0)


def join(upper, lower, plus, minus, mine, after):
    half = NZ // 2

    def kernel(upper_ref, lower_ref, plus_ref, minus_ref, mine_ref, *refs):
        out_ref = refs[-1]
        first = mine_ref[:half].astype(F32) + minus_ref[1].astype(F32) + upper_ref[...].astype(F32)
        second = mine_ref[half:].astype(F32) + plus_ref[1].astype(F32) + lower_ref[...].astype(F32)
        out_ref[:half] = first.astype(BF)
        out_ref[half:] = second.astype(BF)

    return pl.pallas_call(
        kernel,
        out_shape=jax.ShapeDtypeStruct(mine.shape, BF),
        in_specs=[VM] * 5 + [ANY] * len(after),
        out_specs=VM,
        compiler_params=params(10),
        cost_estimate=cheap(),
        name="join",
    )(upper, lower, plus, minus, mine, *after)


def first_hop(plus, minus):
    return shift(plus, "x", 1), shift(minus, "x", -1)


def second_hop(plus, minus, upper, lower, after):
    return shift(add_after(upper, plus, after), "x", 1), shift(add_after(lower, minus, after), "x", -1)


def per_device(
    prompt_states,
    answer_states,
    prompt_cotangent,
    answer_cotangent,
    norm_gain,
    weights,
    answer_length,
    answer_owner,
):
    x, z, c = lax.axis_index("x"), lax.axis_index("z"), lax.axis_index("c")
    ids = jnp.stack([x, z, c]).astype(jnp.int32)
    lengths, owners = answer_length[0], answer_owner[0]
    shard = weights[0]
    gain = norm_gain[0].astype(F32)

    kv_all = spread(shard[:, QC:], "z")
    q_line = direct_x(shard[:, :QC])
    scaled, inverse = norm(prompt_states[0], answer_states[0], norm_gain)
    scaled_t = scaled.T.reshape(NX * NZ, NC, WR, PR + AR)
    own_t = lax.dynamic_index_in_dim(scaled_t, c, 1, keepdims=False)
    other_t = lax.dynamic_index_in_dim(scaled_t, 1 - c, 1, keepdims=False)
    sib_t = shift(other_t, "c", 1)
    kv_pieces, kv_near = ring_x(held(kv_all, (inverse, q_line)))
    kv_sib = shift(kv_pieces, "c", 1)
    kv = project(ids, scaled, kv_pieces, kv_sib)
    pair_line = spread(kv[:PR], "z")
    pair_hops = [shift(pair_line, "x", k) for k in range(NX)]
    gates = (kv_near, (kv,), (pair_line, own_t, other_t), tuple(pair_hops[1:]))
    q_pieces = ring_z(q_line, gates)
    q_sib = shift(q_pieces, "c", 1)
    q = project(ids, scaled, q_pieces, q_sib)
    pairs = stack_after(pair_hops, kv)
    pairs_sib = shift(pairs, "c", 1)

    gq, gkv_answer, own, sib = attention(
        ids, owners, lengths, q, kv, prompt_cotangent[0], answer_cotangent[0], pairs, pairs_sib, sib_t
    )
    gq_sib = shift(gq, "c", 1)
    answer_back, share = answer_grads(
        ids, gq, gkv_answer, q, kv, inverse, norm_gain, answer_states[0], (q_pieces, q_sib, kv_pieces, kv_sib)
    )
    answer_out = shift(answer_back, "section", -1)
    query_parts = weight_grads(ids, own_t, sib_t, gq, gq_sib, (answer_back,))
    query_hop = first_hop(*query_parts[:2])

    terms = (own.astype(F32) + shift(sib, "c", 1).astype(F32)).astype(BF).reshape(NX * NZ, PR, 2 * HD)
    gkv_prompt = add_up(exchange(terms, ("x", "z"))).astype(BF)
    gkv = jnp.concatenate([gkv_prompt, gkv_answer], axis=0)
    gkv_sib = shift(gkv, "c", 1)
    pair_parts = weight_grads(ids, own_t, sib_t, gkv, gkv_sib, query_hop)
    pair_hop = first_hop(*pair_parts[:2])
    query_second = second_hop(*query_hop, *query_parts[2:4], (pair_parts[0],))
    prompt_back = prompt_grads(
        ids, gq, gkv_prompt, q, kv, inverse, norm_gain, prompt_states[0], share, (kv_pieces, kv_sib)
    )
    prompt_out = forward(shift(prompt_back, "section", -1))
    pair_second = second_hop(*pair_hop, *pair_parts[2:4], (prompt_back,))
    query_last = exchange(join(*query_second, *query_hop, query_parts[4], pair_hop), "z")
    pair_last = exchange(join(*pair_second, *pair_hop, pair_parts[4], (answer_out, query_last)), "z")
    query_total, pair_total = add_up(query_last), add_up(pair_last)

    weight_total = jnp.concatenate([query_total, pair_total], axis=1)
    own_gain = lax.dynamic_slice(gain, (((x * NZ + z) * NC + c) * WR,), (WR,))
    gain_total = jnp.sum(weight_total * shard.astype(F32), axis=1) / own_gain
    return (prompt_out[None], forward(answer_out)[None], weight_total[None], gain_total[None])


def solution(mesh):
    fine = Mesh(mesh.devices.reshape(mesh.devices.shape[0], NX, NZ, NC), ("section", "x", "z", "c"))
    dp = ("x", "z", "c")
    placed = (
        P("section", dp, None),
        P("section", dp, None),
        P("section", dp, None),
        P("section", dp, None),
        P("section", None),
        P("section", dp, None),
        P("section", dp),
        P("section", dp),
    )
    return jax.shard_map(
        per_device,
        mesh=fine,
        in_specs=placed,
        out_specs=(
            P("section", dp, None),
            P("section", dp, None),
            P("section", dp, None),
            P("section", dp),
        ),
        check_vma=False,
    )
```

```python
import functools

import jax
import jax.numpy as jnp
from jax import lax
from jax.experimental import pallas as pl
from jax.experimental.pallas import tpu as pltpu
from jax.sharding import Mesh, PartitionSpec as P

HD = 128
HEADS = 4
QC = HEADS * HD
D = 5120
PR = 64
AR = 256
SLOTS = 4
SR = 64
NX, NZ, NC = 4, 8, 2
WR = 80
BLK = D // NX
PROMPTS = 16
PLEN = 256
EPSILON = 1e-06
SCALE = HD**-0.5
BF = jnp.bfloat16
F32 = jnp.float32
MIB = 1024 * 1024


def shift(value, axis, steps):
    count = lax.axis_size(axis)
    if steps % count == 0:
        return value
    return lax.ppermute(value, axis, [(s, (s + steps) % count) for s in range(count)])


def params(mib):
    return pltpu.CompilerParams(vmem_limit_bytes=mib * MIB)


def cheap():
    return pl.CostEstimate(flops=10**6, bytes_accessed=10**5, transcendentals=0)


ANY = pl.BlockSpec(memory_space=pl.ANY)
HBM = pl.BlockSpec(memory_space=pltpu.HBM)
VM = pl.BlockSpec(memory_space=pltpu.VMEM)
SM = pl.BlockSpec(memory_space=pltpu.SMEM)


def nt(a, b):
    return lax.dot_general(a, b, (((1,), (1,)), ((), ())), preferred_element_type=F32)


def tn(a, b):
    return lax.dot_general(a, b, (((0,), (0,)), ((), ())), preferred_element_type=F32)


def nn(a, b):
    return jnp.dot(a, b, preferred_element_type=F32)


def exchange(value, axis):
    return lax.all_to_all(value, axis, 0, 0, tiled=True)


def spread(value, axis):
    count = lax.axis_size(axis)
    return exchange(jnp.broadcast_to(value[None], (count, *value.shape)), axis)


def held(value, after):
    def kernel(*refs):
        del refs

    return pl.pallas_call(
        kernel,
        out_shape=jax.ShapeDtypeStruct(value.shape, value.dtype),
        in_specs=[ANY] * (1 + len(after)),
        out_specs=ANY,
        input_output_aliases={0: 0},
        compiler_params=params(4),
        cost_estimate=cheap(),
        name="held",
    )(value, *after)


def sum_after(left, right, after):
    def kernel(left_ref, right_ref, *refs):
        out_ref = refs[-1]
        out_ref[...] = (left_ref[...].astype(F32) + right_ref[...].astype(F32)).astype(BF)

    return pl.pallas_call(
        kernel,
        out_shape=jax.ShapeDtypeStruct(left.shape, BF),
        in_specs=[VM, VM] + [ANY] * len(after),
        out_specs=VM,
        compiler_params=params(10),
        cost_estimate=cheap(),
        name="sum",
    )(left, right, *after)


def add_after(left, right, after):
    def kernel(left_ref, right_ref, *refs):
        out_ref = refs[-1]
        out_ref[...] = (left_ref[...].astype(F32) + right_ref[0].astype(F32)).astype(BF)

    return pl.pallas_call(
        kernel,
        out_shape=jax.ShapeDtypeStruct(left.shape, BF),
        in_specs=[VM, VM] + [ANY] * len(after),
        out_specs=VM,
        compiler_params=params(6),
        cost_estimate=cheap(),
        name="add",
    )(left, right, *after)


def forward(value):
    rows, width = value.shape
    spec = pl.BlockSpec((32, width), lambda i: (i, 0))

    def kernel(value_ref, out_ref):
        out_ref[...] = value_ref[...]

    return pl.pallas_call(
        kernel,
        out_shape=jax.ShapeDtypeStruct(value.shape, value.dtype),
        grid=(rows // 32,),
        in_specs=[spec],
        out_specs=spec,
        compiler_params=params(4),
        cost_estimate=cheap(),
        name="forward",
    )(value)


def stack_after(pieces, after):
    flat = [part for piece in pieces for part in (piece if isinstance(piece, tuple) else (piece,))]
    shape = pieces[0].shape

    def kernel(*refs):
        out_ref = refs[-1]
        at = 0
        for i, piece in enumerate(pieces):
            if isinstance(piece, tuple):
                cut = shape[0] // 2
                out_ref[i, :cut] = refs[at][...]
                out_ref[i, cut:] = refs[at + 1][...]
                at += 2
            else:
                out_ref[i] = refs[at][...]
                at += 1

    return pl.pallas_call(
        kernel,
        out_shape=jax.ShapeDtypeStruct((len(pieces), *shape), flat[0].dtype),
        in_specs=[VM] * len(flat) + [ANY] * len(after),
        out_specs=VM,
        compiler_params=params(10),
        cost_estimate=cheap(),
        name="stack",
    )(*flat, *after)


def direct_x(value):
    return jnp.stack([shift(value, "x", k) for k in range(NX)])


def both_ways(up, down, axis):
    return shift(up, axis, 1), shift(down, axis, -1)


def norm_kernel(p_ref, a_ref, gain_ref, scaled_ref, inv_ref):
    gain = gain_ref[...].astype(F32)
    for ref, lo, rows in ((p_ref, 0, PR), (a_ref, PR, AR)):
        for r in range(0, rows, 32):
            wide = ref[r : r + 32, :].astype(F32)
            inv = lax.rsqrt(jnp.mean(wide * wide, axis=-1, keepdims=True) + EPSILON)
            scaled_ref[lo + r : lo + r + 32, :] = (wide * inv * gain).astype(BF)
            inv_ref[lo + r : lo + r + 32, :] = inv


def norm(prompt, answer, gain):
    rows = PR + AR
    return pl.pallas_call(
        norm_kernel,
        out_shape=[jax.ShapeDtypeStruct((rows, D), BF), jax.ShapeDtypeStruct((rows, 1), F32)],
        in_specs=[VM] * 3,
        out_specs=[VM] * 2,
        compiler_params=params(16),
        cost_estimate=cheap(),
        name="norm",
    )(prompt, answer, gain)


def place(ids, s_ref, t_ref, w_ref, sem):
    if s_ref.shape[0] == NX:
        copies = []
        for k in range(NX):
            for rel in range(2):
                dst = w_ref.at[k, :, lax.rem(ids[2] + rel, 2)]
                copies.append(pltpu.make_async_copy((s_ref, t_ref)[rel].at[k], dst, sem.at[k, 0, rel]))
                copies[-1].start()
        return [copies[2 * k : 2 * k + 2] for k in range(NX)]
    blocks = []
    for k in range(NX):
        copies = []
        for j in range(NZ):
            for rel in range(2):
                dst = w_ref.at[k, lax.rem(ids[1] - j + NZ, NZ), lax.rem(ids[2] + rel, 2)]
                copies.append(pltpu.make_async_copy((s_ref, t_ref)[rel].at[j, k], dst, sem.at[k, j, rel]))
                copies[-1].start()
        blocks.append(copies)
    return blocks


def block_columns(ids, k):
    return pl.ds(pl.multiple_of(lax.rem(ids[0] - k + NX, NX) * BLK, BLK), BLK)


def project_kernel(ids, a_ref, s_ref, t_ref, out_ref, w_ref, sem):
    width = w_ref.shape[-1]
    copies = place(ids, s_ref, t_ref, w_ref, sem)
    total = jnp.zeros((PR + AR, width), F32)
    for k in range(NX):
        for copy in copies[k]:
            copy.wait()
        total += nn(a_ref[:, block_columns(ids, k)], w_ref[k].reshape(BLK, width))
    out_ref[...] = total.astype(BF)


def project(ids, scaled, pieces, pieces_sib):
    width = pieces.shape[-1]
    rows = scaled.shape[0]
    return pl.pallas_call(
        project_kernel,
        out_shape=jax.ShapeDtypeStruct((rows, width), BF),
        in_specs=[SM, VM, HBM, HBM],
        out_specs=VM,
        scratch_shapes=[pltpu.VMEM((NX, NZ, NC, WR, width), BF), pltpu.SemaphoreType.DMA((NX, NZ, 2))],
        compiler_params=params(16),
        cost_estimate=cheap(),
        name="project",
    )(ids, scaled, pieces, pieces_sib)


def stacked(value):
    return jnp.concatenate([value[:, h * HD : (h + 1) * HD] for h in range(HEADS)], axis=0)


def attention_kernel(
    ids, owners, lengths, q_ref, kv_ref, gp_ref, ga_ref, s_ref, t_ref, after_ref,
    gq_ref, gkv_ref, own_ref, sib_ref, pairs, dense, sem,
):
    del after_ref
    x, z, c = ids[0], ids[1], ids[2]
    own_prompt = x * 4 + z // 2
    prompts = [owners[s] for s in range(SLOTS)] + [own_prompt]
    copies = []
    for b, p in enumerate(prompts):
        k = lax.rem(x - p // 4 + NX, NX)
        for half in range(2):
            for rel in range(2):
                at = pl.multiple_of((half * 2 + lax.rem(c + rel, 2)) * PR, PR)
                src = (s_ref, t_ref)[rel].at[k, lax.rem(p, 4) * 2 + half]
                copies.append(pltpu.make_async_copy(src, pairs.at[b, pl.ds(at, PR)], sem.at[b, half, rel]))
                copies[-1].start()
    dense[...] = jnp.zeros_like(dense)
    row_step = lax.rem(lax.broadcasted_iota(jnp.int32, (HEADS * SR, SR), 0), SR)
    col_step = lax.broadcasted_iota(jnp.int32, (HEADS * SR, SR), 1)
    live_step = lax.broadcasted_iota(jnp.int32, (SR, QC), 0)
    per_block = 4
    for b in range(SLOTS + 1):
        for copy in copies[b * per_block : (b + 1) * per_block]:
            copy.wait()
        keys, values = pairs[b, :, :HD], pairs[b, :, HD:]
        if b < SLOTS:
            lo = PR + b * SR
            length = lengths[b]
            upstream = ga_ref[b * SR : (b + 1) * SR, :]
            upstream = jnp.where(live_step < length, upstream.astype(F32), 0.0).astype(BF)
        else:
            lo = 0
            upstream = gp_ref[...]
        q4 = stacked(q_ref[lo : lo + SR, :])
        g4 = stacked(upstream)
        s1 = SCALE * nt(q4, keys)
        gp1 = nt(g4, values)
        if b < SLOTS:
            k_own = kv_ref[lo : lo + SR, :HD]
            v_own = kv_ref[lo : lo + SR, HD:]
            s2 = SCALE * nt(q4, k_own)
            gp2 = nt(g4, v_own)
            seen = (row_step >= col_step) & (col_step < length)
            s2 = jnp.where(seen, s2, -jnp.inf)
            top = jnp.maximum(jnp.max(s1, axis=1, keepdims=True), jnp.max(s2, axis=1, keepdims=True))
            e1 = jnp.exp(s1 - top)
            e2 = jnp.exp(s2 - top)
            norm = 1.0 / (jnp.sum(e1, axis=1, keepdims=True) + jnp.sum(e2, axis=1, keepdims=True))
            p1 = e1 * norm
            p2 = e2 * norm
            delta = jnp.sum(p1 * gp1, axis=1, keepdims=True) + jnp.sum(p2 * gp2, axis=1, keepdims=True)
            d2 = (p2 * (gp2 - delta)).astype(BF)
        else:
            offset = (lax.rem(z, 2) * 2 + c) * PR
            rows = lax.rem(lax.broadcasted_iota(jnp.int32, (HEADS * SR, PLEN), 0), SR) + offset
            cols = lax.broadcasted_iota(jnp.int32, (HEADS * SR, PLEN), 1)
            s1 = jnp.where(rows >= cols, s1, -jnp.inf)
            top = jnp.max(s1, axis=1, keepdims=True)
            e1 = jnp.exp(s1 - top)
            p1 = e1 * (1.0 / jnp.sum(e1, axis=1, keepdims=True))
            delta = jnp.sum(p1 * gp1, axis=1, keepdims=True)
        d1 = (p1 * (gp1 - delta)).astype(BF)
        gq = nn(d1, keys)
        if b < SLOTS:
            gq += nn(d2, k_own)
            gkv_ref[b * SR : (b + 1) * SR, :HD] = (SCALE * tn(d2, q4)).astype(BF)
            gkv_ref[b * SR : (b + 1) * SR, HD:] = tn(p2.astype(BF), g4).astype(BF)
        gq = (SCALE * gq).astype(BF)
        for h in range(HEADS):
            gq_ref[lo : lo + SR, h * HD : (h + 1) * HD] = gq[h * SR : (h + 1) * SR, :]
        p = prompts[b]
        dense[p, :, :, :HD] += (SCALE * tn(d1, q4)).reshape(4, PR, HD)
        dense[p, :, :, HD:] += tn(p1.astype(BF), g4).reshape(4, PR, HD)
    for half in range(2):
        own_ref[:, half] = dense[:, half * 2 + c].astype(BF)
        sib_ref[:, half] = dense[:, half * 2 + 1 - c].astype(BF)


def attention(ids, owners, lengths, q, kv, gp, ga, pairs, pairs_sib, after):
    return pl.pallas_call(
        attention_kernel,
        out_shape=[
            jax.ShapeDtypeStruct((PR + AR, QC), BF),
            jax.ShapeDtypeStruct((AR, 2 * HD), BF),
            jax.ShapeDtypeStruct((PROMPTS, 2, PR, 2 * HD), BF),
            jax.ShapeDtypeStruct((PROMPTS, 2, PR, 2 * HD), BF),
        ],
        in_specs=[SM] * 3 + [VM] * 4 + [ANY] * 3,
        out_specs=[VM] * 4,
        scratch_shapes=[
            pltpu.VMEM((SLOTS + 1, PLEN, 2 * HD), BF),
            pltpu.VMEM((PROMPTS, 4, PR, 2 * HD), F32),
            pltpu.SemaphoreType.DMA((SLOTS + 1, 2, 2)),
        ],
        compiler_params=params(16),
        cost_estimate=cheap(),
        name="attention",
    )(ids, owners, lengths, q, kv, gp, ga, pairs, pairs_sib, after)


def row_coefficient(gq, gkv, q, kv, inv):
    row_dot = jnp.sum(gq.astype(F32) * q.astype(F32), axis=1, keepdims=True)
    row_dot += jnp.sum(gkv.astype(F32) * kv.astype(F32), axis=1, keepdims=True)
    return inv * inv * row_dot * (1.0 / D)


def answer_grads_kernel(
    ids, gq_ref, gkv_ref, q_ref, kv_ref, inv_ref, gain_ref, x_ref, qs_ref, qt_ref, ks_ref, kt_ref,
    out_ref, share_ref, token_ref, wq, wkv, states, result, sem_q, sem_kv, sem_x, sem_out,
):
    q_copies = place(ids, qs_ref, qt_ref, wq, sem_q)
    kv_copies = place(ids, ks_ref, kt_ref, wkv, sem_kv)
    x_copy = pltpu.make_async_copy(x_ref, states, sem_x)
    x_copy.start()
    gq, gkv = gq_ref[...], gkv_ref[...]
    inv = inv_ref[PR:, :]
    coefficient = row_coefficient(gq_ref[PR:, :], gkv, q_ref[PR:, :], kv_ref[PR:, :], inv)
    out_copies = []
    for k in range(NX):
        for copy in q_copies[k] + kv_copies[k]:
            copy.wait()
        cols = block_columns(ids, k)
        by_query = nt(gq, wq[k].reshape(BLK, QC))
        share_ref[:, cols] = by_query[:PR]
        hidden = by_query[PR:] + nt(gkv, wkv[k].reshape(BLK, 2 * HD))
        if k == 0:
            x_copy.wait()
        moved = inv * gain_ref[:, cols].astype(F32) * hidden - states[:, cols].astype(F32) * coefficient
        result[k] = moved.astype(BF)
        out_copies.append(pltpu.make_async_copy(result.at[k], out_ref.at[:, cols], sem_out.at[k]))
        out_copies[-1].start()
    for copy in out_copies:
        copy.wait()
    token_ref[...] = jnp.zeros_like(token_ref)


def answer_grads(ids, gq, gkv, q, kv, inv, gain, states, pieces):
    return pl.pallas_call(
        answer_grads_kernel,
        out_shape=[
            jax.ShapeDtypeStruct((AR, D), BF),
            jax.ShapeDtypeStruct((PR, D), F32),
            jax.ShapeDtypeStruct((8, 128), F32),
        ],
        in_specs=[SM] + [VM] * 6 + [HBM] * 5,
        out_specs=[HBM, VM, VM],
        scratch_shapes=[
            pltpu.VMEM((NX, NZ, NC, WR, QC), BF),
            pltpu.VMEM((NX, NZ, NC, WR, 2 * HD), BF),
            pltpu.VMEM((AR, D), BF),
            pltpu.VMEM((NX, AR, BLK), BF),
            pltpu.SemaphoreType.DMA((NX, NZ, 2)),
            pltpu.SemaphoreType.DMA((NX, NZ, 2)),
            pltpu.SemaphoreType.DMA,
            pltpu.SemaphoreType.DMA((NX,)),
        ],
        compiler_params=params(52),
        cost_estimate=cheap(),
        name="answer_grads",
    )(ids, gq, gkv, q, kv, inv, gain, states, *pieces)


def prompt_grads_kernel(
    ids, gq_ref, gkv_ref, q_ref, kv_ref, inv_ref, gain_ref, x_ref, share_ref, ks_ref, kt_ref, out_ref, wkv, sem
):
    copies = place(ids, ks_ref, kt_ref, wkv, sem)
    gkv = gkv_ref[...]
    inv = inv_ref[:PR, :]
    coefficient = row_coefficient(gq_ref[:PR, :], gkv, q_ref[:PR, :], kv_ref[:PR, :], inv)
    for k in range(NX):
        for copy in copies[k]:
            copy.wait()
        cols = block_columns(ids, k)
        hidden = share_ref[:, cols] + nt(gkv, wkv[k].reshape(BLK, 2 * HD))
        moved = inv * gain_ref[:, cols].astype(F32) * hidden - x_ref[:, cols].astype(F32) * coefficient
        out_ref[:, cols] = moved.astype(BF)


def prompt_grads(ids, gq, gkv, q, kv, inv, gain, states, share, pieces):
    return pl.pallas_call(
        prompt_grads_kernel,
        out_shape=jax.ShapeDtypeStruct((PR, D), BF),
        in_specs=[SM] + [VM] * 8 + [HBM] * 2,
        out_specs=VM,
        scratch_shapes=[pltpu.VMEM((NX, NZ, NC, WR, 2 * HD), BF), pltpu.SemaphoreType.DMA((NX, NZ, 2))],
        compiler_params=params(12),
        cost_estimate=cheap(),
        name="prompt_grads",
    )(ids, gq, gkv, q, kv, inv, gain, states, share, *pieces)


def weight_grads_kernel(ids, own_ref, sib_ref, g_ref, gs_ref, *refs):
    plus_ref, minus_ref, u_ref, l_ref, mine_ref = refs[-5:]
    x = ids[0]
    width = g_ref.shape[1]
    g, gs = g_ref[...], gs_ref[...]

    def product(k, lo, count):
        at = pl.ds(lax.rem(x + k, NX) * NZ + lo, count)
        rows = count * WR
        total = nn(own_ref[at].reshape(rows, PR + AR), g) + nn(sib_ref[at].reshape(rows, PR + AR), gs)
        return total.astype(BF).reshape(count, WR, width)

    half = NZ // 2
    plus_ref[0] = product(2, 0, half)
    minus_ref[0] = product(2, half, half)
    plus_ref[1] = product(1, half, half)
    minus_ref[1] = product(3, 0, half)
    u_ref[...] = product(1, 0, half)
    l_ref[...] = product(3, half, half)
    mine_ref[...] = product(0, 0, NZ)


def weight_grads(ids, own, sib, grads, grads_sib, after):
    width = grads.shape[1]
    half = NZ // 2

    def shape(*dims):
        return jax.ShapeDtypeStruct((*dims, WR, width), BF)

    return pl.pallas_call(
        weight_grads_kernel,
        out_shape=[shape(2, half), shape(2, half), shape(half), shape(half), shape(NZ)],
        in_specs=[SM] + [VM] * 4 + [ANY] * len(after),
        out_specs=[VM] * 5,
        compiler_params=params(16),
        cost_estimate=cheap(),
        name="weight_grads",
    )(ids, own, sib, grads, grads_sib, *after)


def add_up(value):
    return jnp.sum(value.astype(F32), axis=0)


def join(upper, lower, plus, minus, mine, after):
    half = NZ // 2

    def kernel(upper_ref, lower_ref, plus_ref, minus_ref, mine_ref, *refs):
        out_ref = refs[-1]
        first = mine_ref[:half].astype(F32) + minus_ref[1].astype(F32) + upper_ref[...].astype(F32)
        second = mine_ref[half:].astype(F32) + plus_ref[1].astype(F32) + lower_ref[...].astype(F32)
        out_ref[:half] = first.astype(BF)
        out_ref[half:] = second.astype(BF)

    return pl.pallas_call(
        kernel,
        out_shape=jax.ShapeDtypeStruct(mine.shape, BF),
        in_specs=[VM] * 5 + [ANY] * len(after),
        out_specs=VM,
        compiler_params=params(10),
        cost_estimate=cheap(),
        name="join",
    )(upper, lower, plus, minus, mine, *after)


def first_hop(plus, minus):
    return shift(plus, "x", 1), shift(minus, "x", -1)


def second_hop(plus, minus, upper, lower, after):
    return shift(add_after(upper, plus, after), "x", 1), shift(add_after(lower, minus, after), "x", -1)


def per_device(
    prompt_states,
    answer_states,
    prompt_cotangent,
    answer_cotangent,
    norm_gain,
    weights,
    answer_length,
    answer_owner,
):
    x, z, c = lax.axis_index("x"), lax.axis_index("z"), lax.axis_index("c")
    ids = jnp.stack([x, z, c]).astype(jnp.int32)
    lengths, owners = answer_length[0], answer_owner[0]
    shard = weights[0]
    gain = norm_gain[0].astype(F32)

    kv_all = spread(shard[:, QC:], "z")
    q_line = direct_x(shard[:, :QC])
    scaled, inverse = norm(prompt_states[0], answer_states[0], norm_gain)
    kv_line = held(kv_all, (inverse, q_line))
    kv_near = both_ways(kv_line, kv_line, "x")
    q_line = held(q_line, (kv_line,))
    q_one = both_ways(q_line, q_line, "z")
    kv_near = held(kv_near[0], q_one), held(kv_near[1], q_one)
    kv_far = both_ways(kv_near[0][: NZ // 2], kv_near[1][NZ // 2 :], "x")
    q_one = held(q_one[0], kv_near), held(q_one[1], kv_near)
    q_two = both_ways(*q_one, "z")
    kv_pieces = stack_after([kv_line, kv_near[0], kv_far, kv_near[1]], q_two)
    kv_sib = shift(kv_pieces, "c", 1)
    q_two = held(q_two[0], kv_far), held(q_two[1], kv_far)
    q_three = both_ways(*q_two, "z")
    kv = project(ids, scaled, kv_pieces, kv_sib)
    pair_line = spread(kv[:PR], "z")
    pair_hops = [shift(pair_line, "x", k) for k in range(NX)]
    scaled = held(scaled, (kv,))
    scaled_t = scaled.T.reshape(NX * NZ, NC, WR, PR + AR)
    own_t = lax.dynamic_index_in_dim(scaled_t, c, 1, keepdims=False)
    other_t = lax.dynamic_index_in_dim(scaled_t, 1 - c, 1, keepdims=False)
    sib_t = shift(other_t, "c", 1)
    q_three = held(q_three[0], (pair_line, own_t, other_t)), held(q_three[1], (pair_line, own_t, other_t))
    q_four = both_ways(q_three[0][: NX // 2], q_three[1][NX // 2 :], "z")
    q_pieces = stack_after(
        [q_line, q_one[0], q_two[0], q_three[0], q_four, q_three[1], q_two[1], q_one[1]], tuple(pair_hops[1:])
    )
    q_sib = shift(q_pieces, "c", 1)
    q = project(ids, scaled, q_pieces, q_sib)
    pairs = stack_after(pair_hops, (kv,))
    pairs_sib = shift(pairs, "c", 1)

    gq, gkv_answer, own, sib = attention(
        ids, owners, lengths, q, kv, prompt_cotangent[0], answer_cotangent[0], pairs, pairs_sib, sib_t
    )
    gq_sib = shift(gq, "c", 1)
    answer_back, share, token = answer_grads(
        ids, gq, gkv_answer, q, kv, inverse, norm_gain, answer_states[0], (q_pieces, q_sib, kv_pieces, kv_sib)
    )
    answer_out = shift(answer_back, "section", -1)
    query_parts = weight_grads(ids, own_t, sib_t, gq, gq_sib, (token,))
    query_hop = first_hop(*query_parts[:2])

    terms = sum_after(own, shift(sib, "c", 1), (token,)).reshape(NX * NZ, PR, 2 * HD)
    gkv_prompt = add_up(exchange(terms, ("x", "z"))).astype(BF)
    gkv = jnp.concatenate([gkv_prompt, gkv_answer], axis=0)
    gkv_sib = shift(gkv, "c", 1)
    pair_parts = weight_grads(ids, own_t, sib_t, gkv, gkv_sib, query_hop)
    pair_hop = first_hop(*pair_parts[:2])
    query_second = second_hop(*query_hop, *query_parts[2:4], (pair_parts[0],))
    prompt_back = prompt_grads(
        ids, gq, gkv_prompt, q, kv, inverse, norm_gain, prompt_states[0], share, (kv_pieces, kv_sib)
    )
    prompt_out = forward(shift(prompt_back, "section", -1))
    pair_second = second_hop(*pair_hop, *pair_parts[2:4], (prompt_back,))
    query_last = exchange(join(*query_second, *query_hop, query_parts[4], pair_hop), "z")
    pair_last = exchange(join(*pair_second, *pair_hop, pair_parts[4], (answer_out, query_last)), "z")
    query_total, pair_total = add_up(query_last), add_up(pair_last)

    weight_total = jnp.concatenate([query_total, pair_total], axis=1)
    own_gain = lax.dynamic_slice(gain, (((x * NZ + z) * NC + c) * WR,), (WR,))
    gain_total = jnp.sum(weight_total * shard.astype(F32), axis=1) / own_gain
    return (prompt_out[None], forward(answer_out)[None], weight_total[None], gain_total[None])


def solution(mesh):
    fine = Mesh(mesh.devices.reshape(mesh.devices.shape[0], NX, NZ, NC), ("section", "x", "z", "c"))
    dp = ("x", "z", "c")
    placed = (
        P("section", dp, None),
        P("section", dp, None),
        P("section", dp, None),
        P("section", dp, None),
        P("section", None),
        P("section", dp, None),
        P("section", dp),
        P("section", dp),
    )
    return jax.shard_map(
        per_device,
        mesh=fine,
        in_specs=placed,
        out_specs=(
            P("section", dp, None),
            P("section", dp, None),
            P("section", dp, None),
            P("section", dp),
        ),
        check_vma=False,
    )
```

```python
import functools

import jax
import jax.numpy as jnp
from jax import lax
from jax.experimental import pallas as pl
from jax.experimental.pallas import tpu as pltpu
from jax.sharding import Mesh, PartitionSpec as P

HD = 128
HEADS = 4
QC = HEADS * HD
D = 5120
PR = 64
AR = 256
SLOTS = 4
SR = 64
NX, NZ, NC = 4, 8, 2
WR = 80
BLK = D // NX
PROMPTS = 16
PLEN = 256
EPSILON = 1e-06
SCALE = HD**-0.5
BF = jnp.bfloat16
F32 = jnp.float32
MIB = 1024 * 1024


def shift(value, axis, steps):
    count = lax.axis_size(axis)
    if steps % count == 0:
        return value
    return lax.ppermute(value, axis, [(s, (s + steps) % count) for s in range(count)])


def params(mib):
    return pltpu.CompilerParams(vmem_limit_bytes=mib * MIB)


def cheap():
    return pl.CostEstimate(flops=10**6, bytes_accessed=10**5, transcendentals=0)


ANY = pl.BlockSpec(memory_space=pl.ANY)
HBM = pl.BlockSpec(memory_space=pltpu.HBM)
VM = pl.BlockSpec(memory_space=pltpu.VMEM)
SM = pl.BlockSpec(memory_space=pltpu.SMEM)


def nt(a, b):
    return lax.dot_general(a, b, (((1,), (1,)), ((), ())), preferred_element_type=F32)


def tn(a, b):
    return lax.dot_general(a, b, (((0,), (0,)), ((), ())), preferred_element_type=F32)


def nn(a, b):
    return jnp.dot(a, b, preferred_element_type=F32)


def exchange(value, axis):
    return lax.all_to_all(value, axis, 0, 0, tiled=True)


def spread(value, axis):
    count = lax.axis_size(axis)
    return exchange(jnp.broadcast_to(value[None], (count, *value.shape)), axis)


def held(value, after):
    def kernel(*refs):
        del refs

    return pl.pallas_call(
        kernel,
        out_shape=jax.ShapeDtypeStruct(value.shape, value.dtype),
        in_specs=[ANY] * (1 + len(after)),
        out_specs=ANY,
        input_output_aliases={0: 0},
        compiler_params=params(4),
        cost_estimate=cheap(),
        name="held",
    )(value, *after)


def sum_after(left, right, after):
    def kernel(left_ref, right_ref, *refs):
        out_ref = refs[-1]
        out_ref[...] = (left_ref[...].astype(F32) + right_ref[...].astype(F32)).astype(BF)

    return pl.pallas_call(
        kernel,
        out_shape=jax.ShapeDtypeStruct(left.shape, BF),
        in_specs=[VM, VM] + [ANY] * len(after),
        out_specs=VM,
        compiler_params=params(10),
        cost_estimate=cheap(),
        name="sum",
    )(left, right, *after)


def add_after(left, right, after):
    def kernel(left_ref, right_ref, *refs):
        out_ref = refs[-1]
        out_ref[...] = (left_ref[...].astype(F32) + right_ref[0].astype(F32)).astype(BF)

    return pl.pallas_call(
        kernel,
        out_shape=jax.ShapeDtypeStruct(left.shape, BF),
        in_specs=[VM, VM] + [ANY] * len(after),
        out_specs=VM,
        compiler_params=params(6),
        cost_estimate=cheap(),
        name="add",
    )(left, right, *after)


def forward(value):
    rows, width = value.shape
    spec = pl.BlockSpec((32, width), lambda i: (i, 0))

    def kernel(value_ref, out_ref):
        out_ref[...] = value_ref[...]

    return pl.pallas_call(
        kernel,
        out_shape=jax.ShapeDtypeStruct(value.shape, value.dtype),
        grid=(rows // 32,),
        in_specs=[spec],
        out_specs=spec,
        compiler_params=params(4),
        cost_estimate=cheap(),
        name="forward",
    )(value)


def stack_after(pieces, after):
    flat = [part for piece in pieces for part in (piece if isinstance(piece, tuple) else (piece,))]
    shape = pieces[0].shape

    def kernel(*refs):
        out_ref = refs[-1]
        at = 0
        for i, piece in enumerate(pieces):
            if isinstance(piece, tuple):
                cut = shape[0] // 2
                out_ref[i, :cut] = refs[at][...]
                out_ref[i, cut:] = refs[at + 1][...]
                at += 2
            else:
                out_ref[i] = refs[at][...]
                at += 1

    return pl.pallas_call(
        kernel,
        out_shape=jax.ShapeDtypeStruct((len(pieces), *shape), flat[0].dtype),
        in_specs=[VM] * len(flat) + [ANY] * len(after),
        out_specs=VM,
        compiler_params=params(10),
        cost_estimate=cheap(),
        name="stack",
    )(*flat, *after)


def stack_z(ids, pieces, after):
    half = NZ // 2
    flat = [*pieces[:half], *pieces[half], *pieces[half + 1 :]]
    count, *rest = pieces[0].shape

    def kernel(ids, *refs):
        out_ref = refs[-1]

        def at(j):
            return lax.rem(ids[1] - j + NZ, NZ)

        for j in range(half):
            out_ref[:, at(j)] = refs[j][...]
        out_ref[: count // 2, at(half)] = refs[half][...]
        out_ref[count // 2 :, at(half)] = refs[half + 1][...]
        for j in range(half + 1, NZ):
            out_ref[:, at(j)] = refs[j + 1][...]

    return pl.pallas_call(
        kernel,
        out_shape=jax.ShapeDtypeStruct((count, NZ, *rest), flat[0].dtype),
        in_specs=[SM] + [VM] * len(flat) + [ANY] * len(after),
        out_specs=VM,
        compiler_params=params(10),
        cost_estimate=cheap(),
        name="stack_z",
    )(ids, *flat, *after)


def direct_x(value):
    return jnp.stack([shift(value, "x", k) for k in range(NX)])


def both_ways(up, down, axis):
    return shift(up, axis, 1), shift(down, axis, -1)


def norm_kernel(p_ref, a_ref, gain_ref, scaled_ref, inv_ref):
    gain = gain_ref[...].astype(F32)
    for ref, lo, rows in ((p_ref, 0, PR), (a_ref, PR, AR)):
        for r in range(0, rows, 32):
            wide = ref[r : r + 32, :].astype(F32)
            inv = lax.rsqrt(jnp.mean(wide * wide, axis=-1, keepdims=True) + EPSILON)
            scaled_ref[lo + r : lo + r + 32, :] = (wide * inv * gain).astype(BF)
            inv_ref[lo + r : lo + r + 32, :] = inv


def norm(prompt, answer, gain):
    rows = PR + AR
    return pl.pallas_call(
        norm_kernel,
        out_shape=[jax.ShapeDtypeStruct((rows, D), BF), jax.ShapeDtypeStruct((rows, 1), F32)],
        in_specs=[VM] * 3,
        out_specs=[VM] * 2,
        compiler_params=params(16),
        cost_estimate=cheap(),
        name="norm",
    )(prompt, answer, gain)


def place(ids, s_ref, t_ref, w_ref, sem):
    blocks = []
    for k in range(NX):
        copies = []
        for rel in range(2):
            dst = w_ref.at[k, :, lax.rem(ids[2] + rel, 2)]
            copies.append(pltpu.make_async_copy((s_ref, t_ref)[rel].at[k], dst, sem.at[k, rel]))
            copies[-1].start()
        blocks.append(copies)
    return blocks


def block_columns(ids, k):
    return pl.ds(pl.multiple_of(lax.rem(ids[0] - k + NX, NX) * BLK, BLK), BLK)


def project_kernel(ids, a_ref, s_ref, t_ref, out_ref, w_ref, sem):
    width = w_ref.shape[-1]
    copies = place(ids, s_ref, t_ref, w_ref, sem)
    total = jnp.zeros((PR + AR, width), F32)
    for k in range(NX):
        for copy in copies[k]:
            copy.wait()
        total += nn(a_ref[:, block_columns(ids, k)], w_ref[k].reshape(BLK, width))
    out_ref[...] = total.astype(BF)


def project(ids, scaled, pieces, pieces_sib):
    width = pieces.shape[-1]
    rows = scaled.shape[0]
    return pl.pallas_call(
        project_kernel,
        out_shape=jax.ShapeDtypeStruct((rows, width), BF),
        in_specs=[SM, VM, HBM, HBM],
        out_specs=VM,
        scratch_shapes=[pltpu.VMEM((NX, NZ, NC, WR, width), BF), pltpu.SemaphoreType.DMA((NX, 2))],
        compiler_params=params(16),
        cost_estimate=cheap(),
        name="project",
    )(ids, scaled, pieces, pieces_sib)


def stacked(value):
    return jnp.concatenate([value[:, h * HD : (h + 1) * HD] for h in range(HEADS)], axis=0)


def attention_kernel(
    ids, owners, lengths, q_ref, kv_ref, gp_ref, ga_ref, s_ref, t_ref, after_ref,
    gq_ref, gkv_ref, own_ref, sib_ref, pairs, dense, sem,
):
    del after_ref
    x, z, c = ids[0], ids[1], ids[2]
    own_prompt = x * 4 + z // 2
    prompts = [owners[s] for s in range(SLOTS)] + [own_prompt]
    copies = []
    for b, p in enumerate(prompts):
        k = lax.rem(x - p // 4 + NX, NX)
        for half in range(2):
            for rel in range(2):
                at = pl.multiple_of((half * 2 + lax.rem(c + rel, 2)) * PR, PR)
                src = (s_ref, t_ref)[rel].at[k, lax.rem(p, 4) * 2 + half]
                copies.append(pltpu.make_async_copy(src, pairs.at[b, pl.ds(at, PR)], sem.at[b, half, rel]))
                copies[-1].start()
    dense[...] = jnp.zeros_like(dense)
    row_step = lax.rem(lax.broadcasted_iota(jnp.int32, (HEADS * SR, SR), 0), SR)
    col_step = lax.broadcasted_iota(jnp.int32, (HEADS * SR, SR), 1)
    live_step = lax.broadcasted_iota(jnp.int32, (SR, QC), 0)
    per_block = 4
    for b in range(SLOTS + 1):
        for copy in copies[b * per_block : (b + 1) * per_block]:
            copy.wait()
        keys, values = pairs[b, :, :HD], pairs[b, :, HD:]
        if b < SLOTS:
            lo = PR + b * SR
            length = lengths[b]
            upstream = ga_ref[b * SR : (b + 1) * SR, :]
            upstream = jnp.where(live_step < length, upstream.astype(F32), 0.0).astype(BF)
        else:
            lo = 0
            upstream = gp_ref[...]
        q4 = stacked(q_ref[lo : lo + SR, :])
        g4 = stacked(upstream)
        s1 = SCALE * nt(q4, keys)
        gp1 = nt(g4, values)
        if b < SLOTS:
            k_own = kv_ref[lo : lo + SR, :HD]
            v_own = kv_ref[lo : lo + SR, HD:]
            s2 = SCALE * nt(q4, k_own)
            gp2 = nt(g4, v_own)
            seen = (row_step >= col_step) & (col_step < length)
            s2 = jnp.where(seen, s2, -jnp.inf)
            top = jnp.maximum(jnp.max(s1, axis=1, keepdims=True), jnp.max(s2, axis=1, keepdims=True))
            e1 = jnp.exp(s1 - top)
            e2 = jnp.exp(s2 - top)
            norm = 1.0 / (jnp.sum(e1, axis=1, keepdims=True) + jnp.sum(e2, axis=1, keepdims=True))
            p1 = e1 * norm
            p2 = e2 * norm
            delta = jnp.sum(p1 * gp1, axis=1, keepdims=True) + jnp.sum(p2 * gp2, axis=1, keepdims=True)
            d2 = (p2 * (gp2 - delta)).astype(BF)
        else:
            offset = (lax.rem(z, 2) * 2 + c) * PR
            rows = lax.rem(lax.broadcasted_iota(jnp.int32, (HEADS * SR, PLEN), 0), SR) + offset
            cols = lax.broadcasted_iota(jnp.int32, (HEADS * SR, PLEN), 1)
            s1 = jnp.where(rows >= cols, s1, -jnp.inf)
            top = jnp.max(s1, axis=1, keepdims=True)
            e1 = jnp.exp(s1 - top)
            p1 = e1 * (1.0 / jnp.sum(e1, axis=1, keepdims=True))
            delta = jnp.sum(p1 * gp1, axis=1, keepdims=True)
        d1 = (p1 * (gp1 - delta)).astype(BF)
        gq = nn(d1, keys)
        if b < SLOTS:
            gq += nn(d2, k_own)
            gkv_ref[b * SR : (b + 1) * SR, :HD] = (SCALE * tn(d2, q4)).astype(BF)
            gkv_ref[b * SR : (b + 1) * SR, HD:] = tn(p2.astype(BF), g4).astype(BF)
        gq = (SCALE * gq).astype(BF)
        for h in range(HEADS):
            gq_ref[lo : lo + SR, h * HD : (h + 1) * HD] = gq[h * SR : (h + 1) * SR, :]
        p = prompts[b]
        dense[p, :, :, :HD] += (SCALE * tn(d1, q4)).reshape(4, PR, HD)
        dense[p, :, :, HD:] += tn(p1.astype(BF), g4).reshape(4, PR, HD)
    for half in range(2):
        own_ref[:, half] = dense[:, half * 2 + c].astype(BF)
        sib_ref[:, half] = dense[:, half * 2 + 1 - c].astype(BF)


def attention(ids, owners, lengths, q, kv, gp, ga, pairs, pairs_sib, after):
    return pl.pallas_call(
        attention_kernel,
        out_shape=[
            jax.ShapeDtypeStruct((PR + AR, QC), BF),
            jax.ShapeDtypeStruct((AR, 2 * HD), BF),
            jax.ShapeDtypeStruct((PROMPTS, 2, PR, 2 * HD), BF),
            jax.ShapeDtypeStruct((PROMPTS, 2, PR, 2 * HD), BF),
        ],
        in_specs=[SM] * 3 + [VM] * 4 + [ANY] * 3,
        out_specs=[VM] * 4,
        scratch_shapes=[
            pltpu.VMEM((SLOTS + 1, PLEN, 2 * HD), BF),
            pltpu.VMEM((PROMPTS, 4, PR, 2 * HD), F32),
            pltpu.SemaphoreType.DMA((SLOTS + 1, 2, 2)),
        ],
        compiler_params=params(16),
        cost_estimate=cheap(),
        name="attention",
    )(ids, owners, lengths, q, kv, gp, ga, pairs, pairs_sib, after)


def row_coefficient(gq, gkv, q, kv, inv):
    row_dot = jnp.sum(gq.astype(F32) * q.astype(F32), axis=1, keepdims=True)
    row_dot += jnp.sum(gkv.astype(F32) * kv.astype(F32), axis=1, keepdims=True)
    return inv * inv * row_dot * (1.0 / D)


def answer_grads_kernel(
    ids, gq_ref, gkv_ref, q_ref, kv_ref, inv_ref, gain_ref, x_ref, qs_ref, qt_ref, ks_ref, kt_ref,
    out_ref, share_ref, token_ref, wq, wkv, states, result, sem_q, sem_kv, sem_x, sem_out,
):
    q_copies = place(ids, qs_ref, qt_ref, wq, sem_q)
    kv_copies = place(ids, ks_ref, kt_ref, wkv, sem_kv)
    x_copy = pltpu.make_async_copy(x_ref, states, sem_x)
    x_copy.start()
    gq, gkv = gq_ref[...], gkv_ref[...]
    inv = inv_ref[PR:, :]
    coefficient = row_coefficient(gq_ref[PR:, :], gkv, q_ref[PR:, :], kv_ref[PR:, :], inv)
    out_copies = []
    for k in range(NX):
        for copy in q_copies[k] + kv_copies[k]:
            copy.wait()
        cols = block_columns(ids, k)
        by_query = nt(gq, wq[k].reshape(BLK, QC))
        share_ref[:, cols] = by_query[:PR]
        hidden = by_query[PR:] + nt(gkv, wkv[k].reshape(BLK, 2 * HD))
        if k == 0:
            x_copy.wait()
        moved = inv * gain_ref[:, cols].astype(F32) * hidden - states[:, cols].astype(F32) * coefficient
        result[k] = moved.astype(BF)
        out_copies.append(pltpu.make_async_copy(result.at[k], out_ref.at[:, cols], sem_out.at[k]))
        out_copies[-1].start()
    for copy in out_copies:
        copy.wait()
    token_ref[...] = jnp.zeros_like(token_ref)


def answer_grads(ids, gq, gkv, q, kv, inv, gain, states, pieces):
    return pl.pallas_call(
        answer_grads_kernel,
        out_shape=[
            jax.ShapeDtypeStruct((AR, D), BF),
            jax.ShapeDtypeStruct((PR, D), F32),
            jax.ShapeDtypeStruct((8, 128), F32),
        ],
        in_specs=[SM] + [VM] * 6 + [HBM] * 5,
        out_specs=[HBM, VM, VM],
        scratch_shapes=[
            pltpu.VMEM((NX, NZ, NC, WR, QC), BF),
            pltpu.VMEM((NX, NZ, NC, WR, 2 * HD), BF),
            pltpu.VMEM((AR, D), BF),
            pltpu.VMEM((NX, AR, BLK), BF),
            pltpu.SemaphoreType.DMA((NX, 2)),
            pltpu.SemaphoreType.DMA((NX, 2)),
            pltpu.SemaphoreType.DMA,
            pltpu.SemaphoreType.DMA((NX,)),
        ],
        compiler_params=params(52),
        cost_estimate=cheap(),
        name="answer_grads",
    )(ids, gq, gkv, q, kv, inv, gain, states, *pieces)


def prompt_grads_kernel(
    ids, gq_ref, gkv_ref, q_ref, kv_ref, inv_ref, gain_ref, x_ref, share_ref, ks_ref, kt_ref, out_ref, wkv, sem
):
    copies = place(ids, ks_ref, kt_ref, wkv, sem)
    gkv = gkv_ref[...]
    inv = inv_ref[:PR, :]
    coefficient = row_coefficient(gq_ref[:PR, :], gkv, q_ref[:PR, :], kv_ref[:PR, :], inv)
    for k in range(NX):
        for copy in copies[k]:
            copy.wait()
        cols = block_columns(ids, k)
        hidden = share_ref[:, cols] + nt(gkv, wkv[k].reshape(BLK, 2 * HD))
        moved = inv * gain_ref[:, cols].astype(F32) * hidden - x_ref[:, cols].astype(F32) * coefficient
        out_ref[:, cols] = moved.astype(BF)


def prompt_grads(ids, gq, gkv, q, kv, inv, gain, states, share, pieces):
    return pl.pallas_call(
        prompt_grads_kernel,
        out_shape=jax.ShapeDtypeStruct((PR, D), BF),
        in_specs=[SM] + [VM] * 8 + [HBM] * 2,
        out_specs=VM,
        scratch_shapes=[pltpu.VMEM((NX, NZ, NC, WR, 2 * HD), BF), pltpu.SemaphoreType.DMA((NX, 2))],
        compiler_params=params(12),
        cost_estimate=cheap(),
        name="prompt_grads",
    )(ids, gq, gkv, q, kv, inv, gain, states, share, *pieces)


def weight_grads_kernel(ids, own_ref, sib_ref, g_ref, gs_ref, *refs):
    plus_ref, minus_ref, u_ref, l_ref, mine_ref = refs[-5:]
    x = ids[0]
    width = g_ref.shape[1]
    g, gs = g_ref[...], gs_ref[...]

    def product(k, lo, count):
        at = pl.ds(lax.rem(x + k, NX) * NZ + lo, count)
        rows = count * WR
        total = nn(own_ref[at].reshape(rows, PR + AR), g) + nn(sib_ref[at].reshape(rows, PR + AR), gs)
        return total.astype(BF).reshape(count, WR, width)

    half = NZ // 2
    plus_ref[0] = product(2, 0, half)
    minus_ref[0] = product(2, half, half)
    plus_ref[1] = product(1, half, half)
    minus_ref[1] = product(3, 0, half)
    u_ref[...] = product(1, 0, half)
    l_ref[...] = product(3, half, half)
    mine_ref[...] = product(0, 0, NZ)


def weight_grads(ids, own, sib, grads, grads_sib, after):
    width = grads.shape[1]
    half = NZ // 2

    def shape(*dims):
        return jax.ShapeDtypeStruct((*dims, WR, width), BF)

    return pl.pallas_call(
        weight_grads_kernel,
        out_shape=[shape(2, half), shape(2, half), shape(half), shape(half), shape(NZ)],
        in_specs=[SM] + [VM] * 4 + [ANY] * len(after),
        out_specs=[VM] * 5,
        compiler_params=params(16),
        cost_estimate=cheap(),
        name="weight_grads",
    )(ids, own, sib, grads, grads_sib, *after)


def add_up(value):
    return jnp.sum(value.astype(F32), axis=0)


def join(upper, lower, plus, minus, mine, after):
    half = NZ // 2

    def kernel(upper_ref, lower_ref, plus_ref, minus_ref, mine_ref, *refs):
        out_ref = refs[-1]
        first = mine_ref[:half].astype(F32) + minus_ref[1].astype(F32) + upper_ref[...].astype(F32)
        second = mine_ref[half:].astype(F32) + plus_ref[1].astype(F32) + lower_ref[...].astype(F32)
        out_ref[:half] = first.astype(BF)
        out_ref[half:] = second.astype(BF)

    return pl.pallas_call(
        kernel,
        out_shape=jax.ShapeDtypeStruct(mine.shape, BF),
        in_specs=[VM] * 5 + [ANY] * len(after),
        out_specs=VM,
        compiler_params=params(10),
        cost_estimate=cheap(),
        name="join",
    )(upper, lower, plus, minus, mine, *after)


def first_hop(plus, minus):
    return shift(plus, "x", 1), shift(minus, "x", -1)


def second_sums(plus, minus, upper, lower, after):
    return add_after(upper, plus, after), add_after(lower, minus, after)


def per_device(
    prompt_states,
    answer_states,
    prompt_cotangent,
    answer_cotangent,
    norm_gain,
    weights,
    answer_length,
    answer_owner,
):
    x, z, c = lax.axis_index("x"), lax.axis_index("z"), lax.axis_index("c")
    ids = jnp.stack([x, z, c]).astype(jnp.int32)
    lengths, owners = answer_length[0], answer_owner[0]
    shard = weights[0]
    gain = norm_gain[0].astype(F32)

    kv_all = spread(shard[:, QC:], "z")
    q_line = direct_x(shard[:, :QC])
    scaled, inverse = norm(prompt_states[0], answer_states[0], norm_gain)
    kv_line = held(kv_all, (inverse, q_line))
    kv_near = both_ways(kv_line, kv_line, "x")
    q_line = held(q_line, (kv_line,))
    q_one = both_ways(q_line, q_line, "z")
    kv_near = held(kv_near[0], q_one), held(kv_near[1], q_one)
    kv_far = both_ways(kv_near[0][: NZ // 2], kv_near[1][NZ // 2 :], "x")
    q_one = held(q_one[0], kv_near), held(q_one[1], kv_near)
    q_two = both_ways(*q_one, "z")
    kv_pieces = stack_after([kv_line, kv_near[0], kv_far, kv_near[1]], q_two)
    kv_sib = shift(kv_pieces, "c", 1)
    q_two = held(q_two[0], kv_far), held(q_two[1], kv_far)
    q_three = both_ways(*q_two, "z")
    kv = project(ids, scaled, kv_pieces, kv_sib)
    pair_line = spread(kv[:PR], "z")
    pair_hops = [shift(pair_line, "x", k) for k in range(NX)]
    scaled = held(scaled, (kv,))
    scaled_t = scaled.T.reshape(NX * NZ, NC, WR, PR + AR)
    own_t = lax.dynamic_index_in_dim(scaled_t, c, 1, keepdims=False)
    other_t = lax.dynamic_index_in_dim(scaled_t, 1 - c, 1, keepdims=False)
    sib_t = shift(other_t, "c", 1)
    q_three = held(q_three[0], (pair_line, own_t, other_t)), held(q_three[1], (pair_line, own_t, other_t))
    q_four = both_ways(q_three[0][: NX // 2], q_three[1][NX // 2 :], "z")
    q_pieces = stack_z(
        ids,
        [q_line, q_one[0], q_two[0], q_three[0], q_four, q_three[1], q_two[1], q_one[1]],
        tuple(pair_hops[1:]),
    )
    q_sib = shift(q_pieces, "c", 1)
    q = project(ids, scaled, q_pieces, q_sib)
    pairs = stack_after(pair_hops, (kv,))
    pairs_sib = shift(pairs, "c", 1)

    gq, gkv_answer, own, sib = attention(
        ids, owners, lengths, q, kv, prompt_cotangent[0], answer_cotangent[0], pairs, pairs_sib, sib_t
    )
    gq_sib = shift(gq, "c", 1)
    answer_back, share, token = answer_grads(
        ids, gq, gkv_answer, q, kv, inverse, norm_gain, answer_states[0], (q_pieces, q_sib, kv_pieces, kv_sib)
    )
    answer_out = shift(answer_back, "section", -1)
    query_parts = weight_grads(ids, own_t, sib_t, gq, gq_sib, (token,))
    query_hop = first_hop(*query_parts[:2])

    terms = sum_after(own, shift(sib, "c", 1), (token,)).reshape(NX * NZ, PR, 2 * HD)
    gkv_prompt = add_up(exchange(terms, ("x", "z"))).astype(BF)
    gkv = jnp.concatenate([gkv_prompt, gkv_answer], axis=0)
    gkv_sib = shift(gkv, "c", 1)
    query_sums = second_sums(*query_hop, *query_parts[2:4], ())
    query_second = both_ways(*query_sums, "x")
    pair_parts = weight_grads(ids, own_t, sib_t, gkv, gkv_sib, query_sums)
    pair_hop = first_hop(*pair_parts[:2])
    prompt_back = prompt_grads(
        ids, gq, gkv_prompt, q, kv, inverse, norm_gain, prompt_states[0], share, (kv_pieces, kv_sib)
    )
    prompt_out = forward(shift(prompt_back, "section", -1))
    pair_second = both_ways(*second_sums(*pair_hop, *pair_parts[2:4], ()), "x")
    query_last = exchange(join(*query_second, *query_hop, query_parts[4], (pair_parts[0],)), "z")
    pair_last = exchange(join(*pair_second, *pair_hop, pair_parts[4], (answer_out, query_last)), "z")
    query_total, pair_total = add_up(query_last), add_up(pair_last)

    weight_total = jnp.concatenate([query_total, pair_total], axis=1)
    own_gain = lax.dynamic_slice(gain, (((x * NZ + z) * NC + c) * WR,), (WR,))
    gain_total = jnp.sum(weight_total * shard.astype(F32), axis=1) / own_gain
    return (prompt_out[None], forward(answer_out)[None], weight_total[None], gain_total[None])


def solution(mesh):
    fine = Mesh(mesh.devices.reshape(mesh.devices.shape[0], NX, NZ, NC), ("section", "x", "z", "c"))
    dp = ("x", "z", "c")
    placed = (
        P("section", dp, None),
        P("section", dp, None),
        P("section", dp, None),
        P("section", dp, None),
        P("section", None),
        P("section", dp, None),
        P("section", dp),
        P("section", dp),
    )
    return jax.shard_map(
        per_device,
        mesh=fine,
        in_specs=placed,
        out_specs=(
            P("section", dp, None),
            P("section", dp, None),
            P("section", dp, None),
            P("section", dp),
        ),
        check_vma=False,
    )
```

```python
import functools

import jax
import jax.numpy as jnp
from jax import lax
from jax.experimental import pallas as pl
from jax.experimental.pallas import tpu as pltpu
from jax.sharding import Mesh, PartitionSpec as P

HD = 128
HEADS = 4
QC = HEADS * HD
D = 5120
PR = 64
AR = 256
SLOTS = 4
SR = 64
NX, NZ, NC = 4, 8, 2
WR = 80
BLK = D // NX
PROMPTS = 16
PLEN = 256
EPSILON = 1e-06
SCALE = HD**-0.5
BF = jnp.bfloat16
F32 = jnp.float32
MIB = 1024 * 1024


def shift(value, axis, steps):
    count = lax.axis_size(axis)
    if steps % count == 0:
        return value
    return lax.ppermute(value, axis, [(s, (s + steps) % count) for s in range(count)])


def params(mib):
    return pltpu.CompilerParams(vmem_limit_bytes=mib * MIB)


def cheap():
    return pl.CostEstimate(flops=10**6, bytes_accessed=10**5, transcendentals=0)


ANY = pl.BlockSpec(memory_space=pl.ANY)
HBM = pl.BlockSpec(memory_space=pltpu.HBM)
VM = pl.BlockSpec(memory_space=pltpu.VMEM)
SM = pl.BlockSpec(memory_space=pltpu.SMEM)


def nt(a, b):
    return lax.dot_general(a, b, (((1,), (1,)), ((), ())), preferred_element_type=F32)


def tn(a, b):
    return lax.dot_general(a, b, (((0,), (0,)), ((), ())), preferred_element_type=F32)


def nn(a, b):
    return jnp.dot(a, b, preferred_element_type=F32)


def exchange(value, axis):
    return lax.all_to_all(value, axis, 0, 0, tiled=True)


def spread(value, axis):
    count = lax.axis_size(axis)
    return exchange(jnp.broadcast_to(value[None], (count, *value.shape)), axis)


def held(value, after):
    def kernel(*refs):
        del refs

    return pl.pallas_call(
        kernel,
        out_shape=jax.ShapeDtypeStruct(value.shape, value.dtype),
        in_specs=[ANY] * (1 + len(after)),
        out_specs=ANY,
        input_output_aliases={0: 0},
        compiler_params=params(4),
        cost_estimate=cheap(),
        name="held",
    )(value, *after)


def sum_after(left, right, after):
    def kernel(left_ref, right_ref, *refs):
        out_ref = refs[-1]
        out_ref[...] = (left_ref[...].astype(F32) + right_ref[...].astype(F32)).astype(BF)

    return pl.pallas_call(
        kernel,
        out_shape=jax.ShapeDtypeStruct(left.shape, BF),
        in_specs=[VM, VM] + [ANY] * len(after),
        out_specs=VM,
        compiler_params=params(10),
        cost_estimate=cheap(),
        name="sum",
    )(left, right, *after)


def add_after(left, right, after):
    def kernel(left_ref, right_ref, *refs):
        out_ref = refs[-1]
        out_ref[...] = (left_ref[...].astype(F32) + right_ref[0].astype(F32)).astype(BF)

    return pl.pallas_call(
        kernel,
        out_shape=jax.ShapeDtypeStruct(left.shape, BF),
        in_specs=[VM, VM] + [ANY] * len(after),
        out_specs=VM,
        compiler_params=params(6),
        cost_estimate=cheap(),
        name="add",
    )(left, right, *after)


def forward(value):
    rows, width = value.shape
    spec = pl.BlockSpec((32, width), lambda i: (i, 0))

    def kernel(value_ref, out_ref):
        out_ref[...] = value_ref[...]

    return pl.pallas_call(
        kernel,
        out_shape=jax.ShapeDtypeStruct(value.shape, value.dtype),
        grid=(rows // 32,),
        in_specs=[spec],
        out_specs=spec,
        compiler_params=params(4),
        cost_estimate=cheap(),
        name="forward",
    )(value)


def stack_after(pieces, after):
    flat = [part for piece in pieces for part in (piece if isinstance(piece, tuple) else (piece,))]
    shape = pieces[0].shape

    def kernel(*refs):
        out_ref = refs[-1]
        at = 0
        for i, piece in enumerate(pieces):
            if isinstance(piece, tuple):
                cut = shape[0] // 2
                out_ref[i, :cut] = refs[at][...]
                out_ref[i, cut:] = refs[at + 1][...]
                at += 2
            else:
                out_ref[i] = refs[at][...]
                at += 1

    return pl.pallas_call(
        kernel,
        out_shape=jax.ShapeDtypeStruct((len(pieces), *shape), flat[0].dtype),
        in_specs=[VM] * len(flat) + [ANY] * len(after),
        out_specs=VM,
        compiler_params=params(10),
        cost_estimate=cheap(),
        name="stack",
    )(*flat, *after)


def stack_z(ids, pieces, after):
    half = NZ // 2
    flat = [*pieces[:half], *pieces[half], *pieces[half + 1 :]]
    count, *rest = pieces[0].shape

    def kernel(ids, *refs):
        out_ref = refs[-1]

        def at(j):
            return lax.rem(ids[1] - j + NZ, NZ)

        for j in range(half):
            out_ref[:, at(j)] = refs[j][...]
        out_ref[: count // 2, at(half)] = refs[half][...]
        out_ref[count // 2 :, at(half)] = refs[half + 1][...]
        for j in range(half + 1, NZ):
            out_ref[:, at(j)] = refs[j + 1][...]

    return pl.pallas_call(
        kernel,
        out_shape=jax.ShapeDtypeStruct((count, NZ, *rest), flat[0].dtype),
        in_specs=[SM] + [VM] * len(flat) + [ANY] * len(after),
        out_specs=VM,
        compiler_params=params(10),
        cost_estimate=cheap(),
        name="stack_z",
    )(ids, *flat, *after)


def direct_x(value):
    return jnp.stack([shift(value, "x", k) for k in range(NX)])


def both_ways(up, down, axis):
    return shift(up, axis, 1), shift(down, axis, -1)


def norm_kernel(p_ref, a_ref, gain_ref, scaled_ref, inv_ref):
    gain = gain_ref[...].astype(F32)
    for ref, lo, rows in ((p_ref, 0, PR), (a_ref, PR, AR)):
        for r in range(0, rows, 32):
            wide = ref[r : r + 32, :].astype(F32)
            inv = lax.rsqrt(jnp.mean(wide * wide, axis=-1, keepdims=True) + EPSILON)
            scaled_ref[lo + r : lo + r + 32, :] = (wide * inv * gain).astype(BF)
            inv_ref[lo + r : lo + r + 32, :] = inv


def norm(prompt, answer, gain):
    rows = PR + AR
    return pl.pallas_call(
        norm_kernel,
        out_shape=[jax.ShapeDtypeStruct((rows, D), BF), jax.ShapeDtypeStruct((rows, 1), F32)],
        in_specs=[VM] * 3,
        out_specs=[VM] * 2,
        compiler_params=params(16),
        cost_estimate=cheap(),
        name="norm",
    )(prompt, answer, gain)


def block_copies(ids, s_ref, t_ref, w_ref, sem, k):
    return [
        pltpu.make_async_copy((s_ref, t_ref)[rel].at[k], w_ref.at[k, :, lax.rem(ids[2] + rel, 2)], sem.at[k, rel])
        for rel in range(2)
    ]


def place(ids, s_ref, t_ref, w_ref, sem):
    blocks = [block_copies(ids, s_ref, t_ref, w_ref, sem, k) for k in range(NX)]
    for copies in blocks:
        for copy in copies:
            copy.start()
    return blocks


def block_columns(ids, k):
    return pl.ds(pl.multiple_of(lax.rem(ids[0] - k + NX, NX) * BLK, BLK), BLK)


def project_kernel(ids, a_ref, s_ref, t_ref, out_ref, w_ref, sem):
    width = w_ref.shape[-1]
    copies = place(ids, s_ref, t_ref, w_ref, sem)
    total = jnp.zeros((PR + AR, width), F32)
    for k in range(NX):
        for copy in copies[k]:
            copy.wait()
        total += nn(a_ref[:, block_columns(ids, k)], w_ref[k].reshape(BLK, width))
    out_ref[...] = total.astype(BF)


def project(ids, scaled, pieces, pieces_sib):
    width = pieces.shape[-1]
    rows = scaled.shape[0]
    return pl.pallas_call(
        project_kernel,
        out_shape=jax.ShapeDtypeStruct((rows, width), BF),
        in_specs=[SM, VM, HBM, HBM],
        out_specs=VM,
        scratch_shapes=[pltpu.VMEM((NX, NZ, NC, WR, width), BF), pltpu.SemaphoreType.DMA((NX, 2))],
        compiler_params=params(16),
        cost_estimate=cheap(),
        name="project",
    )(ids, scaled, pieces, pieces_sib)


def stacked(value):
    return jnp.concatenate([value[:, h * HD : (h + 1) * HD] for h in range(HEADS)], axis=0)


def attention_kernel(
    ids, owners, lengths, q_ref, kv_ref, gp_ref, ga_ref, s_ref, t_ref, after_ref,
    gq_ref, gkv_ref, own_ref, sib_ref, pairs, dense, sem,
):
    del after_ref
    x, z, c = ids[0], ids[1], ids[2]
    own_prompt = x * 4 + z // 2
    prompts = [owners[s] for s in range(SLOTS)] + [own_prompt]
    copies = []
    for b, p in enumerate(prompts):
        k = lax.rem(x - p // 4 + NX, NX)
        for half in range(2):
            for rel in range(2):
                at = pl.multiple_of((half * 2 + lax.rem(c + rel, 2)) * PR, PR)
                src = (s_ref, t_ref)[rel].at[k, lax.rem(p, 4) * 2 + half]
                copies.append(pltpu.make_async_copy(src, pairs.at[b, pl.ds(at, PR)], sem.at[b, half, rel]))
                copies[-1].start()
    dense[...] = jnp.zeros_like(dense)
    row_step = lax.rem(lax.broadcasted_iota(jnp.int32, (HEADS * SR, SR), 0), SR)
    col_step = lax.broadcasted_iota(jnp.int32, (HEADS * SR, SR), 1)
    live_step = lax.broadcasted_iota(jnp.int32, (SR, QC), 0)
    per_block = 4
    for b in range(SLOTS + 1):
        for copy in copies[b * per_block : (b + 1) * per_block]:
            copy.wait()
        keys, values = pairs[b, :, :HD], pairs[b, :, HD:]
        if b < SLOTS:
            lo = PR + b * SR
            length = lengths[b]
            upstream = ga_ref[b * SR : (b + 1) * SR, :]
            upstream = jnp.where(live_step < length, upstream.astype(F32), 0.0).astype(BF)
        else:
            lo = 0
            upstream = gp_ref[...]
        q4 = stacked(q_ref[lo : lo + SR, :])
        g4 = stacked(upstream)
        s1 = SCALE * nt(q4, keys)
        gp1 = nt(g4, values)
        if b < SLOTS:
            k_own = kv_ref[lo : lo + SR, :HD]
            v_own = kv_ref[lo : lo + SR, HD:]
            s2 = SCALE * nt(q4, k_own)
            gp2 = nt(g4, v_own)
            seen = (row_step >= col_step) & (col_step < length)
            s2 = jnp.where(seen, s2, -jnp.inf)
            top = jnp.maximum(jnp.max(s1, axis=1, keepdims=True), jnp.max(s2, axis=1, keepdims=True))
            e1 = jnp.exp(s1 - top)
            e2 = jnp.exp(s2 - top)
            norm = 1.0 / (jnp.sum(e1, axis=1, keepdims=True) + jnp.sum(e2, axis=1, keepdims=True))
            p1 = e1 * norm
            p2 = e2 * norm
            delta = jnp.sum(p1 * gp1, axis=1, keepdims=True) + jnp.sum(p2 * gp2, axis=1, keepdims=True)
            d2 = (p2 * (gp2 - delta)).astype(BF)
        else:
            offset = (lax.rem(z, 2) * 2 + c) * PR
            rows = lax.rem(lax.broadcasted_iota(jnp.int32, (HEADS * SR, PLEN), 0), SR) + offset
            cols = lax.broadcasted_iota(jnp.int32, (HEADS * SR, PLEN), 1)
            s1 = jnp.where(rows >= cols, s1, -jnp.inf)
            top = jnp.max(s1, axis=1, keepdims=True)
            e1 = jnp.exp(s1 - top)
            p1 = e1 * (1.0 / jnp.sum(e1, axis=1, keepdims=True))
            delta = jnp.sum(p1 * gp1, axis=1, keepdims=True)
        d1 = (p1 * (gp1 - delta)).astype(BF)
        gq = nn(d1, keys)
        if b < SLOTS:
            gq += nn(d2, k_own)
            gkv_ref[b * SR : (b + 1) * SR, :HD] = (SCALE * tn(d2, q4)).astype(BF)
            gkv_ref[b * SR : (b + 1) * SR, HD:] = tn(p2.astype(BF), g4).astype(BF)
        gq = (SCALE * gq).astype(BF)
        for h in range(HEADS):
            gq_ref[lo : lo + SR, h * HD : (h + 1) * HD] = gq[h * SR : (h + 1) * SR, :]
        p = prompts[b]
        dense[p, :, :, :HD] += (SCALE * tn(d1, q4)).reshape(4, PR, HD)
        dense[p, :, :, HD:] += tn(p1.astype(BF), g4).reshape(4, PR, HD)
    for half in range(2):
        own_ref[:, half] = dense[:, half * 2 + c].astype(BF)
        sib_ref[:, half] = dense[:, half * 2 + 1 - c].astype(BF)


def attention(ids, owners, lengths, q, kv, gp, ga, pairs, pairs_sib, after):
    return pl.pallas_call(
        attention_kernel,
        out_shape=[
            jax.ShapeDtypeStruct((PR + AR, QC), BF),
            jax.ShapeDtypeStruct((AR, 2 * HD), BF),
            jax.ShapeDtypeStruct((PROMPTS, 2, PR, 2 * HD), BF),
            jax.ShapeDtypeStruct((PROMPTS, 2, PR, 2 * HD), BF),
        ],
        in_specs=[SM] * 3 + [VM] * 4 + [ANY] * 3,
        out_specs=[VM] * 4,
        scratch_shapes=[
            pltpu.VMEM((SLOTS + 1, PLEN, 2 * HD), BF),
            pltpu.VMEM((PROMPTS, 4, PR, 2 * HD), F32),
            pltpu.SemaphoreType.DMA((SLOTS + 1, 2, 2)),
        ],
        compiler_params=params(16),
        cost_estimate=cheap(),
        name="attention",
    )(ids, owners, lengths, q, kv, gp, ga, pairs, pairs_sib, after)


def row_coefficient(gq, gkv, q, kv, inv):
    row_dot = jnp.sum(gq.astype(F32) * q.astype(F32), axis=1, keepdims=True)
    row_dot += jnp.sum(gkv.astype(F32) * kv.astype(F32), axis=1, keepdims=True)
    return inv * inv * row_dot * (1.0 / D)


def answer_grads_kernel(
    ids, gq_ref, gkv_ref, q_ref, kv_ref, inv_ref, gain_ref, x_ref, qs_ref, qt_ref, ks_ref, kt_ref,
    out_ref, share_ref, token_ref, wq, wkv, states, result, sem_q, sem_kv, sem_x, sem_out,
):
    x_copy = pltpu.make_async_copy(x_ref, states, sem_x)
    blocks = []
    for k in range(NX):
        blocks.append(
            block_copies(ids, qs_ref, qt_ref, wq, sem_q, k) + block_copies(ids, ks_ref, kt_ref, wkv, sem_kv, k)
        )
        for copy in blocks[k]:
            copy.start()
        if k == 0:
            x_copy.start()
    gq, gkv = gq_ref[...], gkv_ref[...]
    inv = inv_ref[PR:, :]
    coefficient = row_coefficient(gq_ref[PR:, :], gkv, q_ref[PR:, :], kv_ref[PR:, :], inv)
    out_copies = []
    for k in range(NX):
        for copy in blocks[k]:
            copy.wait()
        cols = block_columns(ids, k)
        by_query = nt(gq, wq[k].reshape(BLK, QC))
        share_ref[:, cols] = by_query[:PR]
        hidden = by_query[PR:] + nt(gkv, wkv[k].reshape(BLK, 2 * HD))
        if k == 0:
            x_copy.wait()
        moved = inv * gain_ref[:, cols].astype(F32) * hidden - states[:, cols].astype(F32) * coefficient
        result[k] = moved.astype(BF)
        out_copies.append(pltpu.make_async_copy(result.at[k], out_ref.at[:, cols], sem_out.at[k]))
        out_copies[-1].start()
    for copy in out_copies:
        copy.wait()
    token_ref[...] = jnp.zeros_like(token_ref)


def answer_grads(ids, gq, gkv, q, kv, inv, gain, states, pieces):
    return pl.pallas_call(
        answer_grads_kernel,
        out_shape=[
            jax.ShapeDtypeStruct((AR, D), BF),
            jax.ShapeDtypeStruct((PR, D), F32),
            jax.ShapeDtypeStruct((8, 128), F32),
        ],
        in_specs=[SM] + [VM] * 6 + [HBM] * 5,
        out_specs=[HBM, VM, VM],
        scratch_shapes=[
            pltpu.VMEM((NX, NZ, NC, WR, QC), BF),
            pltpu.VMEM((NX, NZ, NC, WR, 2 * HD), BF),
            pltpu.VMEM((AR, D), BF),
            pltpu.VMEM((NX, AR, BLK), BF),
            pltpu.SemaphoreType.DMA((NX, 2)),
            pltpu.SemaphoreType.DMA((NX, 2)),
            pltpu.SemaphoreType.DMA,
            pltpu.SemaphoreType.DMA((NX,)),
        ],
        compiler_params=params(52),
        cost_estimate=cheap(),
        name="answer_grads",
    )(ids, gq, gkv, q, kv, inv, gain, states, *pieces)


def prompt_grads_kernel(
    ids, gq_ref, gkv_ref, q_ref, kv_ref, inv_ref, gain_ref, x_ref, share_ref, ks_ref, kt_ref, out_ref, wkv, sem
):
    copies = place(ids, ks_ref, kt_ref, wkv, sem)
    gkv = gkv_ref[...]
    inv = inv_ref[:PR, :]
    coefficient = row_coefficient(gq_ref[:PR, :], gkv, q_ref[:PR, :], kv_ref[:PR, :], inv)
    for k in range(NX):
        for copy in copies[k]:
            copy.wait()
        cols = block_columns(ids, k)
        hidden = share_ref[:, cols] + nt(gkv, wkv[k].reshape(BLK, 2 * HD))
        moved = inv * gain_ref[:, cols].astype(F32) * hidden - x_ref[:, cols].astype(F32) * coefficient
        out_ref[:, cols] = moved.astype(BF)


def prompt_grads(ids, gq, gkv, q, kv, inv, gain, states, share, pieces):
    return pl.pallas_call(
        prompt_grads_kernel,
        out_shape=jax.ShapeDtypeStruct((PR, D), BF),
        in_specs=[SM] + [VM] * 8 + [HBM] * 2,
        out_specs=VM,
        scratch_shapes=[pltpu.VMEM((NX, NZ, NC, WR, 2 * HD), BF), pltpu.SemaphoreType.DMA((NX, 2))],
        compiler_params=params(12),
        cost_estimate=cheap(),
        name="prompt_grads",
    )(ids, gq, gkv, q, kv, inv, gain, states, share, *pieces)


def weight_grads_kernel(ids, own_ref, sib_ref, g_ref, gs_ref, *refs):
    plus_ref, minus_ref, u_ref, l_ref, mine_ref = refs[-5:]
    x = ids[0]
    width = g_ref.shape[1]
    g, gs = g_ref[...], gs_ref[...]

    def product(k, lo, count):
        at = pl.ds(lax.rem(x + k, NX) * NZ + lo, count)
        rows = count * WR
        total = nn(own_ref[at].reshape(rows, PR + AR), g) + nn(sib_ref[at].reshape(rows, PR + AR), gs)
        return total.astype(BF).reshape(count, WR, width)

    half = NZ // 2
    plus_ref[0] = product(2, 0, half)
    minus_ref[0] = product(2, half, half)
    plus_ref[1] = product(1, half, half)
    minus_ref[1] = product(3, 0, half)
    u_ref[...] = product(1, 0, half)
    l_ref[...] = product(3, half, half)
    mine_ref[...] = product(0, 0, NZ)


def weight_grads(ids, own, sib, grads, grads_sib, after):
    width = grads.shape[1]
    half = NZ // 2

    def shape(*dims):
        return jax.ShapeDtypeStruct((*dims, WR, width), BF)

    return pl.pallas_call(
        weight_grads_kernel,
        out_shape=[shape(2, half), shape(2, half), shape(half), shape(half), shape(NZ)],
        in_specs=[SM] + [VM] * 4 + [ANY] * len(after),
        out_specs=[VM] * 5,
        compiler_params=params(16),
        cost_estimate=cheap(),
        name="weight_grads",
    )(ids, own, sib, grads, grads_sib, *after)


def add_up(value):
    return jnp.sum(value.astype(F32), axis=0)


def join(upper, lower, plus, minus, mine, after):
    half = NZ // 2

    def kernel(upper_ref, lower_ref, plus_ref, minus_ref, mine_ref, *refs):
        out_ref = refs[-1]
        first = mine_ref[:half].astype(F32) + minus_ref[1].astype(F32) + upper_ref[...].astype(F32)
        second = mine_ref[half:].astype(F32) + plus_ref[1].astype(F32) + lower_ref[...].astype(F32)
        out_ref[:half] = first.astype(BF)
        out_ref[half:] = second.astype(BF)

    return pl.pallas_call(
        kernel,
        out_shape=jax.ShapeDtypeStruct(mine.shape, BF),
        in_specs=[VM] * 5 + [ANY] * len(after),
        out_specs=VM,
        compiler_params=params(10),
        cost_estimate=cheap(),
        name="join",
    )(upper, lower, plus, minus, mine, *after)


def first_hop(plus, minus):
    return shift(plus, "x", 1), shift(minus, "x", -1)


def second_sums(plus, minus, upper, lower, after):
    return add_after(upper, plus, after), add_after(lower, minus, after)


def per_device(
    prompt_states,
    answer_states,
    prompt_cotangent,
    answer_cotangent,
    norm_gain,
    weights,
    answer_length,
    answer_owner,
):
    x, z, c = lax.axis_index("x"), lax.axis_index("z"), lax.axis_index("c")
    ids = jnp.stack([x, z, c]).astype(jnp.int32)
    lengths, owners = answer_length[0], answer_owner[0]
    shard = weights[0]
    gain = norm_gain[0].astype(F32)

    kv_all = spread(shard[:, QC:], "z")
    q_line = direct_x(shard[:, :QC])
    scaled, inverse = norm(prompt_states[0], answer_states[0], norm_gain)
    kv_line = held(kv_all, (inverse, q_line))
    kv_near = both_ways(kv_line, kv_line, "x")
    q_line = held(q_line, (kv_line,))
    q_one = both_ways(q_line, q_line, "z")
    kv_near = held(kv_near[0], q_one), held(kv_near[1], q_one)
    kv_far = both_ways(kv_near[0][: NZ // 2], kv_near[1][NZ // 2 :], "x")
    q_one = held(q_one[0], kv_near), held(q_one[1], kv_near)
    q_two = both_ways(*q_one, "z")
    kv_pieces = stack_after([kv_line, kv_near[0], kv_far, kv_near[1]], q_two)
    kv_sib = shift(kv_pieces, "c", 1)
    q_two = held(q_two[0], kv_far), held(q_two[1], kv_far)
    q_three = both_ways(*q_two, "z")
    kv = project(ids, scaled, kv_pieces, kv_sib)
    pair_line = spread(kv[:PR], "z")
    pair_hops = [shift(pair_line, "x", k) for k in range(NX)]
    scaled = held(scaled, (kv,))
    scaled_t = scaled.T.reshape(NX * NZ, NC, WR, PR + AR)
    own_t = lax.dynamic_index_in_dim(scaled_t, c, 1, keepdims=False)
    other_t = lax.dynamic_index_in_dim(scaled_t, 1 - c, 1, keepdims=False)
    sib_t = shift(other_t, "c", 1)
    q_three = held(q_three[0], (pair_line, scaled_t)), held(q_three[1], (pair_line, scaled_t))
    q_four = both_ways(q_three[0][: NX // 2], q_three[1][NX // 2 :], "z")
    q_pieces = stack_z(
        ids,
        [q_line, q_one[0], q_two[0], q_three[0], q_four, q_three[1], q_two[1], q_one[1]],
        tuple(pair_hops[1:]),
    )
    q_sib = shift(q_pieces, "c", 1)
    q = project(ids, scaled, q_pieces, q_sib)
    pairs = stack_after(pair_hops, ())
    pairs_sib = shift(pairs, "c", 1)

    gq, gkv_answer, own, sib = attention(
        ids, owners, lengths, q, kv, prompt_cotangent[0], answer_cotangent[0], pairs, pairs_sib, other_t
    )
    gq_sib = shift(gq, "c", 1)
    answer_back, share, token = answer_grads(
        ids, gq, gkv_answer, q, kv, inverse, norm_gain, answer_states[0], (q_pieces, q_sib, kv_pieces, kv_sib)
    )
    answer_out = shift(answer_back, "section", -1)
    query_parts = weight_grads(ids, own_t, sib_t, gq, gq_sib, (token,))
    query_hop = first_hop(*query_parts[:2])

    terms = sum_after(own, shift(sib, "c", 1), ()).reshape(NX * NZ, PR, 2 * HD)
    gkv_prompt = add_up(exchange(terms, ("x", "z"))).astype(BF)
    gkv = jnp.concatenate([gkv_prompt, gkv_answer], axis=0)
    gkv_sib = shift(gkv, "c", 1)
    query_sums = second_sums(*query_hop, *query_parts[2:4], ())
    query_second = both_ways(*query_sums, "x")
    pair_parts = weight_grads(ids, own_t, sib_t, gkv, gkv_sib, query_sums)
    pair_hop = first_hop(*pair_parts[:2])
    prompt_back = prompt_grads(
        ids, gq, gkv_prompt, q, kv, inverse, norm_gain, prompt_states[0], share, (kv_pieces, kv_sib)
    )
    prompt_out = forward(shift(prompt_back, "section", -1))
    pair_second = both_ways(*second_sums(*pair_hop, *pair_parts[2:4], ()), "x")
    query_last = exchange(join(*query_second, *query_hop, query_parts[4], (pair_parts[0],)), "z")
    pair_last = exchange(join(*pair_second, *pair_hop, pair_parts[4], (answer_out, query_last)), "z")
    query_total, pair_total = add_up(query_last), add_up(pair_last)

    weight_total = jnp.concatenate([query_total, pair_total], axis=1)
    own_gain = lax.dynamic_slice(gain, (((x * NZ + z) * NC + c) * WR,), (WR,))
    gain_total = jnp.sum(weight_total * shard.astype(F32), axis=1) / own_gain
    return (prompt_out[None], forward(answer_out)[None], weight_total[None], gain_total[None])


def solution(mesh):
    fine = Mesh(mesh.devices.reshape(mesh.devices.shape[0], NX, NZ, NC), ("section", "x", "z", "c"))
    dp = ("x", "z", "c")
    placed = (
        P("section", dp, None),
        P("section", dp, None),
        P("section", dp, None),
        P("section", dp, None),
        P("section", None),
        P("section", dp, None),
        P("section", dp),
        P("section", dp),
    )
    return jax.shard_map(
        per_device,
        mesh=fine,
        in_specs=placed,
        out_specs=(
            P("section", dp, None),
            P("section", dp, None),
            P("section", dp, None),
            P("section", dp),
        ),
        check_vma=False,
    )
```

```python
import functools

import jax
import jax.numpy as jnp
from jax import lax
from jax.experimental import pallas as pl
from jax.experimental.pallas import tpu as pltpu
from jax.sharding import Mesh, PartitionSpec as P

HD = 128
HEADS = 4
QC = HEADS * HD
D = 5120
PR = 64
AR = 256
SLOTS = 4
SR = 64
NX, NZ, NC = 4, 8, 2
WR = 80
BLK = D // NX
PROMPTS = 16
PLEN = 256
EPSILON = 1e-06
SCALE = HD**-0.5
BF = jnp.bfloat16
F32 = jnp.float32
MIB = 1024 * 1024


def shift(value, axis, steps):
    count = lax.axis_size(axis)
    if steps % count == 0:
        return value
    return lax.ppermute(value, axis, [(s, (s + steps) % count) for s in range(count)])


def params(mib):
    return pltpu.CompilerParams(vmem_limit_bytes=mib * MIB)


def cheap():
    return pl.CostEstimate(flops=10**6, bytes_accessed=10**5, transcendentals=0)


ANY = pl.BlockSpec(memory_space=pl.ANY)
HBM = pl.BlockSpec(memory_space=pltpu.HBM)
VM = pl.BlockSpec(memory_space=pltpu.VMEM)
SM = pl.BlockSpec(memory_space=pltpu.SMEM)


def nt(a, b):
    return lax.dot_general(a, b, (((1,), (1,)), ((), ())), preferred_element_type=F32)


def tn(a, b):
    return lax.dot_general(a, b, (((0,), (0,)), ((), ())), preferred_element_type=F32)


def nn(a, b):
    return jnp.dot(a, b, preferred_element_type=F32)


def exchange(value, axis):
    return lax.all_to_all(value, axis, 0, 0, tiled=True)


def spread(value, axis):
    count = lax.axis_size(axis)
    return exchange(jnp.broadcast_to(value[None], (count, *value.shape)), axis)


def held(value, after):
    def kernel(*refs):
        del refs

    return pl.pallas_call(
        kernel,
        out_shape=jax.ShapeDtypeStruct(value.shape, value.dtype),
        in_specs=[ANY] * (1 + len(after)),
        out_specs=ANY,
        input_output_aliases={0: 0},
        compiler_params=params(4),
        cost_estimate=cheap(),
        name="held",
    )(value, *after)


def sum_after(left, right, after):
    def kernel(left_ref, right_ref, *refs):
        out_ref = refs[-1]
        out_ref[...] = (left_ref[...].astype(F32) + right_ref[...].astype(F32)).astype(BF)

    return pl.pallas_call(
        kernel,
        out_shape=jax.ShapeDtypeStruct(left.shape, BF),
        in_specs=[VM, VM] + [ANY] * len(after),
        out_specs=VM,
        compiler_params=params(10),
        cost_estimate=cheap(),
        name="sum",
    )(left, right, *after)


def add_after(left, right, after):
    def kernel(left_ref, right_ref, *refs):
        out_ref = refs[-1]
        out_ref[...] = (left_ref[...].astype(F32) + right_ref[0].astype(F32)).astype(BF)

    return pl.pallas_call(
        kernel,
        out_shape=jax.ShapeDtypeStruct(left.shape, BF),
        in_specs=[VM, VM] + [ANY] * len(after),
        out_specs=VM,
        compiler_params=params(6),
        cost_estimate=cheap(),
        name="add",
    )(left, right, *after)


def forward(value):
    rows, width = value.shape
    spec = pl.BlockSpec((32, width), lambda i: (i, 0))

    def kernel(value_ref, out_ref):
        out_ref[...] = value_ref[...]

    return pl.pallas_call(
        kernel,
        out_shape=jax.ShapeDtypeStruct(value.shape, value.dtype),
        grid=(rows // 32,),
        in_specs=[spec],
        out_specs=spec,
        compiler_params=params(4),
        cost_estimate=cheap(),
        name="forward",
    )(value)


def stack_after(pieces, after):
    flat = [part for piece in pieces for part in (piece if isinstance(piece, tuple) else (piece,))]
    shape = pieces[0].shape

    def kernel(*refs):
        out_ref = refs[-1]
        at = 0
        for i, piece in enumerate(pieces):
            if isinstance(piece, tuple):
                cut = shape[0] // 2
                out_ref[i, :cut] = refs[at][...]
                out_ref[i, cut:] = refs[at + 1][...]
                at += 2
            else:
                out_ref[i] = refs[at][...]
                at += 1

    return pl.pallas_call(
        kernel,
        out_shape=jax.ShapeDtypeStruct((len(pieces), *shape), flat[0].dtype),
        in_specs=[VM] * len(flat) + [ANY] * len(after),
        out_specs=VM,
        compiler_params=params(10),
        cost_estimate=cheap(),
        name="stack",
    )(*flat, *after)


def stack_z(ids, pieces, after):
    half = NZ // 2
    flat = [*pieces[:half], *pieces[half], *pieces[half + 1 :]]
    count, *rest = pieces[0].shape

    def kernel(ids, *refs):
        out_ref = refs[-1]

        def at(j):
            return lax.rem(ids[1] - j + NZ, NZ)

        for j in range(half):
            out_ref[:, at(j)] = refs[j][...]
        out_ref[: count // 2, at(half)] = refs[half][...]
        out_ref[count // 2 :, at(half)] = refs[half + 1][...]
        for j in range(half + 1, NZ):
            out_ref[:, at(j)] = refs[j + 1][...]

    return pl.pallas_call(
        kernel,
        out_shape=jax.ShapeDtypeStruct((count, NZ, *rest), flat[0].dtype),
        in_specs=[SM] + [VM] * len(flat) + [ANY] * len(after),
        out_specs=VM,
        compiler_params=params(10),
        cost_estimate=cheap(),
        name="stack_z",
    )(ids, *flat, *after)


def direct_x(value):
    return jnp.stack([shift(value, "x", k) for k in range(NX)])


def both_ways(up, down, axis):
    return shift(up, axis, 1), shift(down, axis, -1)


def norm_kernel(p_ref, a_ref, gain_ref, scaled_ref, inv_ref):
    gain = gain_ref[...].astype(F32)
    for ref, lo, rows in ((p_ref, 0, PR), (a_ref, PR, AR)):
        for r in range(0, rows, 32):
            wide = ref[r : r + 32, :].astype(F32)
            inv = lax.rsqrt(jnp.mean(wide * wide, axis=-1, keepdims=True) + EPSILON)
            scaled_ref[lo + r : lo + r + 32, :] = (wide * inv * gain).astype(BF)
            inv_ref[lo + r : lo + r + 32, :] = inv


def norm(prompt, answer, gain):
    rows = PR + AR
    return pl.pallas_call(
        norm_kernel,
        out_shape=[jax.ShapeDtypeStruct((rows, D), BF), jax.ShapeDtypeStruct((rows, 1), F32)],
        in_specs=[VM] * 3,
        out_specs=[VM] * 2,
        compiler_params=params(16),
        cost_estimate=cheap(),
        name="norm",
    )(prompt, answer, gain)


def block_copies(ids, s_ref, t_ref, w_ref, sem, k):
    return [
        pltpu.make_async_copy((s_ref, t_ref)[rel].at[k], w_ref.at[k, :, lax.rem(ids[2] + rel, 2)], sem.at[k, rel])
        for rel in range(2)
    ]


def place(ids, s_ref, t_ref, w_ref, sem):
    blocks = [block_copies(ids, s_ref, t_ref, w_ref, sem, k) for k in range(NX)]
    for copies in blocks:
        for copy in copies:
            copy.start()
    return blocks


def block_columns(ids, k):
    return pl.ds(pl.multiple_of(lax.rem(ids[0] - k + NX, NX) * BLK, BLK), BLK)


def project_kernel(ids, a_ref, s_ref, t_ref, out_ref, w_ref, sem):
    width = w_ref.shape[-1]
    copies = place(ids, s_ref, t_ref, w_ref, sem)
    total = jnp.zeros((PR + AR, width), F32)
    for k in range(NX):
        for copy in copies[k]:
            copy.wait()
        total += nn(a_ref[:, block_columns(ids, k)], w_ref[k].reshape(BLK, width))
    out_ref[...] = total.astype(BF)


def project(ids, scaled, pieces, pieces_sib):
    width = pieces.shape[-1]
    rows = scaled.shape[0]
    return pl.pallas_call(
        project_kernel,
        out_shape=jax.ShapeDtypeStruct((rows, width), BF),
        in_specs=[SM, VM, HBM, HBM],
        out_specs=VM,
        scratch_shapes=[pltpu.VMEM((NX, NZ, NC, WR, width), BF), pltpu.SemaphoreType.DMA((NX, 2))],
        compiler_params=params(16),
        cost_estimate=cheap(),
        name="project",
    )(ids, scaled, pieces, pieces_sib)


def stacked(value):
    return jnp.concatenate([value[:, h * HD : (h + 1) * HD] for h in range(HEADS)], axis=0)


def attention_kernel(
    ids, owners, lengths, q_ref, kv_ref, gp_ref, ga_ref, s_ref, t_ref, after_ref,
    gq_ref, gkv_ref, own_ref, sib_ref, pairs, dense, sem,
):
    del after_ref
    x, z, c = ids[0], ids[1], ids[2]
    own_prompt = x * 4 + z // 2
    prompts = [owners[s] for s in range(SLOTS)] + [own_prompt]
    copies = []
    for b, p in enumerate(prompts):
        k = lax.rem(x - p // 4 + NX, NX)
        for half in range(2):
            for rel in range(2):
                at = pl.multiple_of((half * 2 + lax.rem(c + rel, 2)) * PR, PR)
                src = (s_ref, t_ref)[rel].at[k, lax.rem(p, 4) * 2 + half]
                copies.append(pltpu.make_async_copy(src, pairs.at[b, pl.ds(at, PR)], sem.at[b, half, rel]))
                copies[-1].start()
    dense[...] = jnp.zeros_like(dense)
    row_step = lax.rem(lax.broadcasted_iota(jnp.int32, (HEADS * SR, SR), 0), SR)
    col_step = lax.broadcasted_iota(jnp.int32, (HEADS * SR, SR), 1)
    live_step = lax.broadcasted_iota(jnp.int32, (SR, QC), 0)
    per_block = 4
    for b in range(SLOTS + 1):
        for copy in copies[b * per_block : (b + 1) * per_block]:
            copy.wait()
        keys, values = pairs[b, :, :HD], pairs[b, :, HD:]
        if b < SLOTS:
            lo = PR + b * SR
            length = lengths[b]
            upstream = ga_ref[b * SR : (b + 1) * SR, :]
            upstream = jnp.where(live_step < length, upstream.astype(F32), 0.0).astype(BF)
        else:
            lo = 0
            upstream = gp_ref[...]
        q4 = stacked(q_ref[lo : lo + SR, :])
        g4 = stacked(upstream)
        s1 = SCALE * nt(q4, keys)
        gp1 = nt(g4, values)
        if b < SLOTS:
            k_own = kv_ref[lo : lo + SR, :HD]
            v_own = kv_ref[lo : lo + SR, HD:]
            s2 = SCALE * nt(q4, k_own)
            gp2 = nt(g4, v_own)
            seen = (row_step >= col_step) & (col_step < length)
            s2 = jnp.where(seen, s2, -jnp.inf)
            top = jnp.maximum(jnp.max(s1, axis=1, keepdims=True), jnp.max(s2, axis=1, keepdims=True))
            e1 = jnp.exp(s1 - top)
            e2 = jnp.exp(s2 - top)
            norm = 1.0 / (jnp.sum(e1, axis=1, keepdims=True) + jnp.sum(e2, axis=1, keepdims=True))
            p1 = e1 * norm
            p2 = e2 * norm
            delta = jnp.sum(p1 * gp1, axis=1, keepdims=True) + jnp.sum(p2 * gp2, axis=1, keepdims=True)
            d2 = (p2 * (gp2 - delta)).astype(BF)
        else:
            offset = (lax.rem(z, 2) * 2 + c) * PR
            rows = lax.rem(lax.broadcasted_iota(jnp.int32, (HEADS * SR, PLEN), 0), SR) + offset
            cols = lax.broadcasted_iota(jnp.int32, (HEADS * SR, PLEN), 1)
            s1 = jnp.where(rows >= cols, s1, -jnp.inf)
            top = jnp.max(s1, axis=1, keepdims=True)
            e1 = jnp.exp(s1 - top)
            p1 = e1 * (1.0 / jnp.sum(e1, axis=1, keepdims=True))
            delta = jnp.sum(p1 * gp1, axis=1, keepdims=True)
        d1 = (p1 * (gp1 - delta)).astype(BF)
        gq = nn(d1, keys)
        if b < SLOTS:
            gq += nn(d2, k_own)
            gkv_ref[b * SR : (b + 1) * SR, :HD] = (SCALE * tn(d2, q4)).astype(BF)
            gkv_ref[b * SR : (b + 1) * SR, HD:] = tn(p2.astype(BF), g4).astype(BF)
        gq = (SCALE * gq).astype(BF)
        for h in range(HEADS):
            gq_ref[lo : lo + SR, h * HD : (h + 1) * HD] = gq[h * SR : (h + 1) * SR, :]
        p = prompts[b]
        dense[p, :, :, :HD] += (SCALE * tn(d1, q4)).reshape(4, PR, HD)
        dense[p, :, :, HD:] += tn(p1.astype(BF), g4).reshape(4, PR, HD)
    for half in range(2):
        own_ref[:, half] = dense[:, half * 2 + c].astype(BF)
        sib_ref[:, half] = dense[:, half * 2 + 1 - c].astype(BF)


def attention(ids, owners, lengths, q, kv, gp, ga, pairs, pairs_sib, after):
    return pl.pallas_call(
        attention_kernel,
        out_shape=[
            jax.ShapeDtypeStruct((PR + AR, QC), BF),
            jax.ShapeDtypeStruct((AR, 2 * HD), BF),
            jax.ShapeDtypeStruct((PROMPTS, 2, PR, 2 * HD), BF),
            jax.ShapeDtypeStruct((PROMPTS, 2, PR, 2 * HD), BF),
        ],
        in_specs=[SM] * 3 + [VM] * 4 + [ANY] * 3,
        out_specs=[VM] * 4,
        scratch_shapes=[
            pltpu.VMEM((SLOTS + 1, PLEN, 2 * HD), BF),
            pltpu.VMEM((PROMPTS, 4, PR, 2 * HD), F32),
            pltpu.SemaphoreType.DMA((SLOTS + 1, 2, 2)),
        ],
        compiler_params=params(16),
        cost_estimate=cheap(),
        name="attention",
    )(ids, owners, lengths, q, kv, gp, ga, pairs, pairs_sib, after)


def row_coefficient(gq, gkv, q, kv, inv):
    row_dot = jnp.sum(gq.astype(F32) * q.astype(F32), axis=1, keepdims=True)
    row_dot += jnp.sum(gkv.astype(F32) * kv.astype(F32), axis=1, keepdims=True)
    return inv * inv * row_dot * (1.0 / D)


def answer_grads_kernel(
    ids, gq_ref, gkv_ref, q_ref, kv_ref, inv_ref, gain_ref, x_ref, qs_ref, qt_ref, ks_ref, kt_ref,
    out_ref, share_ref, token_ref, wq, wkv, states, result, sem_q, sem_kv, sem_x, sem_out,
):
    x_copy = pltpu.make_async_copy(x_ref, states, sem_x)
    blocks = []
    for k in range(NX):
        blocks.append(
            block_copies(ids, qs_ref, qt_ref, wq, sem_q, k) + block_copies(ids, ks_ref, kt_ref, wkv, sem_kv, k)
        )
        for copy in blocks[k]:
            copy.start()
        if k == 0:
            x_copy.start()
    gq, gkv = gq_ref[...], gkv_ref[...]
    inv = inv_ref[PR:, :]
    coefficient = row_coefficient(gq_ref[PR:, :], gkv, q_ref[PR:, :], kv_ref[PR:, :], inv)
    out_copies = []
    for k in range(NX):
        for copy in blocks[k]:
            copy.wait()
        cols = block_columns(ids, k)
        by_query = nt(gq, wq[k].reshape(BLK, QC))
        share_ref[:, cols] = by_query[:PR]
        hidden = by_query[PR:] + nt(gkv, wkv[k].reshape(BLK, 2 * HD))
        if k == 0:
            x_copy.wait()
        moved = inv * gain_ref[:, cols].astype(F32) * hidden - states[:, cols].astype(F32) * coefficient
        result[k] = moved.astype(BF)
        out_copies.append(pltpu.make_async_copy(result.at[k], out_ref.at[:, cols], sem_out.at[k]))
        out_copies[-1].start()
    for copy in out_copies:
        copy.wait()
    token_ref[...] = jnp.zeros_like(token_ref)


def answer_grads(ids, gq, gkv, q, kv, inv, gain, states, pieces):
    return pl.pallas_call(
        answer_grads_kernel,
        out_shape=[
            jax.ShapeDtypeStruct((AR, D), BF),
            jax.ShapeDtypeStruct((PR, D), F32),
            jax.ShapeDtypeStruct((8, 128), F32),
        ],
        in_specs=[SM] + [VM] * 6 + [HBM] * 5,
        out_specs=[HBM, VM, VM],
        scratch_shapes=[
            pltpu.VMEM((NX, NZ, NC, WR, QC), BF),
            pltpu.VMEM((NX, NZ, NC, WR, 2 * HD), BF),
            pltpu.VMEM((AR, D), BF),
            pltpu.VMEM((NX, AR, BLK), BF),
            pltpu.SemaphoreType.DMA((NX, 2)),
            pltpu.SemaphoreType.DMA((NX, 2)),
            pltpu.SemaphoreType.DMA,
            pltpu.SemaphoreType.DMA((NX,)),
        ],
        compiler_params=params(52),
        cost_estimate=cheap(),
        name="answer_grads",
    )(ids, gq, gkv, q, kv, inv, gain, states, *pieces)


def prompt_grads_kernel(
    ids, gq_ref, gkv_ref, q_ref, kv_ref, inv_ref, gain_ref, x_ref, share_ref, ks_ref, kt_ref, out_ref, wkv, sem
):
    copies = place(ids, ks_ref, kt_ref, wkv, sem)
    gkv = gkv_ref[...]
    inv = inv_ref[:PR, :]
    coefficient = row_coefficient(gq_ref[:PR, :], gkv, q_ref[:PR, :], kv_ref[:PR, :], inv)
    for k in range(NX):
        for copy in copies[k]:
            copy.wait()
        cols = block_columns(ids, k)
        hidden = share_ref[:, cols] + nt(gkv, wkv[k].reshape(BLK, 2 * HD))
        moved = inv * gain_ref[:, cols].astype(F32) * hidden - x_ref[:, cols].astype(F32) * coefficient
        out_ref[:, cols] = moved.astype(BF)


def prompt_grads(ids, gq, gkv, q, kv, inv, gain, states, share, pieces):
    return pl.pallas_call(
        prompt_grads_kernel,
        out_shape=jax.ShapeDtypeStruct((PR, D), BF),
        in_specs=[SM] + [VM] * 8 + [HBM] * 2,
        out_specs=VM,
        scratch_shapes=[pltpu.VMEM((NX, NZ, NC, WR, 2 * HD), BF), pltpu.SemaphoreType.DMA((NX, 2))],
        compiler_params=params(12),
        cost_estimate=cheap(),
        name="prompt_grads",
    )(ids, gq, gkv, q, kv, inv, gain, states, share, *pieces)


def weight_grads_kernel(ids, own_ref, sib_ref, g_ref, gs_ref, *refs):
    plus_ref, minus_ref, u_ref, l_ref, mine_ref = refs[-5:]
    x = ids[0]
    width = g_ref.shape[1]
    g, gs = g_ref[...], gs_ref[...]

    def product(k, lo, count):
        at = pl.ds(lax.rem(x + k, NX) * NZ + lo, count)
        rows = count * WR
        total = nn(own_ref[at].reshape(rows, PR + AR), g) + nn(sib_ref[at].reshape(rows, PR + AR), gs)
        return total.astype(BF).reshape(count, WR, width)

    half = NZ // 2
    plus_ref[0] = product(2, 0, half)
    minus_ref[0] = product(2, half, half)
    plus_ref[1] = product(1, half, half)
    minus_ref[1] = product(3, 0, half)
    u_ref[...] = product(1, 0, half)
    l_ref[...] = product(3, half, half)
    mine_ref[...] = product(0, 0, NZ)


def weight_grads(ids, own, sib, grads, grads_sib, after):
    width = grads.shape[1]
    half = NZ // 2

    def shape(*dims):
        return jax.ShapeDtypeStruct((*dims, WR, width), BF)

    return pl.pallas_call(
        weight_grads_kernel,
        out_shape=[shape(2, half), shape(2, half), shape(half), shape(half), shape(NZ)],
        in_specs=[SM] + [VM] * 4 + [ANY] * len(after),
        out_specs=[VM] * 5,
        compiler_params=params(16),
        cost_estimate=cheap(),
        name="weight_grads",
    )(ids, own, sib, grads, grads_sib, *after)


def add_up(value):
    return jnp.sum(value.astype(F32), axis=0)


def join(query, pair):
    half = NZ // 2
    width = query[4].shape[-1]

    def kernel(*refs):
        out_ref = refs[-1]
        for (upper, lower, plus, minus, mine), cols in (
            (refs[:5], slice(0, width)),
            (refs[5:10], slice(width, None)),
        ):
            first = mine[:half].astype(F32) + minus[1].astype(F32) + upper[...].astype(F32)
            second = mine[half:].astype(F32) + plus[1].astype(F32) + lower[...].astype(F32)
            out_ref[:half, :, cols] = first.astype(BF)
            out_ref[half:, :, cols] = second.astype(BF)

    return pl.pallas_call(
        kernel,
        out_shape=jax.ShapeDtypeStruct((NZ, WR, width + pair[4].shape[-1]), BF),
        in_specs=[VM] * 10,
        out_specs=VM,
        compiler_params=params(14),
        cost_estimate=cheap(),
        name="join",
    )(*query, *pair)


def first_hop(plus, minus):
    return shift(plus, "x", 1), shift(minus, "x", -1)


def second_sums(plus, minus, upper, lower, after):
    return add_after(upper, plus, after), add_after(lower, minus, after)


def per_device(
    prompt_states,
    answer_states,
    prompt_cotangent,
    answer_cotangent,
    norm_gain,
    weights,
    answer_length,
    answer_owner,
):
    x, z, c = lax.axis_index("x"), lax.axis_index("z"), lax.axis_index("c")
    ids = jnp.stack([x, z, c]).astype(jnp.int32)
    lengths, owners = answer_length[0], answer_owner[0]
    shard = weights[0]
    gain = norm_gain[0].astype(F32)

    kv_all = spread(shard[:, QC:], "z")
    q_line = direct_x(shard[:, :QC])
    scaled, inverse = norm(prompt_states[0], answer_states[0], norm_gain)
    kv_line = held(kv_all, (inverse, q_line))
    kv_near = both_ways(kv_line, kv_line, "x")
    q_line = held(q_line, (kv_line,))
    q_one = both_ways(q_line, q_line, "z")
    kv_near = held(kv_near[0], q_one), held(kv_near[1], q_one)
    kv_far = both_ways(kv_near[0][: NZ // 2], kv_near[1][NZ // 2 :], "x")
    q_one = held(q_one[0], kv_near), held(q_one[1], kv_near)
    q_two = both_ways(*q_one, "z")
    kv_pieces = stack_after([kv_line, kv_near[0], kv_far, kv_near[1]], q_two)
    kv_sib = shift(kv_pieces, "c", 1)
    q_two = held(q_two[0], kv_far), held(q_two[1], kv_far)
    q_three = both_ways(*q_two, "z")
    kv = project(ids, scaled, kv_pieces, kv_sib)
    pair_line = spread(kv[:PR], "z")
    pair_hops = [shift(pair_line, "x", k) for k in range(NX)]
    scaled = held(scaled, (kv,))
    scaled_t = scaled.T.reshape(NX * NZ, NC, WR, PR + AR)
    own_t = lax.dynamic_index_in_dim(scaled_t, c, 1, keepdims=False)
    other_t = lax.dynamic_index_in_dim(scaled_t, 1 - c, 1, keepdims=False)
    sib_t = shift(other_t, "c", 1)
    q_three = held(q_three[0], (pair_line, own_t, other_t)), held(q_three[1], (pair_line, own_t, other_t))
    q_four = both_ways(q_three[0][: NX // 2], q_three[1][NX // 2 :], "z")
    q_pieces = stack_z(
        ids,
        [q_line, q_one[0], q_two[0], q_three[0], q_four, q_three[1], q_two[1], q_one[1]],
        tuple(pair_hops[1:]),
    )
    q_sib = shift(q_pieces, "c", 1)
    q = project(ids, scaled, q_pieces, q_sib)
    pairs = stack_after(pair_hops, (kv,))
    pairs_sib = shift(pairs, "c", 1)

    gq, gkv_answer, own, sib = attention(
        ids, owners, lengths, q, kv, prompt_cotangent[0], answer_cotangent[0], pairs, pairs_sib, sib_t
    )
    gq_sib = shift(gq, "c", 1)
    answer_back, share, token = answer_grads(
        ids, gq, gkv_answer, q, kv, inverse, norm_gain, answer_states[0], (q_pieces, q_sib, kv_pieces, kv_sib)
    )
    answer_out = shift(answer_back, "section", -1)
    query_parts = weight_grads(ids, own_t, sib_t, gq, gq_sib, (token,))
    query_hop = first_hop(*query_parts[:2])

    terms = sum_after(own, shift(sib, "c", 1), ()).reshape(NX * NZ, PR, 2 * HD)
    gkv_prompt = add_up(exchange(terms, ("x", "z"))).astype(BF)
    gkv = jnp.concatenate([gkv_prompt, gkv_answer], axis=0)
    gkv_sib = shift(gkv, "c", 1)
    pair_parts = weight_grads(ids, own_t, sib_t, gkv, gkv_sib, (query_parts[2],))
    pair_hop = first_hop(*pair_parts[:2])
    query_second = both_ways(*second_sums(*query_hop, *query_parts[2:4], (pair_parts[2],)), "x")
    prompt_back = prompt_grads(
        ids, gq, gkv_prompt, q, kv, inverse, norm_gain, prompt_states[0], share, (kv_pieces, kv_sib)
    )
    prompt_out = forward(shift(prompt_back, "section", -1))
    pair_second = both_ways(*second_sums(*pair_hop, *pair_parts[2:4], (prompt_back,)), "x")
    joined = join((*query_second, *query_hop, query_parts[4]), (*pair_second, *pair_hop, pair_parts[4]))
    weight_total = add_up(exchange(joined, "z"))

    own_gain = lax.dynamic_slice(gain, (((x * NZ + z) * NC + c) * WR,), (WR,))
    gain_total = jnp.sum(weight_total * shard.astype(F32), axis=1) / own_gain
    return (prompt_out[None], forward(answer_out)[None], weight_total[None], gain_total[None])


def solution(mesh):
    fine = Mesh(mesh.devices.reshape(mesh.devices.shape[0], NX, NZ, NC), ("section", "x", "z", "c"))
    dp = ("x", "z", "c")
    placed = (
        P("section", dp, None),
        P("section", dp, None),
        P("section", dp, None),
        P("section", dp, None),
        P("section", None),
        P("section", dp, None),
        P("section", dp),
        P("section", dp),
    )
    return jax.shard_map(
        per_device,
        mesh=fine,
        in_specs=placed,
        out_specs=(
            P("section", dp, None),
            P("section", dp, None),
            P("section", dp, None),
            P("section", dp),
        ),
        check_vma=False,
    )
```

```python
import functools

import jax
import jax.numpy as jnp
from jax import lax
from jax.experimental import pallas as pl
from jax.experimental.pallas import tpu as pltpu
from jax.sharding import Mesh, PartitionSpec as P

HD = 128
HEADS = 4
QC = HEADS * HD
D = 5120
PR = 64
AR = 256
SLOTS = 4
SR = 64
NX, NZ, NC = 4, 8, 2
WR = 80
BLK = D // NX
PROMPTS = 16
PLEN = 256
EPSILON = 1e-06
SCALE = HD**-0.5
BF = jnp.bfloat16
F32 = jnp.float32
MIB = 1024 * 1024


def shift(value, axis, steps):
    count = lax.axis_size(axis)
    if steps % count == 0:
        return value
    return lax.ppermute(value, axis, [(s, (s + steps) % count) for s in range(count)])


def params(mib):
    return pltpu.CompilerParams(vmem_limit_bytes=mib * MIB)


def cheap():
    return pl.CostEstimate(flops=10**6, bytes_accessed=10**5, transcendentals=0)


ANY = pl.BlockSpec(memory_space=pl.ANY)
HBM = pl.BlockSpec(memory_space=pltpu.HBM)
VM = pl.BlockSpec(memory_space=pltpu.VMEM)
SM = pl.BlockSpec(memory_space=pltpu.SMEM)


def nt(a, b):
    return lax.dot_general(a, b, (((1,), (1,)), ((), ())), preferred_element_type=F32)


def tn(a, b):
    return lax.dot_general(a, b, (((0,), (0,)), ((), ())), preferred_element_type=F32)


def nn(a, b):
    return jnp.dot(a, b, preferred_element_type=F32)


def exchange(value, axis):
    return lax.all_to_all(value, axis, 0, 0, tiled=True)


def spread(value, axis):
    count = lax.axis_size(axis)
    return exchange(jnp.broadcast_to(value[None], (count, *value.shape)), axis)


def held(value, after):
    def kernel(*refs):
        del refs

    return pl.pallas_call(
        kernel,
        out_shape=jax.ShapeDtypeStruct(value.shape, value.dtype),
        in_specs=[ANY] * (1 + len(after)),
        out_specs=ANY,
        input_output_aliases={0: 0},
        compiler_params=params(4),
        cost_estimate=cheap(),
        name="held",
    )(value, *after)


def sum_after(left, right, after):
    def kernel(left_ref, right_ref, *refs):
        out_ref = refs[-1]
        out_ref[...] = (left_ref[...].astype(F32) + right_ref[...].astype(F32)).astype(BF)

    return pl.pallas_call(
        kernel,
        out_shape=jax.ShapeDtypeStruct(left.shape, BF),
        in_specs=[VM, VM] + [ANY] * len(after),
        out_specs=VM,
        compiler_params=params(10),
        cost_estimate=cheap(),
        name="sum",
    )(left, right, *after)


def add_after(left, right, after):
    def kernel(left_ref, right_ref, *refs):
        out_ref = refs[-1]
        out_ref[...] = (left_ref[...].astype(F32) + right_ref[0].astype(F32)).astype(BF)

    return pl.pallas_call(
        kernel,
        out_shape=jax.ShapeDtypeStruct(left.shape, BF),
        in_specs=[VM, VM] + [ANY] * len(after),
        out_specs=VM,
        compiler_params=params(6),
        cost_estimate=cheap(),
        name="add",
    )(left, right, *after)


def forward(value):
    rows, width = value.shape
    spec = pl.BlockSpec((32, width), lambda i: (i, 0))

    def kernel(value_ref, out_ref):
        out_ref[...] = value_ref[...]

    return pl.pallas_call(
        kernel,
        out_shape=jax.ShapeDtypeStruct(value.shape, value.dtype),
        grid=(rows // 32,),
        in_specs=[spec],
        out_specs=spec,
        compiler_params=params(4),
        cost_estimate=cheap(),
        name="forward",
    )(value)


def stack_after(pieces, after):
    flat = [part for piece in pieces for part in (piece if isinstance(piece, tuple) else (piece,))]
    shape = pieces[0].shape

    def kernel(*refs):
        out_ref = refs[-1]
        at = 0
        for i, piece in enumerate(pieces):
            if isinstance(piece, tuple):
                cut = shape[0] // 2
                out_ref[i, :cut] = refs[at][...]
                out_ref[i, cut:] = refs[at + 1][...]
                at += 2
            else:
                out_ref[i] = refs[at][...]
                at += 1

    return pl.pallas_call(
        kernel,
        out_shape=jax.ShapeDtypeStruct((len(pieces), *shape), flat[0].dtype),
        in_specs=[VM] * len(flat) + [ANY] * len(after),
        out_specs=VM,
        compiler_params=params(10),
        cost_estimate=cheap(),
        name="stack",
    )(*flat, *after)


def stack_z(ids, pieces, after):
    half = NZ // 2
    flat = [*pieces[:half], *pieces[half], *pieces[half + 1 :]]
    count, *rest = pieces[0].shape

    def kernel(ids, *refs):
        out_ref = refs[-1]

        def at(j):
            return lax.rem(ids[1] - j + NZ, NZ)

        for j in range(half):
            out_ref[:, at(j)] = refs[j][...]
        out_ref[: count // 2, at(half)] = refs[half][...]
        out_ref[count // 2 :, at(half)] = refs[half + 1][...]
        for j in range(half + 1, NZ):
            out_ref[:, at(j)] = refs[j + 1][...]

    return pl.pallas_call(
        kernel,
        out_shape=jax.ShapeDtypeStruct((count, NZ, *rest), flat[0].dtype),
        in_specs=[SM] + [VM] * len(flat) + [ANY] * len(after),
        out_specs=VM,
        compiler_params=params(10),
        cost_estimate=cheap(),
        name="stack_z",
    )(ids, *flat, *after)


def direct_x(value):
    return jnp.stack([shift(value, "x", k) for k in range(NX)])


def both_ways(up, down, axis):
    return shift(up, axis, 1), shift(down, axis, -1)


def norm_kernel(p_ref, a_ref, gain_ref, scaled_ref, inv_ref):
    gain = gain_ref[...].astype(F32)
    for ref, lo, rows in ((p_ref, 0, PR), (a_ref, PR, AR)):
        for r in range(0, rows, 32):
            wide = ref[r : r + 32, :].astype(F32)
            inv = lax.rsqrt(jnp.mean(wide * wide, axis=-1, keepdims=True) + EPSILON)
            scaled_ref[lo + r : lo + r + 32, :] = (wide * inv * gain).astype(BF)
            inv_ref[lo + r : lo + r + 32, :] = inv


def norm(prompt, answer, gain):
    rows = PR + AR
    return pl.pallas_call(
        norm_kernel,
        out_shape=[jax.ShapeDtypeStruct((rows, D), BF), jax.ShapeDtypeStruct((rows, 1), F32)],
        in_specs=[VM] * 3,
        out_specs=[VM] * 2,
        compiler_params=params(16),
        cost_estimate=cheap(),
        name="norm",
    )(prompt, answer, gain)


def block_copies(ids, s_ref, t_ref, w_ref, sem, k):
    return [
        pltpu.make_async_copy((s_ref, t_ref)[rel].at[k], w_ref.at[k, :, lax.rem(ids[2] + rel, 2)], sem.at[k, rel])
        for rel in range(2)
    ]


def place(ids, s_ref, t_ref, w_ref, sem):
    blocks = [block_copies(ids, s_ref, t_ref, w_ref, sem, k) for k in range(NX)]
    for copies in blocks:
        for copy in copies:
            copy.start()
    return blocks


def block_columns(ids, k):
    return pl.ds(pl.multiple_of(lax.rem(ids[0] - k + NX, NX) * BLK, BLK), BLK)


def project_kernel(ids, a_ref, s_ref, t_ref, out_ref, w_ref, sem):
    width = w_ref.shape[-1]
    copies = place(ids, s_ref, t_ref, w_ref, sem)
    total = jnp.zeros((PR + AR, width), F32)
    for k in range(NX):
        for copy in copies[k]:
            copy.wait()
        total += nn(a_ref[:, block_columns(ids, k)], w_ref[k].reshape(BLK, width))
    out_ref[...] = total.astype(BF)


def project(ids, scaled, pieces, pieces_sib):
    width = pieces.shape[-1]
    rows = scaled.shape[0]
    return pl.pallas_call(
        project_kernel,
        out_shape=jax.ShapeDtypeStruct((rows, width), BF),
        in_specs=[SM, VM, HBM, HBM],
        out_specs=VM,
        scratch_shapes=[pltpu.VMEM((NX, NZ, NC, WR, width), BF), pltpu.SemaphoreType.DMA((NX, 2))],
        compiler_params=params(16),
        cost_estimate=cheap(),
        name="project",
    )(ids, scaled, pieces, pieces_sib)


def stacked(value):
    return jnp.concatenate([value[:, h * HD : (h + 1) * HD] for h in range(HEADS)], axis=0)


def attention_kernel(
    ids, owners, lengths, q_ref, kv_ref, gp_ref, ga_ref, s_ref, t_ref, after_ref,
    gq_ref, gkv_ref, own_ref, sib_ref, pairs, dense, sem,
):
    del after_ref
    x, z, c = ids[0], ids[1], ids[2]
    own_prompt = x * 4 + z // 2
    prompts = [owners[s] for s in range(SLOTS)] + [own_prompt]
    copies = []
    for b, p in enumerate(prompts):
        k = lax.rem(x - p // 4 + NX, NX)
        for half in range(2):
            for rel in range(2):
                at = pl.multiple_of((half * 2 + lax.rem(c + rel, 2)) * PR, PR)
                src = (s_ref, t_ref)[rel].at[k, lax.rem(p, 4) * 2 + half]
                copies.append(pltpu.make_async_copy(src, pairs.at[b, pl.ds(at, PR)], sem.at[b, half, rel]))
                copies[-1].start()
    dense[...] = jnp.zeros_like(dense)
    row_step = lax.rem(lax.broadcasted_iota(jnp.int32, (HEADS * SR, SR), 0), SR)
    col_step = lax.broadcasted_iota(jnp.int32, (HEADS * SR, SR), 1)
    live_step = lax.broadcasted_iota(jnp.int32, (SR, QC), 0)
    per_block = 4
    for b in range(SLOTS + 1):
        for copy in copies[b * per_block : (b + 1) * per_block]:
            copy.wait()
        keys, values = pairs[b, :, :HD], pairs[b, :, HD:]
        if b < SLOTS:
            lo = PR + b * SR
            length = lengths[b]
            upstream = ga_ref[b * SR : (b + 1) * SR, :]
            upstream = jnp.where(live_step < length, upstream.astype(F32), 0.0).astype(BF)
        else:
            lo = 0
            upstream = gp_ref[...]
        q4 = stacked(q_ref[lo : lo + SR, :])
        g4 = stacked(upstream)
        s1 = SCALE * nt(q4, keys)
        gp1 = nt(g4, values)
        if b < SLOTS:
            k_own = kv_ref[lo : lo + SR, :HD]
            v_own = kv_ref[lo : lo + SR, HD:]
            s2 = SCALE * nt(q4, k_own)
            gp2 = nt(g4, v_own)
            seen = (row_step >= col_step) & (col_step < length)
            s2 = jnp.where(seen, s2, -jnp.inf)
            top = jnp.maximum(jnp.max(s1, axis=1, keepdims=True), jnp.max(s2, axis=1, keepdims=True))
            e1 = jnp.exp(s1 - top)
            e2 = jnp.exp(s2 - top)
            norm = 1.0 / (jnp.sum(e1, axis=1, keepdims=True) + jnp.sum(e2, axis=1, keepdims=True))
            p1 = e1 * norm
            p2 = e2 * norm
            delta = jnp.sum(p1 * gp1, axis=1, keepdims=True) + jnp.sum(p2 * gp2, axis=1, keepdims=True)
            d2 = (p2 * (gp2 - delta)).astype(BF)
        else:
            offset = (lax.rem(z, 2) * 2 + c) * PR
            rows = lax.rem(lax.broadcasted_iota(jnp.int32, (HEADS * SR, PLEN), 0), SR) + offset
            cols = lax.broadcasted_iota(jnp.int32, (HEADS * SR, PLEN), 1)
            s1 = jnp.where(rows >= cols, s1, -jnp.inf)
            top = jnp.max(s1, axis=1, keepdims=True)
            e1 = jnp.exp(s1 - top)
            p1 = e1 * (1.0 / jnp.sum(e1, axis=1, keepdims=True))
            delta = jnp.sum(p1 * gp1, axis=1, keepdims=True)
        d1 = (p1 * (gp1 - delta)).astype(BF)
        gq = nn(d1, keys)
        if b < SLOTS:
            gq += nn(d2, k_own)
            gkv_ref[b * SR : (b + 1) * SR, :HD] = (SCALE * tn(d2, q4)).astype(BF)
            gkv_ref[b * SR : (b + 1) * SR, HD:] = tn(p2.astype(BF), g4).astype(BF)
        gq = (SCALE * gq).astype(BF)
        for h in range(HEADS):
            gq_ref[lo : lo + SR, h * HD : (h + 1) * HD] = gq[h * SR : (h + 1) * SR, :]
        p = prompts[b]
        dense[p, :, :, :HD] += (SCALE * tn(d1, q4)).reshape(4, PR, HD)
        dense[p, :, :, HD:] += tn(p1.astype(BF), g4).reshape(4, PR, HD)
    for half in range(2):
        own_ref[:, half] = dense[:, half * 2 + c].astype(BF)
        sib_ref[:, half] = dense[:, half * 2 + 1 - c].astype(BF)


def attention(ids, owners, lengths, q, kv, gp, ga, pairs, pairs_sib, after):
    return pl.pallas_call(
        attention_kernel,
        out_shape=[
            jax.ShapeDtypeStruct((PR + AR, QC), BF),
            jax.ShapeDtypeStruct((AR, 2 * HD), BF),
            jax.ShapeDtypeStruct((PROMPTS, 2, PR, 2 * HD), BF),
            jax.ShapeDtypeStruct((PROMPTS, 2, PR, 2 * HD), BF),
        ],
        in_specs=[SM] * 3 + [VM] * 4 + [ANY] * 3,
        out_specs=[VM] * 4,
        scratch_shapes=[
            pltpu.VMEM((SLOTS + 1, PLEN, 2 * HD), BF),
            pltpu.VMEM((PROMPTS, 4, PR, 2 * HD), F32),
            pltpu.SemaphoreType.DMA((SLOTS + 1, 2, 2)),
        ],
        compiler_params=params(16),
        cost_estimate=cheap(),
        name="attention",
    )(ids, owners, lengths, q, kv, gp, ga, pairs, pairs_sib, after)


def row_coefficient(gq, gkv, q, kv, inv):
    row_dot = jnp.sum(gq.astype(F32) * q.astype(F32), axis=1, keepdims=True)
    row_dot += jnp.sum(gkv.astype(F32) * kv.astype(F32), axis=1, keepdims=True)
    return inv * inv * row_dot * (1.0 / D)


def answer_grads_kernel(
    ids, gq_ref, gkv_ref, q_ref, kv_ref, inv_ref, gain_ref, x_ref, qs_ref, qt_ref, ks_ref, kt_ref,
    out_ref, share_ref, token_ref, wq, wkv, states, result, sem_q, sem_kv, sem_x, sem_out,
):
    x_copy = pltpu.make_async_copy(x_ref, states, sem_x)
    blocks = []
    for k in range(NX):
        blocks.append(
            block_copies(ids, qs_ref, qt_ref, wq, sem_q, k) + block_copies(ids, ks_ref, kt_ref, wkv, sem_kv, k)
        )
        for copy in blocks[k]:
            copy.start()
        if k == 0:
            x_copy.start()
    gq, gkv = gq_ref[...], gkv_ref[...]
    inv = inv_ref[PR:, :]
    coefficient = row_coefficient(gq_ref[PR:, :], gkv, q_ref[PR:, :], kv_ref[PR:, :], inv)
    out_copies = []
    for k in range(NX):
        for copy in blocks[k]:
            copy.wait()
        cols = block_columns(ids, k)
        by_query = nt(gq, wq[k].reshape(BLK, QC))
        share_ref[:, cols] = by_query[:PR]
        hidden = by_query[PR:] + nt(gkv, wkv[k].reshape(BLK, 2 * HD))
        if k == 0:
            x_copy.wait()
        moved = inv * gain_ref[:, cols].astype(F32) * hidden - states[:, cols].astype(F32) * coefficient
        result[k] = moved.astype(BF)
        out_copies.append(pltpu.make_async_copy(result.at[k], out_ref.at[:, cols], sem_out.at[k]))
        out_copies[-1].start()
    for copy in out_copies:
        copy.wait()
    token_ref[...] = jnp.zeros_like(token_ref)


def answer_grads(ids, gq, gkv, q, kv, inv, gain, states, pieces):
    return pl.pallas_call(
        answer_grads_kernel,
        out_shape=[
            jax.ShapeDtypeStruct((AR, D), BF),
            jax.ShapeDtypeStruct((PR, D), F32),
            jax.ShapeDtypeStruct((8, 128), F32),
        ],
        in_specs=[SM] + [VM] * 6 + [HBM] * 5,
        out_specs=[HBM, VM, VM],
        scratch_shapes=[
            pltpu.VMEM((NX, NZ, NC, WR, QC), BF),
            pltpu.VMEM((NX, NZ, NC, WR, 2 * HD), BF),
            pltpu.VMEM((AR, D), BF),
            pltpu.VMEM((NX, AR, BLK), BF),
            pltpu.SemaphoreType.DMA((NX, 2)),
            pltpu.SemaphoreType.DMA((NX, 2)),
            pltpu.SemaphoreType.DMA,
            pltpu.SemaphoreType.DMA((NX,)),
        ],
        compiler_params=params(52),
        cost_estimate=cheap(),
        name="answer_grads",
    )(ids, gq, gkv, q, kv, inv, gain, states, *pieces)


def prompt_grads_kernel(
    ids, gq_ref, gkv_ref, q_ref, kv_ref, inv_ref, gain_ref, x_ref, share_ref, ks_ref, kt_ref, out_ref, wkv, sem
):
    copies = place(ids, ks_ref, kt_ref, wkv, sem)
    gkv = gkv_ref[...]
    inv = inv_ref[:PR, :]
    coefficient = row_coefficient(gq_ref[:PR, :], gkv, q_ref[:PR, :], kv_ref[:PR, :], inv)
    for k in range(NX):
        for copy in copies[k]:
            copy.wait()
        cols = block_columns(ids, k)
        hidden = share_ref[:, cols] + nt(gkv, wkv[k].reshape(BLK, 2 * HD))
        moved = inv * gain_ref[:, cols].astype(F32) * hidden - x_ref[:, cols].astype(F32) * coefficient
        out_ref[:, cols] = moved.astype(BF)


def prompt_grads(ids, gq, gkv, q, kv, inv, gain, states, share, pieces):
    return pl.pallas_call(
        prompt_grads_kernel,
        out_shape=jax.ShapeDtypeStruct((PR, D), BF),
        in_specs=[SM] + [VM] * 8 + [HBM] * 2,
        out_specs=VM,
        scratch_shapes=[pltpu.VMEM((NX, NZ, NC, WR, 2 * HD), BF), pltpu.SemaphoreType.DMA((NX, 2))],
        compiler_params=params(12),
        cost_estimate=cheap(),
        name="prompt_grads",
    )(ids, gq, gkv, q, kv, inv, gain, states, share, *pieces)


def weight_grads_kernel(ids, own_ref, sib_ref, g_ref, gs_ref, *refs):
    plus_ref, minus_ref, u_ref, l_ref, mine_ref = refs[-5:]
    x = ids[0]
    width = g_ref.shape[1]
    g, gs = g_ref[...], gs_ref[...]

    def product(k, lo, count):
        at = pl.ds(lax.rem(x + k, NX) * NZ + lo, count)
        rows = count * WR
        total = nn(own_ref[at].reshape(rows, PR + AR), g) + nn(sib_ref[at].reshape(rows, PR + AR), gs)
        return total.astype(BF).reshape(count, WR, width)

    half = NZ // 2
    plus_ref[0] = product(2, 0, half)
    minus_ref[0] = product(2, half, half)
    plus_ref[1] = product(1, half, half)
    minus_ref[1] = product(3, 0, half)
    u_ref[...] = product(1, 0, half)
    l_ref[...] = product(3, half, half)
    mine_ref[...] = product(0, 0, NZ)


def weight_grads(ids, own, sib, grads, grads_sib, after):
    width = grads.shape[1]
    half = NZ // 2

    def shape(*dims):
        return jax.ShapeDtypeStruct((*dims, WR, width), BF)

    return pl.pallas_call(
        weight_grads_kernel,
        out_shape=[shape(2, half), shape(2, half), shape(half), shape(half), shape(NZ)],
        in_specs=[SM] + [VM] * 4 + [ANY] * len(after),
        out_specs=[VM] * 5,
        compiler_params=params(16),
        cost_estimate=cheap(),
        name="weight_grads",
    )(ids, own, sib, grads, grads_sib, *after)


def add_up(value):
    return jnp.sum(value.astype(F32), axis=0)


def join(query, pair):
    half = NZ // 2
    width = query[4].shape[-1]

    def kernel(*refs):
        out_ref = refs[-1]
        for (upper, lower, plus, minus, mine), cols in (
            (refs[:5], slice(0, width)),
            (refs[5:10], slice(width, None)),
        ):
            first = mine[:half].astype(F32) + minus[1].astype(F32) + upper[...].astype(F32)
            second = mine[half:].astype(F32) + plus[1].astype(F32) + lower[...].astype(F32)
            out_ref[:half, :, cols] = first.astype(BF)
            out_ref[half:, :, cols] = second.astype(BF)

    return pl.pallas_call(
        kernel,
        out_shape=jax.ShapeDtypeStruct((NZ, WR, width + pair[4].shape[-1]), BF),
        in_specs=[VM] * 10,
        out_specs=VM,
        compiler_params=params(14),
        cost_estimate=cheap(),
        name="join",
    )(*query, *pair)


def first_hop(plus, minus):
    return shift(plus, "x", 1), shift(minus, "x", -1)


def second_sums(plus, minus, upper, lower, after):
    return add_after(upper, plus, after), add_after(lower, minus, after)


def per_device(
    prompt_states,
    answer_states,
    prompt_cotangent,
    answer_cotangent,
    norm_gain,
    weights,
    answer_length,
    answer_owner,
):
    x, z, c = lax.axis_index("x"), lax.axis_index("z"), lax.axis_index("c")
    ids = jnp.stack([x, z, c]).astype(jnp.int32)
    lengths, owners = answer_length[0], answer_owner[0]
    shard = weights[0]
    gain = norm_gain[0].astype(F32)

    kv_all = spread(shard[:, QC:], "z")
    q_line = direct_x(shard[:, :QC])
    scaled, inverse = norm(prompt_states[0], answer_states[0], norm_gain)
    kv_line = held(kv_all, (inverse, q_line))
    kv_near = both_ways(kv_line, kv_line, "x")
    q_line = held(q_line, (kv_line,))
    q_one = both_ways(q_line, q_line, "z")
    kv_near = held(kv_near[0], q_one), held(kv_near[1], q_one)
    kv_far = both_ways(kv_near[0][: NZ // 2], kv_near[1][NZ // 2 :], "x")
    q_one = held(q_one[0], kv_near), held(q_one[1], kv_near)
    q_two = both_ways(*q_one, "z")
    kv_pieces = stack_after([kv_line, kv_near[0], kv_far, kv_near[1]], q_two)
    kv_sib = shift(kv_pieces, "c", 1)
    q_two = held(q_two[0], kv_far), held(q_two[1], kv_far)
    q_three = both_ways(*q_two, "z")
    kv = project(ids, scaled, kv_pieces, kv_sib)
    pair_line = spread(kv[:PR], "z")
    pair_hops = [shift(pair_line, "x", k) for k in range(NX)]
    scaled = held(scaled, (kv,))
    scaled_t = scaled.T.reshape(NX * NZ, NC, WR, PR + AR)
    own_t = lax.dynamic_index_in_dim(scaled_t, c, 1, keepdims=False)
    other_t = lax.dynamic_index_in_dim(scaled_t, 1 - c, 1, keepdims=False)
    sib_t = shift(other_t, "c", 1)
    q_three = held(q_three[0], (pair_line, own_t, other_t)), held(q_three[1], (pair_line, own_t, other_t))
    q_four = both_ways(q_three[0][: NX // 2], q_three[1][NX // 2 :], "z")
    q_pieces = stack_z(
        ids,
        [q_line, q_one[0], q_two[0], q_three[0], q_four, q_three[1], q_two[1], q_one[1]],
        tuple(pair_hops[1:]),
    )
    q_sib = shift(q_pieces, "c", 1)
    q = project(ids, scaled, q_pieces, q_sib)
    pairs = stack_after(pair_hops, (kv,))
    pairs_sib = shift(pairs, "c", 1)

    gq, gkv_answer, own, sib = attention(
        ids, owners, lengths, q, kv, prompt_cotangent[0], answer_cotangent[0], pairs, pairs_sib, sib_t
    )
    gq_sib = shift(gq, "c", 1)
    answer_back, share, token = answer_grads(
        ids, gq, gkv_answer, q, kv, inverse, norm_gain, answer_states[0], (q_pieces, q_sib, kv_pieces, kv_sib)
    )
    answer_out = shift(answer_back, "section", -1)
    query_parts = weight_grads(ids, own_t, sib_t, gq, gq_sib, (token,))
    query_hop = first_hop(*query_parts[:2])

    terms = sum_after(own, shift(sib, "c", 1), (gq_sib,)).reshape(NX * NZ, PR, 2 * HD)
    gkv_prompt = add_up(exchange(terms, ("x", "z"))).astype(BF)
    gkv = jnp.concatenate([gkv_prompt, gkv_answer], axis=0)
    gkv_sib = shift(gkv, "c", 1)
    pair_parts = weight_grads(ids, own_t, sib_t, gkv, gkv_sib, (query_parts[2],))
    pair_hop = first_hop(*pair_parts[:2])
    query_second = both_ways(*second_sums(*query_hop, *query_parts[2:4], (pair_parts[2],)), "x")
    prompt_back = prompt_grads(
        ids, gq, gkv_prompt, q, kv, inverse, norm_gain, prompt_states[0], share, (kv_pieces, kv_sib)
    )
    prompt_out = forward(shift(held(prompt_back, (answer_out,)), "section", -1))
    pair_second = both_ways(*second_sums(*pair_hop, *pair_parts[2:4], (prompt_back,)), "x")
    joined = join((*query_second, *query_hop, query_parts[4]), (*pair_second, *pair_hop, pair_parts[4]))
    weight_total = add_up(exchange(joined, "z"))

    own_gain = lax.dynamic_slice(gain, (((x * NZ + z) * NC + c) * WR,), (WR,))
    gain_total = jnp.sum(weight_total * shard.astype(F32), axis=1) / own_gain
    return (prompt_out[None], forward(answer_out)[None], weight_total[None], gain_total[None])


def solution(mesh):
    fine = Mesh(mesh.devices.reshape(mesh.devices.shape[0], NX, NZ, NC), ("section", "x", "z", "c"))
    dp = ("x", "z", "c")
    placed = (
        P("section", dp, None),
        P("section", dp, None),
        P("section", dp, None),
        P("section", dp, None),
        P("section", None),
        P("section", dp, None),
        P("section", dp),
        P("section", dp),
    )
    return jax.shard_map(
        per_device,
        mesh=fine,
        in_specs=placed,
        out_specs=(
            P("section", dp, None),
            P("section", dp, None),
            P("section", dp, None),
            P("section", dp),
        ),
        check_vma=False,
    )
```
